32 devices in a mesh: groups: 2 (over y), owner: 16 (over z, x, core).
Axes of the slice: x: 2, y: 2, z: 4, core: 2. Of those that a mesh axis runs over, the one named last changes fastest.
Arguments:
- hidden: bfloat16 [4096, 8192], P(('groups', 'owner')), parts along dimension 0, may hold values from -6 to 6
- adapter_id: int32 [4096], P(('groups', 'owner')), parts along dimension 0, may hold values from 0 to 31, as said below
- adapter_slot: int32 [64], P('groups'), parts along dimension 0, may hold values from 0 to 31, as said below
- cache_len: int32 [4096], P(('groups', 'owner')), parts along dimension 0, may hold values from 2 to 16, as said below
- base_q: bfloat16 [4096, 4096], P(('groups', 'owner')), parts along dimension 0, may hold values from -6 to 6
- kv_cache: bfloat16 [4096, 2, 16, 512], P(('groups', 'owner')), parts along dimension 0, may hold values from -160 to 160
- a_maps: bfloat16 [8192, 2048], P(None, 'owner'), may hold values from -0.0625 to 0.0625
- b_maps: bfloat16 [2048, 4096], P('owner'), may hold values from -0.75 to 0.75
Outputs:
- attended: bfloat16 [4096, 4096], P(('groups', 'owner')), parts along dimension 0
The draws below stay inside these ranges and needn't reach their ends.
There are 2 independent parts, one for each index of `groups`. The reference program is written for one: setup_inputs(seed, part) draws one part's arguments, and reference() takes and returns one part's arrays. A program takes and returns all parts, laid end to end along the dimension named above; an argument that names none is the same for every part. Nothing has to cross between parts.
Inputs may be any that keep to these rules, and one draw needn't show every extreme that they name: `adapter_id`: each replica's owners hold the slots in blocks of 2: owner o holds slots o * 2 to o * 2 + 1. Within the 128 rows of one device, at most 8 rows name adapters whose slots lie in one owner's block; in every draw some owner receives exactly 8 rows from every device. `adapter_slot`: A permutation of the slots. `cache_len`: each device's rows include one with 16 cached positions.
All inputs are finite; a program needn't handle non-finite values.
Results may differ from the reference program's by a relative error of at most 0.0071.
Values may be sent and summed in bfloat16 or wider, within the bound.
No kernel may reach another device: no remote copies, remote signals or barrier semaphores. Data moves between devices by JAX's collectives and lax.ppermute only.
A program may use at most 64 MiB of HBM per device.

```python
import jax
import jax.numpy as jnp
from jax import lax

D = 8192
HEAD = 128
KVH = 4
RANK = 64
ADP_DEV = 2
TOK_DEV = 128
CTX = 16
GROUP = 8
QW = 4096
KVW = 512
ADAPTERS = 32
TOKENS = 2048
SLOT = 8
N_OWNER = 16


def routing_tables(key):
    slot_of = jax.random.permutation(jax.random.fold_in(key, 11), ADAPTERS)
    hot_owner = jax.random.randint(jax.random.fold_in(key, 12), (), 0, N_OWNER)
    entries = N_OWNER * SLOT

    def per_source(source_key):
        first_key, second_key = jax.random.split(source_key)
        priority = jax.random.permutation(first_key, entries)
        index = jnp.arange(entries)
        priority = jnp.where(index // SLOT == hot_owner, index - 2 * entries, priority)
        order = jnp.argsort(priority, stable=True)
        owners = order[:TOK_DEV] // SLOT
        return jax.random.permutation(second_key, owners)
    source_keys = jax.random.split(jax.random.fold_in(key, 13), N_OWNER)
    owners = jax.vmap(per_source)(source_keys).reshape(TOKENS)
    pick = jax.random.randint(jax.random.fold_in(key, 14), (TOKENS,), 0, ADP_DEV)
    slots = owners * ADP_DEV + pick
    adapter_of_slot = jnp.argsort(slot_of, stable=True)
    return (slot_of.astype(jnp.int32), adapter_of_slot[slots].astype(jnp.int32))


def draw_adapter_id(key, part):
    tables = routing_tables(key)
    return tables[1]


def draw_adapter_slot(key, part):
    tables = routing_tables(key)
    return tables[0]


def draw_cache_len(key, part):
    key = jax.random.fold_in(key, 21)
    lengths = jax.random.randint(jax.random.fold_in(key, 1), (N_OWNER, TOK_DEV), 2, CTX + 1)
    longest = jax.random.randint(jax.random.fold_in(key, 2), (N_OWNER, 1), 0, TOK_DEV)
    lengths = jnp.where(jnp.arange(TOK_DEV)[None, :] == longest, CTX, lengths)
    return lengths.reshape(TOKENS).astype(jnp.int32)


def attention_fields(key):
    base = jnp.clip(jax.random.normal(jax.random.fold_in(key, 31), (TOKENS, QW), jnp.float32), -6.0, 6.0)
    cache = jnp.clip(jax.random.normal(jax.random.fold_in(key, 32), (TOKENS, 2, CTX, KVW), jnp.float32), -6.0, 6.0)
    return (base, cache)


def draw_base_q(key, part):
    fields = attention_fields(key)
    return fields[0].astype(jnp.bfloat16)


def draw_kv_cache(key, part):
    fields = attention_fields(key)
    return fields[1].astype(jnp.bfloat16)


def steps_of(own_key, extent, cuts, least, largest):
    factor_of = 1.0
    for dim, blocks in cuts:
        heights = jax.random.uniform(jax.random.fold_in(jax.random.fold_in(own_key, 6), dim), (blocks,), jnp.float32, least / len(cuts), largest / len(cuts))
        factor_of = factor_of * jnp.repeat(jnp.exp(heights), extent[dim] // blocks).reshape((-1,) + (1,) * (len(extent) - 1 - dim))
    return factor_of


def scatter_about(own_key, extent, width, bound, shards=(), kind=jnp.bfloat16):
    array = jax.random.normal(own_key, extent, jnp.float32) * width
    if len(shards) > 0:
        array = steps_of(own_key, extent, shards, -0.22, 0.18) * array
    return jnp.clip(array, min=-bound, max=bound).astype(kind)


def setup_inputs(seed: int = 0, part: int = 0) -> dict:
    key_of = jax.random.split(jax.random.key(seed), 9)
    part_splits = jax.random.split(jax.random.fold_in(key_of[8], part), 9)
    hidden = scatter_about(part_splits[0], (TOKENS, D), 1.0, 6.0, ((0, 16),))
    adapter_id = draw_adapter_id(jax.random.fold_in(jax.random.fold_in(key_of[8], part), 71), part)
    adapter_slot = draw_adapter_slot(jax.random.fold_in(jax.random.fold_in(key_of[8], part), 71), part)
    cache_len = draw_cache_len(jax.random.fold_in(jax.random.fold_in(key_of[8], part), 71), part)
    base_q = draw_base_q(jax.random.fold_in(jax.random.fold_in(key_of[8], part), 71), part)
    kv_cache = draw_kv_cache(jax.random.fold_in(jax.random.fold_in(key_of[8], part), 71), part)
    a_maps = scatter_about(key_of[6], (D, ADAPTERS * RANK), D ** -0.5, 0.0625, ((1, 16),))
    b_maps = scatter_about(key_of[7], (ADAPTERS * RANK, QW), RANK ** -0.5, 0.75, ((0, 16),))
    return dict(hidden=hidden, adapter_id=adapter_id, adapter_slot=adapter_slot, cache_len=cache_len, base_q=base_q, kv_cache=kv_cache, a_maps=a_maps, b_maps=b_maps)


SCALE = 2.0

def attend_block(base_block, delta_block, kv_block, len_block):
    rows = base_block.shape[0]
    keys = kv_block[:, 0].reshape(rows, CTX, KVH, HEAD).astype(jnp.float32)
    values = kv_block[:, 1].reshape(rows, CTX, KVH, HEAD).astype(jnp.float32)
    query_base = base_block.reshape(rows, KVH, GROUP, HEAD).astype(jnp.float32)
    query_delta = delta_block.reshape(rows, KVH, GROUP, HEAD).astype(jnp.float32)
    scores = jnp.einsum('rkgd,rtkd->rkgt', query_base, keys) + jnp.einsum('rkgd,rtkd->rkgt', query_delta, keys)
    scores = scores * (1.0 / jnp.sqrt(jnp.float32(HEAD)))
    live = jnp.arange(CTX, dtype=jnp.int32)[None, None, None, :] < len_block[:, None, None, None]
    scores = jnp.where(live, scores, -jnp.inf)
    top = lax.optimization_barrier(jnp.max(scores, axis=-1, keepdims=True))
    expo = jnp.where(live, jnp.exp(scores - top), 0.0)
    probs = (expo / lax.optimization_barrier(jnp.sum(expo, axis=-1, keepdims=True))).astype(jnp.bfloat16)
    out = jnp.einsum('rkgt,rtkd->rkgd', probs.astype(jnp.float32), values)
    return out.reshape(rows, QW).astype(jnp.bfloat16)

def reference(hidden, adapter_id, adapter_slot, cache_len, base_q, kv_cache, a_maps, b_maps):
    slot = adapter_slot[adapter_id]
    a_all = a_maps.reshape(D, ADAPTERS, RANK).transpose(1, 0, 2)
    b_all = b_maps.reshape(ADAPTERS, RANK, QW)
    blocks = TOKENS // TOK_DEV

    def one_block(pieces):
        rows_x, rows_slot, base_block, kv_block, len_block = pieces
        low = jnp.einsum('rd,rdk->rk', rows_x.astype(jnp.float32), a_all[rows_slot].astype(jnp.float32)).astype(jnp.bfloat16)
        delta = (SCALE * jnp.einsum('rk,rkq->rq', low.astype(jnp.float32), b_all[rows_slot].astype(jnp.float32))).astype(jnp.bfloat16)
        return attend_block(base_block, delta, kv_block, len_block)
    out = lax.map(one_block, (hidden.reshape(blocks, TOK_DEV, D), slot.reshape(blocks, TOK_DEV), base_q.reshape(blocks, TOK_DEV, QW), kv_cache.reshape(blocks, TOK_DEV, 2, CTX, KVW), cache_len.reshape(blocks, TOK_DEV)))
    return out.reshape(TOKENS, QW)
```

```python
import functools

import jax
import jax.numpy as jnp
from jax import lax
from jax.experimental import pallas as pl
from jax.experimental.pallas import tpu as pltpu
from jax.sharding import PartitionSpec as P

HEAD = 128
KVH = 4
RANK = 64
LANES = 128
SCALE = 2.0
ROWS_STEP = 16


def routing(owners, slot_count, held, slots_ref, ids_ref):
    ids = ids_ref[...]
    rows = ids.shape[1]

    def look(s, slot):
        return jnp.where(ids == s, slots_ref[s], slot)

    slot = lax.fori_loop(0, slots_ref.shape[0], look, jnp.zeros_like(ids), unroll=8)
    owner = lax.div(slot, held)
    local = slot - owner * held
    hits = owner == lax.broadcasted_iota(jnp.int32, (owners, rows), 0)
    earlier = lax.broadcasted_iota(jnp.int32, (rows, rows), 0) < lax.broadcasted_iota(
        jnp.int32, (rows, rows), 1
    )
    before = jnp.dot(
        hits.astype(jnp.bfloat16), earlier.astype(jnp.bfloat16), preferred_element_type=jnp.float32
    )
    place = jnp.sum(jnp.where(hits, before, 0.0), axis=0, keepdims=True).astype(jnp.int32)
    bins = owner * slot_count + place
    routed = bins == lax.broadcasted_iota(jnp.int32, (owners * slot_count, rows), 0)
    label = jnp.sum(jnp.where(routed, local.astype(jnp.float32), 0.0), axis=1, keepdims=True)
    return routed.astype(jnp.bfloat16), label


def pack_kernel(owners, slot_count, held, slots_ref, ids_ref, hidden_ref, packed_ref, routed_ref, label_ref):
    step = pl.program_id(0)

    @pl.when(step == 0)
    def _():
        routed, label = routing(owners, slot_count, held, slots_ref, ids_ref)
        routed_ref[...] = routed
        label_ref[...] = jnp.broadcast_to(label, label_ref.shape)

    packed_ref[...] = jnp.dot(
        routed_ref[...], hidden_ref[...], preferred_element_type=jnp.float32
    ).astype(packed_ref.dtype)

    @pl.when(step == pl.num_programs(0) - 1)
    def _():
        packed_ref[:, packed_ref.shape[1] - LANES :] = label_ref[...].astype(packed_ref.dtype)


def pack(hidden, adapter_id, adapter_slot, owners, slot_count, held):
    rows, width = hidden.shape
    bins = owners * slot_count
    total = width + LANES
    steps = next(n for n in range(4, total // LANES + 1) if total % (n * LANES) == 0)
    block = total // steps
    return pl.pallas_call(
        functools.partial(pack_kernel, owners, slot_count, held),
        grid=(steps,),
        in_specs=[
            pl.BlockSpec(memory_space=pltpu.SMEM),
            pl.BlockSpec((1, rows), lambda i: (0, 0)),
            pl.BlockSpec((rows, block), lambda i: (0, i)),
        ],
        out_specs=[
            pl.BlockSpec((bins, block), lambda i: (0, i)),
            pl.BlockSpec((bins, rows), lambda i: (0, 0)),
        ],
        out_shape=[
            jax.ShapeDtypeStruct((bins, total), hidden.dtype),
            jax.ShapeDtypeStruct((bins, rows), jnp.bfloat16),
        ],
        scratch_shapes=[pltpu.VMEM((bins, LANES), jnp.float32)],
        compiler_params=pltpu.CompilerParams(vmem_limit_bytes=16 * 2**20),
        name="pack",
    )(adapter_slot, adapter_id.reshape(1, rows), hidden)


def adapt_kernel(chunk, arrived_ref, a_ref, b_ref, change_ref, held_ref, sems):
    width = a_ref.shape[0]
    spans = [(c, min(chunk, width + LANES - c)) for c in range(0, width + LANES, chunk)]
    copies = [
        pltpu.make_async_copy(
            arrived_ref.at[:, pl.ds(at, size)], held_ref.at[:, pl.ds(at, size)], sems.at[i]
        )
        for i, (at, size) in enumerate(spans)
    ]
    for copy in copies:
        copy.start()
    low = jnp.zeros((arrived_ref.shape[0], a_ref.shape[1]), jnp.float32)
    for copy, (at, size) in zip(copies, spans):
        copy.wait()
        size = min(size, width - at)
        if size > 0:
            low += jnp.dot(
                held_ref[:, at : at + size],
                a_ref[at : at + size, :],
                preferred_element_type=jnp.float32,
            )
    label = held_ref[:, width:].astype(jnp.float32)[:, :1].astype(jnp.int32)
    column = lax.broadcasted_iota(jnp.int32, low.shape, 1) // RANK
    low = jnp.where(column == label, low, 0.0).astype(jnp.bfloat16)
    out_width = b_ref.shape[1]
    piece = min(1024, out_width)
    for at in range(0, out_width, piece):
        change_ref[:, at : at + piece] = (
            SCALE
            * jnp.dot(low, b_ref[:, at : at + piece], preferred_element_type=jnp.float32)
        ).astype(change_ref.dtype)


def adapt(arrived, a_maps, b_maps):
    bins = arrived.shape[0]
    chunk = 2048
    chunks = -(-arrived.shape[1] // chunk)
    return pl.pallas_call(
        functools.partial(adapt_kernel, chunk),
        in_specs=[
            pl.BlockSpec(memory_space=pl.ANY),
            pl.BlockSpec(memory_space=pltpu.VMEM),
            pl.BlockSpec(memory_space=pltpu.VMEM),
        ],
        out_specs=pl.BlockSpec(memory_space=pltpu.VMEM),
        out_shape=jax.ShapeDtypeStruct((bins, b_maps.shape[1]), jnp.bfloat16),
        scratch_shapes=[
            pltpu.VMEM(arrived.shape, arrived.dtype),
            pltpu.SemaphoreType.DMA((chunks,)),
        ],
        compiler_params=pltpu.CompilerParams(vmem_limit_bytes=24 * 2**20),
        name="adapt",
    )(arrived, a_maps, b_maps)


def attend_kernel(context, routed_ref, returned_ref, base_ref, kv_ref, len_ref, out_ref, delta_ref):
    rows, width = base_ref.shape
    group = width // (KVH * HEAD)
    span = group * HEAD
    step = ROWS_STEP
    cells = step * context
    for k in range(KVH):
        delta_ref[:, k * span : (k + 1) * span] = lax.dot_general(
            routed_ref[...],
            returned_ref[:, k * span : (k + 1) * span],
            (((0,), (0,)), ((), ())),
            preferred_element_type=jnp.float32,
        ).astype(delta_ref.dtype)
    lane = lax.broadcasted_iota(jnp.int32, (group * step, cells), 1)
    line = lax.broadcasted_iota(jnp.int32, (group * step, cells), 0)
    own = lane // context == lax.rem(line, step)
    position = lax.rem(lane, context)
    factor = 1.0 / jnp.sqrt(jnp.float32(HEAD))

    def tall(ref, at, k):
        return jnp.concatenate(
            [
                ref[pl.ds(at, step), (k * group + g) * HEAD : (k * group + g + 1) * HEAD]
                for g in range(group)
            ],
            axis=0,
        )

    def rows_step(i, carry):
        at = pl.multiple_of(i * step, step)
        live = own & (position < len_ref[pl.ds(i, 1), :])
        for k in range(KVH):
            keys = kv_ref[pl.ds(at, step), 0, :, k * HEAD : (k + 1) * HEAD].reshape(cells, HEAD)
            values = kv_ref[pl.ds(at, step), 1, :, k * HEAD : (k + 1) * HEAD].reshape(cells, HEAD)
            query = jnp.concatenate([tall(base_ref, at, k), tall(delta_ref, at, k)], axis=1)
            scores = lax.dot_general(
                query,
                jnp.concatenate([keys, keys], axis=1),
                (((1,), (1,)), ((), ())),
                preferred_element_type=jnp.float32,
            )
            scores = jnp.where(live, scores * factor, -jnp.inf)
            expo = jnp.exp(scores - jnp.max(scores, axis=1, keepdims=True))
            probs = (expo * (1.0 / jnp.sum(expo, axis=1, keepdims=True))).astype(jnp.bfloat16)
            out = jnp.dot(probs, values, preferred_element_type=jnp.float32).astype(out_ref.dtype)
            for g in range(group):
                out_ref[
                    pl.ds(at, step), (k * group + g) * HEAD : (k * group + g + 1) * HEAD
                ] = out[g * step : (g + 1) * step, :]
        return carry

    lax.fori_loop(0, rows // step, rows_step, 0)


def attend(routed, returned, base_q, kv_cache, cache_len):
    rows = base_q.shape[0]
    context = kv_cache.shape[2]
    lens = jnp.repeat(cache_len, context).reshape(rows // ROWS_STEP, ROWS_STEP * context)
    return pl.pallas_call(
        functools.partial(attend_kernel, context),
        in_specs=[pl.BlockSpec(memory_space=pltpu.VMEM)] * 5,
        out_specs=pl.BlockSpec(memory_space=pltpu.VMEM),
        out_shape=jax.ShapeDtypeStruct(base_q.shape, jnp.bfloat16),
        scratch_shapes=[pltpu.VMEM(base_q.shape, jnp.bfloat16)],
        compiler_params=pltpu.CompilerParams(vmem_limit_bytes=24 * 2**20),
        name="attend",
    )(routed, returned, base_q, kv_cache, lens)


def on_device(hidden, adapter_id, adapter_slot, cache_len, base_q, kv_cache, a_maps, b_maps):
    owners = lax.axis_size("owner")
    rows = hidden.shape[0]
    held = a_maps.shape[1] // RANK
    slot_count = max(2, 2 * ((rows + 2 * owners - 1) // (2 * owners)))
    bins = owners * slot_count
    packed, routed = pack(hidden, adapter_id, adapter_slot, owners, slot_count, held)
    packed = packed.reshape(owners, slot_count, packed.shape[1])
    arrived = lax.all_to_all(packed, "owner", split_axis=0, concat_axis=0, tiled=True)
    change = adapt(arrived.reshape(bins, arrived.shape[2]), a_maps, b_maps)
    change = change.reshape(owners, slot_count, change.shape[1])
    returned = lax.all_to_all(change, "owner", split_axis=0, concat_axis=0, tiled=True)
    return attend(routed, returned.reshape(bins, returned.shape[2]), base_q, kv_cache, cache_len)


def solution(mesh):
    return jax.shard_map(
        on_device,
        mesh=mesh,
        in_specs=(
            P(("groups", "owner"), None),
            P(("groups", "owner")),
            P("groups"),
            P(("groups", "owner")),
            P(("groups", "owner"), None),
            P(("groups", "owner"), None, None, None),
            P(None, "owner"),
            P("owner", None),
        ),
        out_specs=P(("groups", "owner"), None),
        check_vma=False,
    )
```

```python
import functools

import jax
import jax.numpy as jnp
from jax import lax
from jax.experimental import pallas as pl
from jax.experimental.pallas import tpu as pltpu
from jax.sharding import PartitionSpec as P

HEAD = 128
KVH = 4
RANK = 64
LANES = 128
SCALE = 2.0
ROWS_STEP = 16


def routing(owners, slot_count, held, slots_ref, ids_ref):
    ids = ids_ref[...]
    rows = ids.shape[1]

    def look(s, slot):
        return jnp.where(ids == s, slots_ref[s], slot)

    slot = lax.fori_loop(0, slots_ref.shape[0], look, jnp.zeros_like(ids), unroll=8)
    owner = lax.div(slot, held)
    local = slot - owner * held
    owner = owner ^ lax.axis_index("owner")
    hits = owner == lax.broadcasted_iota(jnp.int32, (owners, rows), 0)
    earlier = lax.broadcasted_iota(jnp.int32, (rows, rows), 0) < lax.broadcasted_iota(
        jnp.int32, (rows, rows), 1
    )
    before = jnp.dot(
        hits.astype(jnp.bfloat16), earlier.astype(jnp.bfloat16), preferred_element_type=jnp.float32
    )
    place = jnp.sum(jnp.where(hits, before, 0.0), axis=0, keepdims=True).astype(jnp.int32)
    bins = owner * slot_count + place
    routed = bins == lax.broadcasted_iota(jnp.int32, (owners * slot_count, rows), 0)
    label = jnp.sum(jnp.where(routed, local.astype(jnp.float32), 0.0), axis=1, keepdims=True)
    return routed.astype(jnp.bfloat16), label


def pack_kernel(owners, slot_count, held, slots_ref, ids_ref, hidden_ref, *refs):
    packed_refs, (routed_ref, label_ref) = refs[:owners], refs[owners:]
    step = pl.program_id(0)

    @pl.when(step == 0)
    def _():
        routed, label = routing(owners, slot_count, held, slots_ref, ids_ref)
        routed_ref[...] = routed
        label_ref[...] = jnp.broadcast_to(label, label_ref.shape)

    packed = jnp.dot(routed_ref[...], hidden_ref[...], preferred_element_type=jnp.float32)
    for s, packed_ref in enumerate(packed_refs):
        packed_ref[...] = packed[s * slot_count : (s + 1) * slot_count].astype(packed_ref.dtype)

    @pl.when(step == pl.num_programs(0) - 1)
    def _():
        for s, packed_ref in enumerate(packed_refs):
            packed_ref[:, packed_ref.shape[1] - LANES :] = label_ref[
                s * slot_count : (s + 1) * slot_count
            ].astype(packed_ref.dtype)


def pack(hidden, adapter_id, adapter_slot, owners, slot_count, held):
    rows, width = hidden.shape
    bins = owners * slot_count
    total = width + LANES
    steps = next(n for n in range(4, total // LANES + 1) if total % (n * LANES) == 0)
    block = total // steps
    return pl.pallas_call(
        functools.partial(pack_kernel, owners, slot_count, held),
        grid=(steps,),
        in_specs=[
            pl.BlockSpec(memory_space=pltpu.SMEM),
            pl.BlockSpec((1, rows), lambda i: (0, 0)),
            pl.BlockSpec((rows, block), lambda i: (0, i)),
        ],
        out_specs=[pl.BlockSpec((slot_count, block), lambda i: (0, i))] * owners
        + [pl.BlockSpec((bins, rows), lambda i: (0, 0))],
        out_shape=[jax.ShapeDtypeStruct((slot_count, total), hidden.dtype)] * owners
        + [jax.ShapeDtypeStruct((bins, rows), jnp.bfloat16)],
        scratch_shapes=[pltpu.VMEM((bins, LANES), jnp.float32)],
        compiler_params=pltpu.CompilerParams(vmem_limit_bytes=16 * 2**20),
        name="pack",
    )(adapter_slot, adapter_id.reshape(1, rows), hidden)


def stack(refs, columns):
    return jnp.concatenate([ref[:, columns].astype(jnp.float32) for ref in refs], axis=0).astype(
        jnp.bfloat16
    )


def adapt_kernel(count, *refs):
    arrived_refs, (a_ref, b_ref), change_refs = refs[:count], refs[count : count + 2], refs[count + 2 :]
    width = a_ref.shape[0]
    slot_count = arrived_refs[0].shape[0]
    chunk = 2048
    low = jnp.zeros((count * slot_count, a_ref.shape[1]), jnp.float32)
    for at in range(0, width, chunk):
        low += jnp.dot(
            stack(arrived_refs, slice(at, at + chunk)),
            a_ref[at : at + chunk, :],
            preferred_element_type=jnp.float32,
        )
    label = stack(arrived_refs, slice(width, width + LANES)).astype(jnp.float32)[:, :1]
    column = lax.broadcasted_iota(jnp.int32, low.shape, 1) // RANK
    low = jnp.where(column == label.astype(jnp.int32), low, 0.0).astype(jnp.bfloat16)
    out_width = b_ref.shape[1]
    piece = min(1024, out_width)
    for at in range(0, out_width, piece):
        change = SCALE * jnp.dot(low, b_ref[:, at : at + piece], preferred_element_type=jnp.float32)
        for i, change_ref in enumerate(change_refs):
            change_ref[:, at : at + piece] = change[i * slot_count : (i + 1) * slot_count].astype(
                change_ref.dtype
            )


def adapt(arrived, a_maps, b_maps):
    count = len(arrived)
    slot_count = arrived[0].shape[0]
    return pl.pallas_call(
        functools.partial(adapt_kernel, count),
        in_specs=[pl.BlockSpec(memory_space=pltpu.VMEM)] * (count + 2),
        out_specs=[pl.BlockSpec(memory_space=pltpu.VMEM)] * count,
        out_shape=[jax.ShapeDtypeStruct((slot_count, b_maps.shape[1]), jnp.bfloat16)] * count,
        compiler_params=pltpu.CompilerParams(vmem_limit_bytes=16 * 2**20),
        name="adapt",
    )(*arrived, a_maps, b_maps)


def attend_kernel(owners, context, *refs):
    returned_refs = refs[:owners]
    routed_ref, base_ref, kv_ref, len_ref, out_ref, delta_ref = refs[owners:]
    rows, width = base_ref.shape
    group = width // (KVH * HEAD)
    span = group * HEAD
    step = ROWS_STEP
    cells = step * context
    for k in range(KVH):
        delta_ref[:, k * span : (k + 1) * span] = lax.dot_general(
            routed_ref[...],
            stack(returned_refs, slice(k * span, (k + 1) * span)),
            (((0,), (0,)), ((), ())),
            preferred_element_type=jnp.float32,
        ).astype(delta_ref.dtype)
    lane = lax.broadcasted_iota(jnp.int32, (group * step, cells), 1)
    line = lax.broadcasted_iota(jnp.int32, (group * step, cells), 0)
    own = lane // context == lax.rem(line, step)
    position = lax.rem(lane, context)
    factor = 1.0 / jnp.sqrt(jnp.float32(HEAD))

    def tall(ref, at, k):
        return jnp.concatenate(
            [
                ref[pl.ds(at, step), (k * group + g) * HEAD : (k * group + g + 1) * HEAD]
                for g in range(group)
            ],
            axis=0,
        )

    def rows_step(i, carry):
        at = pl.multiple_of(i * step, step)
        live = own & (position < len_ref[pl.ds(i, 1), :])
        for k in range(KVH):
            keys = kv_ref[pl.ds(at, step), 0, :, k * HEAD : (k + 1) * HEAD].reshape(cells, HEAD)
            values = kv_ref[pl.ds(at, step), 1, :, k * HEAD : (k + 1) * HEAD].reshape(cells, HEAD)
            query = jnp.concatenate([tall(base_ref, at, k), tall(delta_ref, at, k)], axis=1)
            scores = lax.dot_general(
                query,
                jnp.concatenate([keys, keys], axis=1),
                (((1,), (1,)), ((), ())),
                preferred_element_type=jnp.float32,
            )
            scores = jnp.where(live, scores * factor, -jnp.inf)
            expo = jnp.exp(scores - jnp.max(scores, axis=1, keepdims=True))
            probs = (expo * (1.0 / jnp.sum(expo, axis=1, keepdims=True))).astype(jnp.bfloat16)
            out = jnp.dot(probs, values, preferred_element_type=jnp.float32).astype(out_ref.dtype)
            for g in range(group):
                out_ref[
                    pl.ds(at, step), (k * group + g) * HEAD : (k * group + g + 1) * HEAD
                ] = out[g * step : (g + 1) * step, :]
        return carry

    lax.fori_loop(0, rows // step, rows_step, 0)


def attend(routed, returned, base_q, kv_cache, cache_len):
    rows = base_q.shape[0]
    context = kv_cache.shape[2]
    lens = jnp.repeat(cache_len, context).reshape(rows // ROWS_STEP, ROWS_STEP * context)
    return pl.pallas_call(
        functools.partial(attend_kernel, len(returned), context),
        in_specs=[pl.BlockSpec(memory_space=pltpu.VMEM)] * (len(returned) + 4),
        out_specs=pl.BlockSpec(memory_space=pltpu.VMEM),
        out_shape=jax.ShapeDtypeStruct(base_q.shape, jnp.bfloat16),
        scratch_shapes=[pltpu.VMEM(base_q.shape, jnp.bfloat16)],
        compiler_params=pltpu.CompilerParams(vmem_limit_bytes=24 * 2**20),
        name="attend",
    )(*returned, routed, base_q, kv_cache, lens)


def on_device(hidden, adapter_id, adapter_slot, cache_len, base_q, kv_cache, a_maps, b_maps):
    owners = lax.axis_size("owner")
    rows = hidden.shape[0]
    held = a_maps.shape[1] // RANK
    slot_count = max(2, 2 * ((rows + 2 * owners - 1) // (2 * owners)))
    *packed, routed = pack(hidden, adapter_id, adapter_slot, owners, slot_count, held)
    send = functools.partial(exchange, owners)
    quarter = max(1, owners // 4)
    groups = [range(at, at + quarter) for at in range(0, owners, quarter)]
    groups = groups[2:] + groups[1::-1]
    arrived = {s: send(s, packed[s]) for group in groups for s in group}
    returned = [None] * owners
    for group in groups[::-1]:
        for s, change in zip(group, adapt([arrived[s] for s in group], a_maps, b_maps)):
            returned[s] = send(s, change)
    return attend(routed, returned, base_q, kv_cache, cache_len)


def exchange(owners, s, message):
    if s == 0:
        return message
    return lax.ppermute(message, "owner", [(i, i ^ s) for i in range(owners)])


def solution(mesh):
    return jax.shard_map(
        on_device,
        mesh=mesh,
        in_specs=(
            P(("groups", "owner"), None),
            P(("groups", "owner")),
            P("groups"),
            P(("groups", "owner")),
            P(("groups", "owner"), None),
            P(("groups", "owner"), None, None, None),
            P(None, "owner"),
            P("owner", None),
        ),
        out_specs=P(("groups", "owner"), None),
        check_vma=False,
    )
```

```python
import functools

import jax
import jax.numpy as jnp
from jax import lax
from jax.experimental import pallas as pl
from jax.experimental.pallas import tpu as pltpu
from jax.sharding import PartitionSpec as P

HEAD = 128
KVH = 4
RANK = 64
LANES = 128
SCALE = 2.0
ROWS_STEP = 8
COLUMNS_STEP = 2048


def routing(owners, slot_count, held, slots_ref, ids_ref):
    ids = ids_ref[...]
    rows = ids.shape[1]

    def look(s, slot):
        return jnp.where(ids == s, slots_ref[s], slot)

    slot = lax.fori_loop(0, slots_ref.shape[0], look, jnp.zeros_like(ids), unroll=8)
    owner = lax.div(slot, held)
    local = slot - owner * held
    hits = owner == lax.broadcasted_iota(jnp.int32, (owners, rows), 0)
    earlier = lax.broadcasted_iota(jnp.int32, (rows, rows), 0) < lax.broadcasted_iota(
        jnp.int32, (rows, rows), 1
    )
    before = jnp.dot(
        hits.astype(jnp.bfloat16), earlier.astype(jnp.bfloat16), preferred_element_type=jnp.float32
    )
    place = jnp.sum(jnp.where(hits, before, 0.0), axis=0, keepdims=True).astype(jnp.int32)
    bins = owner * slot_count + place
    routed = bins == lax.broadcasted_iota(jnp.int32, (owners * slot_count, rows), 0)
    label = jnp.sum(jnp.where(routed, local.astype(jnp.float32), 0.0), axis=1, keepdims=True)
    return routed.astype(jnp.bfloat16), label


def pack_kernel(
    owners, slot_count, held, slots_ref, ids_ref, hidden_ref, packed_ref, routed_ref, rows_ref, bins_ref, sems, out_sems
):
    width = hidden_ref.shape[1]
    spans = [pl.ds(at, min(COLUMNS_STEP, width - at)) for at in range(0, width, COLUMNS_STEP)]
    loads = [
        pltpu.make_async_copy(hidden_ref.at[:, span], rows_ref.at[:, span], sems.at[i])
        for i, span in enumerate(spans)
    ]
    spans[-1] = pl.ds(spans[-1].start, spans[-1].size + LANES)
    stores = [
        pltpu.make_async_copy(bins_ref.at[:, span], packed_ref.at[:, span], out_sems.at[i])
        for i, span in enumerate(spans)
    ]
    for load in loads:
        load.start()
    routed, label = routing(owners, slot_count, held, slots_ref, ids_ref)
    routed_ref[...] = jnp.transpose(routed.astype(jnp.float32)).astype(routed_ref.dtype)
    bins_ref[:, width:] = jnp.broadcast_to(label, (label.shape[0], LANES)).astype(bins_ref.dtype)
    for load, store, span in zip(loads, stores, spans):
        load.wait()
        at, end = span.start, min(span.start + span.size, width)
        bins_ref[:, at:end] = jnp.dot(
            routed, rows_ref[:, at:end], preferred_element_type=jnp.float32
        ).astype(bins_ref.dtype)
        store.start()
    for store in stores:
        store.wait()


def pack(hidden, adapter_id, adapter_slot, owners, slot_count, held):
    rows, width = hidden.shape
    bins = owners * slot_count
    steps = pl.cdiv(width, COLUMNS_STEP)
    return pl.pallas_call(
        functools.partial(pack_kernel, owners, slot_count, held),
        in_specs=[
            pl.BlockSpec(memory_space=pltpu.SMEM),
            pl.BlockSpec(memory_space=pltpu.VMEM),
            pl.BlockSpec(memory_space=pl.ANY),
        ],
        out_specs=[pl.BlockSpec(memory_space=pl.ANY), pl.BlockSpec(memory_space=pltpu.VMEM)],
        out_shape=[
            jax.ShapeDtypeStruct((bins, width + LANES), hidden.dtype),
            jax.ShapeDtypeStruct((rows, bins), jnp.bfloat16),
        ],
        scratch_shapes=[
            pltpu.VMEM((rows, width), hidden.dtype),
            pltpu.VMEM((bins, width + LANES), hidden.dtype),
            pltpu.SemaphoreType.DMA((steps,)),
            pltpu.SemaphoreType.DMA((steps,)),
        ],
        compiler_params=pltpu.CompilerParams(vmem_limit_bytes=56 * 2**20),
        name="pack",
    )(adapter_slot, adapter_id.reshape(1, rows), hidden)


def adapt_kernel(arrived_ref, a_ref, b_ref, change_ref):
    width = a_ref.shape[0]
    low = jnp.zeros((arrived_ref.shape[0], a_ref.shape[1]), jnp.float32)
    for at in range(0, width, COLUMNS_STEP):
        low += jnp.dot(
            arrived_ref[:, at : at + COLUMNS_STEP],
            a_ref[at : at + COLUMNS_STEP, :],
            preferred_element_type=jnp.float32,
        )
    label = arrived_ref[:, width:].astype(jnp.float32)[:, :1].astype(jnp.int32)
    column = lax.broadcasted_iota(jnp.int32, low.shape, 1) // RANK
    low = jnp.where(column == label, low, 0.0).astype(jnp.bfloat16)
    out_width = b_ref.shape[1]
    piece = min(1024, out_width)
    for at in range(0, out_width, piece):
        change_ref[:, at : at + piece] = (
            SCALE * jnp.dot(low, b_ref[:, at : at + piece], preferred_element_type=jnp.float32)
        ).astype(change_ref.dtype)


def adapt(arrived, a_maps, b_maps):
    return pl.pallas_call(
        adapt_kernel,
        in_specs=[pl.BlockSpec(memory_space=pltpu.VMEM)] * 3,
        out_specs=pl.BlockSpec(memory_space=pltpu.VMEM),
        out_shape=jax.ShapeDtypeStruct((arrived.shape[0], b_maps.shape[1]), jnp.bfloat16),
        compiler_params=pltpu.CompilerParams(vmem_limit_bytes=16 * 2**20),
        name="adapt",
    )(arrived, a_maps, b_maps)


def tall(rows, group):
    return jnp.concatenate([rows[:, g * HEAD : (g + 1) * HEAD] for g in range(group)], axis=0)


def prep_kernel(group, context, base_ref, kv_ref, len_ref, keys_ref, values_ref, scores_ref):
    step = ROWS_STEP
    cells = step * context
    lane = lax.broadcasted_iota(jnp.int32, (group * step, cells), 1)
    line = lax.broadcasted_iota(jnp.int32, (group * step, cells), 0)
    live = (lane // context == lax.rem(line, step)) & (lax.rem(lane, context) < len_ref[...][0])
    factor = 1.0 / jnp.sqrt(jnp.float32(HEAD))
    for k in range(KVH):
        head = slice(k * HEAD, (k + 1) * HEAD)
        keys = kv_ref[:, 0, :, head].astype(jnp.float32).reshape(cells, HEAD)
        keys = jnp.transpose(keys).astype(keys_ref.dtype)
        keys_ref[k] = keys
        values_ref[k] = kv_ref[:, 1, :, head].reshape(cells, HEAD)
        base = base_ref[:, k * group * HEAD : (k + 1) * group * HEAD].astype(jnp.float32)
        scores = jnp.dot(
            tall(base, group).astype(jnp.bfloat16), keys, preferred_element_type=jnp.float32
        )
        scores_ref[k, 0] = jnp.where(live, scores * factor, -jnp.inf)


def prep(base_q, kv_cache, cache_len):
    rows, width = base_q.shape
    context = kv_cache.shape[2]
    group = width // (KVH * HEAD)
    step = ROWS_STEP
    steps = rows // step
    cells = step * context
    lens = jnp.repeat(cache_len, context).reshape(steps, 1, cells)
    return pl.pallas_call(
        functools.partial(prep_kernel, group, context),
        grid=(steps,),
        in_specs=[
            pl.BlockSpec((step, width), lambda i: (i, 0)),
            pl.BlockSpec((step, *kv_cache.shape[1:]), lambda i: (i, 0, 0, 0)),
            pl.BlockSpec((1, 1, cells), lambda i: (i, 0, 0)),
        ],
        out_specs=[
            pl.BlockSpec((KVH, HEAD, cells), lambda i: (0, 0, i)),
            pl.BlockSpec((KVH, cells, HEAD), lambda i: (0, i, 0)),
            pl.BlockSpec((KVH, 1, group * step, cells), lambda i: (0, i, 0, 0)),
        ],
        out_shape=[
            jax.ShapeDtypeStruct((KVH, HEAD, rows * context), jnp.bfloat16),
            jax.ShapeDtypeStruct((KVH, rows * context, HEAD), jnp.bfloat16),
            jax.ShapeDtypeStruct((KVH, steps, group * step, cells), jnp.float32),
        ],
        compiler_params=pltpu.CompilerParams(vmem_limit_bytes=16 * 2**20),
        cost_estimate=pl.CostEstimate(
            flops=2 * rows * width * cells, bytes_accessed=16 * 2**20, transcendentals=0
        ),
        name="prep",
    )(base_q, kv_cache, lens)


def attend_kernel(group, routed_ref, returned_ref, keys_ref, values_ref, scores_ref, out_ref):
    step = ROWS_STEP
    steps, _, cells = scores_ref.shape[1:]
    span = group * HEAD
    factor = 1.0 / jnp.sqrt(jnp.float32(HEAD))
    for k in range(KVH):
        delta = jnp.dot(
            routed_ref[...],
            returned_ref[:, k * span : (k + 1) * span],
            preferred_element_type=jnp.float32,
        )
        for i in range(steps):
            lines = slice(i * step, (i + 1) * step)
            at = slice(i * cells, (i + 1) * cells)
            change = jnp.dot(
                tall(delta[lines], group).astype(jnp.bfloat16),
                keys_ref[k, :, at],
                preferred_element_type=jnp.float32,
            )
            scores = scores_ref[k, i] + change * factor
            expo = jnp.exp(scores - jnp.max(scores, axis=1, keepdims=True))
            probs = expo * (1.0 / jnp.sum(expo, axis=1, keepdims=True))
            out = jnp.dot(
                probs.astype(jnp.bfloat16), values_ref[k, at, :], preferred_element_type=jnp.float32
            )
            for g in range(group):
                out_ref[lines, (k * group + g) * HEAD : (k * group + g + 1) * HEAD] = out[
                    g * step : (g + 1) * step
                ].astype(out_ref.dtype)


def attend(routed, returned, keys, values, scores):
    rows, width = routed.shape[0], returned.shape[1]
    return pl.pallas_call(
        functools.partial(attend_kernel, width // (KVH * HEAD)),
        in_specs=[pl.BlockSpec(memory_space=pltpu.VMEM)] * 5,
        out_specs=pl.BlockSpec(memory_space=pltpu.VMEM),
        out_shape=jax.ShapeDtypeStruct((rows, width), jnp.bfloat16),
        compiler_params=pltpu.CompilerParams(vmem_limit_bytes=24 * 2**20),
        name="attend",
    )(routed, returned, keys, values, scores)


def on_device(hidden, adapter_id, adapter_slot, cache_len, base_q, kv_cache, a_maps, b_maps):
    owners = lax.axis_size("owner")
    rows = hidden.shape[0]
    held = a_maps.shape[1] // RANK
    slot_count = max(2, 2 * ((rows + 2 * owners - 1) // (2 * owners)))
    bins = owners * slot_count
    packed, routed = pack(hidden, adapter_id, adapter_slot, owners, slot_count, held)
    packed = packed.reshape(owners, slot_count, packed.shape[1])
    arrived = lax.all_to_all(packed, "owner", split_axis=0, concat_axis=0, tiled=True)
    keys, values, scores = prep(base_q, kv_cache, cache_len)
    change = adapt(arrived.reshape(bins, arrived.shape[2]), a_maps, b_maps)
    change = change.reshape(owners, slot_count, change.shape[1])
    returned = lax.all_to_all(change, "owner", split_axis=0, concat_axis=0, tiled=True)
    return attend(routed, returned.reshape(bins, returned.shape[2]), keys, values, scores)


def solution(mesh):
    return jax.shard_map(
        on_device,
        mesh=mesh,
        in_specs=(
            P(("groups", "owner"), None),
            P(("groups", "owner")),
            P("groups"),
            P(("groups", "owner")),
            P(("groups", "owner"), None),
            P(("groups", "owner"), None, None, None),
            P(None, "owner"),
            P("owner", None),
        ),
        out_specs=P(("groups", "owner"), None),
        check_vma=False,
    )
```

```python
import functools

import jax
import jax.numpy as jnp
from jax import lax
from jax.experimental import pallas as pl
from jax.experimental.pallas import tpu as pltpu
from jax.sharding import PartitionSpec as P

HEAD = 128
KVH = 4
RANK = 64
LANES = 128
SCALE = 2.0
ROWS_STEP = 8
COLUMNS_STEP = 2048
HALVES = 2


def fold_of(bins, slot_count, columns):
    line = lax.broadcasted_iota(jnp.int32, (bins, columns), 0)
    return lax.rem(line, slot_count) // (slot_count // HALVES)


def routing(chunk, owners, slot_count, held, slots_ref, ids_ref):
    ids = ids_ref[...]
    rows = ids.shape[1]
    bins = owners * slot_count
    part = slot_count // HALVES

    def look(s, slot):
        return jnp.where(ids == s, slots_ref[s], slot)

    slot = lax.fori_loop(0, slots_ref.shape[0], look, jnp.zeros_like(ids), unroll=8)
    owner = lax.div(slot, held)
    local = slot - owner * held
    hits = owner == lax.broadcasted_iota(jnp.int32, (owners, rows), 0)
    earlier = lax.broadcasted_iota(jnp.int32, (rows, rows), 0) < lax.broadcasted_iota(
        jnp.int32, (rows, rows), 1
    )
    before = jnp.dot(
        hits.astype(jnp.bfloat16), earlier.astype(jnp.bfloat16), preferred_element_type=jnp.float32
    )
    place = jnp.sum(jnp.where(hits, before, 0.0), axis=0, keepdims=True).astype(jnp.int32)
    line = lax.broadcasted_iota(jnp.int32, (bins, rows), 0)
    fold = fold_of(bins, slot_count, rows)
    routed = line + (chunk - fold) * part == owner * slot_count + place
    label = jnp.sum(jnp.where(routed, local.astype(jnp.float32), 0.0), axis=1, keepdims=True)
    return [(routed & (fold == f)).astype(jnp.float32) for f in range(HALVES)], label


def pack_kernel(
    chunk, owners, slot_count, held, slots_ref, ids_ref, hidden_ref, packed_ref, routed_ref, rows_ref, bins_ref, sems, out_sems
):
    rows, width = hidden_ref.shape
    half = width // HALVES
    spans = [(at, min(COLUMNS_STEP, half - at)) for at in range(0, half, COLUMNS_STEP)]
    loads = [
        [
            pltpu.make_async_copy(
                hidden_ref.at[:, pl.ds(f * half + at, size)],
                rows_ref.at[pl.ds(f * rows, rows), pl.ds(at, size)],
                sems.at[i, f],
            )
            for f in range(HALVES)
        ]
        for i, (at, size) in enumerate(spans)
    ]
    stores = [
        pltpu.make_async_copy(
            bins_ref.at[:, pl.ds(at, size)], packed_ref.at[:, pl.ds(at, size)], out_sems.at[i]
        )
        for i, (at, size) in enumerate([(half, LANES)] + spans)
    ]
    for load in loads:
        for copy in load:
            copy.start()
    routed, label = routing(chunk, owners, slot_count, held, slots_ref, ids_ref)
    bins_ref[:, half:] = jnp.broadcast_to(label, (label.shape[0], LANES)).astype(bins_ref.dtype)
    stores[0].start()
    folded = jnp.concatenate(routed, axis=1).astype(jnp.bfloat16)
    for load, store, (at, size) in zip(loads, stores[1:], spans):
        for copy in load:
            copy.wait()
        bins_ref[:, at : at + size] = jnp.dot(
            folded, rows_ref[:, at : at + size], preferred_element_type=jnp.float32
        ).astype(bins_ref.dtype)
        store.start()
    for f in range(HALVES):
        routed_ref[f] = jnp.transpose(routed[f]).astype(routed_ref.dtype)
    for store in stores:
        store.wait()


def pack(hidden, adapter_id, adapter_slot, chunk, owners, slot_count, held):
    rows, width = hidden.shape
    half = width // HALVES
    bins = owners * slot_count
    steps = pl.cdiv(half, COLUMNS_STEP)
    return pl.pallas_call(
        functools.partial(pack_kernel, chunk, owners, slot_count, held),
        in_specs=[
            pl.BlockSpec(memory_space=pltpu.SMEM),
            pl.BlockSpec(memory_space=pltpu.VMEM),
            pl.BlockSpec(memory_space=pl.ANY),
        ],
        out_specs=[pl.BlockSpec(memory_space=pl.ANY), pl.BlockSpec(memory_space=pltpu.VMEM)],
        out_shape=[
            jax.ShapeDtypeStruct((bins, half + LANES), hidden.dtype),
            jax.ShapeDtypeStruct((HALVES, rows, bins), jnp.bfloat16),
        ],
        scratch_shapes=[
            pltpu.VMEM((HALVES * rows, half), hidden.dtype),
            pltpu.VMEM((bins, half + LANES), hidden.dtype),
            pltpu.SemaphoreType.DMA((steps, HALVES)),
            pltpu.SemaphoreType.DMA((steps + 1,)),
        ],
        compiler_params=pltpu.CompilerParams(vmem_limit_bytes=56 * 2**20),
        name="pack",
    )(adapter_slot, adapter_id.reshape(1, rows), hidden)


def adapt_kernel(slot_count, arrived_ref, a_ref, b_ref, change_ref):
    bins = arrived_ref.shape[0]
    half = a_ref.shape[0] // HALVES
    columns = a_ref.shape[1]
    part = slot_count // HALVES
    both = jnp.zeros((bins, HALVES * columns), jnp.float32)
    for at in range(0, half, COLUMNS_STEP):
        both += jnp.dot(
            arrived_ref[:, at : at + COLUMNS_STEP],
            jnp.concatenate(
                [a_ref[f * half + at : f * half + at + COLUMNS_STEP, :] for f in range(HALVES)], axis=1
            ),
            preferred_element_type=jnp.float32,
        )
    upper = fold_of(bins, slot_count, columns) == 0
    low = jnp.where(upper, both[:, :columns], both[:, columns:])
    low += jnp.where(upper, pltpu.roll(low, bins - part, 0), pltpu.roll(low, part, 0))
    label = arrived_ref[:, half:].astype(jnp.float32)[:, :1].astype(jnp.int32)
    column = lax.broadcasted_iota(jnp.int32, low.shape, 1) // RANK
    low = jnp.where(column == label, low, 0.0)
    low = jnp.concatenate([jnp.where(upper, low, 0.0), jnp.where(upper, 0.0, low)], axis=1)
    low = low.astype(jnp.bfloat16)
    half_out = b_ref.shape[1] // HALVES
    piece = min(1024, half_out)
    for at in range(0, half_out, piece):
        b = jnp.concatenate(
            [b_ref[:, f * half_out + at : f * half_out + at + piece] for f in range(HALVES)], axis=0
        )
        change_ref[:, at : at + piece] = (
            SCALE * jnp.dot(low, b, preferred_element_type=jnp.float32)
        ).astype(change_ref.dtype)


def adapt(arrived, a_maps, b_maps, slot_count):
    return pl.pallas_call(
        functools.partial(adapt_kernel, slot_count),
        in_specs=[pl.BlockSpec(memory_space=pltpu.VMEM)] * 3,
        out_specs=pl.BlockSpec(memory_space=pltpu.VMEM),
        out_shape=jax.ShapeDtypeStruct((arrived.shape[0], b_maps.shape[1] // HALVES), jnp.bfloat16),
        compiler_params=pltpu.CompilerParams(vmem_limit_bytes=16 * 2**20),
        cost_estimate=pl.CostEstimate(
            flops=4 * arrived.shape[0] * a_maps.size, bytes_accessed=4 * 2**20, transcendentals=0
        ),
        name="adapt",
    )(arrived, a_maps, b_maps)


def tall(rows, group):
    return jnp.concatenate([rows[:, g * HEAD : (g + 1) * HEAD] for g in range(group)], axis=0)


def prep_kernel(group, context, base_ref, kv_ref, len_ref, keys_ref, values_ref, scores_ref):
    step = ROWS_STEP
    cells = step * context
    lane = lax.broadcasted_iota(jnp.int32, (group * step, cells), 1)
    line = lax.broadcasted_iota(jnp.int32, (group * step, cells), 0)
    live = (lane // context == lax.rem(line, step)) & (lax.rem(lane, context) < len_ref[...][0])
    factor = 1.0 / jnp.sqrt(jnp.float32(HEAD))
    for k in range(KVH):
        head = slice(k * HEAD, (k + 1) * HEAD)
        keys = kv_ref[:, 0, :, head].astype(jnp.float32).reshape(cells, HEAD)
        keys = jnp.transpose(keys).astype(keys_ref.dtype)
        keys_ref[k] = keys
        values_ref[k] = kv_ref[:, 1, :, head].reshape(cells, HEAD)
        base = base_ref[:, k * group * HEAD : (k + 1) * group * HEAD].astype(jnp.float32)
        scores = jnp.dot(
            tall(base, group).astype(jnp.bfloat16), keys, preferred_element_type=jnp.float32
        )
        scores_ref[k, 0] = jnp.where(live, scores * factor, -jnp.inf)


def prep(base_q, kv_cache, cache_len):
    rows, width = base_q.shape
    context = kv_cache.shape[2]
    group = width // (KVH * HEAD)
    step = ROWS_STEP
    steps = rows // step
    cells = step * context
    lens = jnp.repeat(cache_len, context).reshape(steps, 1, cells)
    return pl.pallas_call(
        functools.partial(prep_kernel, group, context),
        grid=(steps,),
        in_specs=[
            pl.BlockSpec((step, width), lambda i: (i, 0)),
            pl.BlockSpec((step, *kv_cache.shape[1:]), lambda i: (i, 0, 0, 0)),
            pl.BlockSpec((1, 1, cells), lambda i: (i, 0, 0)),
        ],
        out_specs=[
            pl.BlockSpec((KVH, HEAD, cells), lambda i: (0, 0, i)),
            pl.BlockSpec((KVH, cells, HEAD), lambda i: (0, i, 0)),
            pl.BlockSpec((KVH, 1, group * step, cells), lambda i: (0, i, 0, 0)),
        ],
        out_shape=[
            jax.ShapeDtypeStruct((KVH, HEAD, rows * context), jnp.bfloat16),
            jax.ShapeDtypeStruct((KVH, rows * context, HEAD), jnp.bfloat16),
            jax.ShapeDtypeStruct((KVH, steps, group * step, cells), jnp.float32),
        ],
        compiler_params=pltpu.CompilerParams(vmem_limit_bytes=16 * 2**20),
        cost_estimate=pl.CostEstimate(
            flops=2 * rows * width * cells, bytes_accessed=16 * 2**20, transcendentals=0
        ),
        name="prep",
    )(base_q, kv_cache, lens)


def attend_kernel(group, *refs):
    routed_refs, returned_refs, refs = refs[:HALVES], refs[HALVES : 2 * HALVES], refs[2 * HALVES :]
    laid_refs, (out_ref, *held_refs, sems) = refs[:3], refs[3:]
    keys_ref, values_ref, scores_ref = held_refs
    step = ROWS_STEP
    steps, _, cells = scores_ref.shape[1:]
    span = group * HEAD
    heads = KVH // HALVES
    factor = 1.0 / jnp.sqrt(jnp.float32(HEAD))
    copies = [
        [
            pltpu.make_async_copy(laid_ref.at[k], held_ref.at[k], sems.at[k, i])
            for i, (laid_ref, held_ref) in enumerate(zip(laid_refs, held_refs))
        ]
        for k in range(KVH)
    ]
    for copy in copies:
        for one in copy:
            one.start()
    for k in range(KVH):
        fold, at = k // heads, k % heads * span
        delta = jnp.dot(
            jnp.concatenate([routed_ref[fold] for routed_ref in routed_refs], axis=1),
            jnp.concatenate(
                [returned_ref[:, at : at + span] for returned_ref in returned_refs], axis=0
            ),
            preferred_element_type=jnp.float32,
        )
        for one in copies[k]:
            one.wait()
        for i in range(steps):
            lines = slice(i * step, (i + 1) * step)
            at = slice(i * cells, (i + 1) * cells)
            change = jnp.dot(
                tall(delta[lines], group).astype(jnp.bfloat16),
                keys_ref[k, :, at],
                preferred_element_type=jnp.float32,
            )
            scores = scores_ref[k, i] + change * factor
            expo = jnp.exp(scores - jnp.max(scores, axis=1, keepdims=True))
            probs = expo * (1.0 / jnp.sum(expo, axis=1, keepdims=True))
            out = jnp.dot(
                probs.astype(jnp.bfloat16), values_ref[k, at, :], preferred_element_type=jnp.float32
            )
            for g in range(group):
                out_ref[lines, (k * group + g) * HEAD : (k * group + g + 1) * HEAD] = out[
                    g * step : (g + 1) * step
                ].astype(out_ref.dtype)


def attend(routed, returned, laid, width):
    rows = routed[0].shape[1]
    return pl.pallas_call(
        functools.partial(attend_kernel, width // (KVH * HEAD)),
        in_specs=[pl.BlockSpec(memory_space=pltpu.VMEM)] * (2 * HALVES)
        + [pl.BlockSpec(memory_space=pl.ANY)] * len(laid),
        out_specs=pl.BlockSpec(memory_space=pltpu.VMEM),
        out_shape=jax.ShapeDtypeStruct((rows, width), jnp.bfloat16),
        scratch_shapes=[pltpu.VMEM(part.shape, part.dtype) for part in laid]
        + [pltpu.SemaphoreType.DMA((KVH, len(laid)))],
        compiler_params=pltpu.CompilerParams(vmem_limit_bytes=56 * 2**20),
        name="attend",
    )(*routed, *returned, *laid)


def on_device(hidden, adapter_id, adapter_slot, cache_len, base_q, kv_cache, a_maps, b_maps):
    owners = lax.axis_size("owner")
    rows = hidden.shape[0]
    held = a_maps.shape[1] // RANK
    slot_count = max(2, 2 * ((rows + 2 * owners - 1) // (2 * owners)))

    def swap(message):
        blocks = message.reshape(owners, slot_count, message.shape[1])
        blocks = lax.all_to_all(blocks, "owner", split_axis=0, concat_axis=0, tiled=True)
        return blocks.reshape(message.shape)

    routed, arrived = [], []
    for chunk in range(HALVES):
        packed, hits = pack(hidden, adapter_id, adapter_slot, chunk, owners, slot_count, held)
        routed.append(hits)
        if chunk > 0:
            arrived[0], packed = lax.optimization_barrier((arrived[0], packed))
        arrived.append(swap(packed))
    laid = prep(base_q, kv_cache, cache_len)
    arrived[0], *laid = lax.optimization_barrier((arrived[0], *laid))
    returned = [swap(adapt(rows_in, a_maps, b_maps, slot_count)) for rows_in in arrived]
    return attend(routed, returned, laid, base_q.shape[1])


def solution(mesh):
    return jax.shard_map(
        on_device,
        mesh=mesh,
        in_specs=(
            P(("groups", "owner"), None),
            P(("groups", "owner")),
            P("groups"),
            P(("groups", "owner")),
            P(("groups", "owner"), None),
            P(("groups", "owner"), None, None, None),
            P(None, "owner"),
            P("owner", None),
        ),
        out_specs=P(("groups", "owner"), None),
        check_vma=False,
    )
```

```python
import functools

import jax
import jax.numpy as jnp
from jax import lax
from jax.experimental import pallas as pl
from jax.experimental.pallas import tpu as pltpu
from jax.sharding import PartitionSpec as P

HEAD = 128
KVH = 4
RANK = 64
LANES = 128
SCALE = 2.0
ROWS_STEP = 8
COLUMNS_STEP = 2048


def place_of(index, quarter):
    return lax.div(index, 2 * quarter) * quarter + lax.rem(index, quarter)


def routing(pairs, owners, slot_count, held, slots_ref, ids_ref):
    ids = ids_ref[...]
    rows = ids.shape[1]
    quarter = owners // 4

    def look(s, slot):
        return jnp.where(ids == s, slots_ref[s], slot)

    slot = lax.fori_loop(0, slots_ref.shape[0], look, jnp.zeros_like(ids), unroll=8)
    owner = lax.div(slot, held)
    local = slot - owner * held
    hits = owner == lax.broadcasted_iota(jnp.int32, (owners, rows), 0)
    earlier = lax.broadcasted_iota(jnp.int32, (rows, rows), 0) < lax.broadcasted_iota(
        jnp.int32, (rows, rows), 1
    )
    before = jnp.dot(
        hits.astype(jnp.bfloat16), earlier.astype(jnp.bfloat16), preferred_element_type=jnp.float32
    )
    place = jnp.sum(jnp.where(hits, before, 0.0), axis=0, keepdims=True).astype(jnp.int32)
    apart = owner ^ lax.axis_index("owner")
    message = place_of(apart if pairs else owner, quarter)
    meant = lax.rem(lax.div(apart, quarter), 2) == (1 if pairs else 0)
    line = lax.broadcasted_iota(jnp.int32, (owners // 2 * slot_count, rows), 0)
    routed = line == jnp.where(meant, message * slot_count + place, -1)
    label = jnp.sum(jnp.where(routed, local.astype(jnp.float32), 0.0), axis=1, keepdims=True)
    return routed.astype(jnp.bfloat16), label


def pack_kernel(
    pairs, owners, slot_count, held, slots_ref, ids_ref, hidden_ref, after_ref, routed_ref, *refs
):
    *packed_refs, rows_ref, sems = refs
    width = hidden_ref.shape[1]
    spans = [(at, min(COLUMNS_STEP, width - at)) for at in range(0, width, COLUMNS_STEP)]
    loads = [
        pltpu.make_async_copy(
            hidden_ref.at[:, pl.ds(at, size)], rows_ref.at[:, pl.ds(at, size)], sems.at[i]
        )
        for i, (at, size) in enumerate(spans)
    ]
    for load in loads:
        load.start()
    routed, label = routing(pairs, owners, slot_count, held, slots_ref, ids_ref)
    routed_ref[...] = routed
    label = jnp.broadcast_to(label, (label.shape[0], LANES))
    count = packed_refs[0].shape[0]

    def put(at, lines):
        for i, packed_ref in enumerate(packed_refs):
            packed_ref[:, at : at + lines.shape[1]] = lines[i * count : (i + 1) * count].astype(
                packed_ref.dtype
            )

    put(width, label)
    for load, (at, size) in zip(loads, spans):
        load.wait()
        put(at, jnp.dot(routed, rows_ref[:, at : at + size], preferred_element_type=jnp.float32))


def pack(hidden, adapter_id, adapter_slot, after, pairs, owners, slot_count, held):
    rows, width = hidden.shape
    lines = owners // 2 * slot_count
    messages = owners // 2 if pairs else 1
    steps = pl.cdiv(width, COLUMNS_STEP)
    return pl.pallas_call(
        functools.partial(pack_kernel, pairs, owners, slot_count, held),
        in_specs=[
            pl.BlockSpec(memory_space=pltpu.SMEM),
            pl.BlockSpec(memory_space=pltpu.VMEM),
            pl.BlockSpec(memory_space=pl.ANY),
            pl.BlockSpec(memory_space=pl.ANY),
        ],
        out_specs=[pl.BlockSpec(memory_space=pltpu.VMEM)] * (1 + messages),
        out_shape=[jax.ShapeDtypeStruct((lines, rows), jnp.bfloat16)]
        + [jax.ShapeDtypeStruct((lines // messages, width + LANES), hidden.dtype)] * messages,
        scratch_shapes=[
            pltpu.VMEM((rows, width), hidden.dtype),
            pltpu.SemaphoreType.DMA((steps,)),
        ],
        compiler_params=pltpu.CompilerParams(vmem_limit_bytes=56 * 2**20),
        name="pack_pairs" if pairs else "pack",
    )(adapter_slot, adapter_id.reshape(1, rows), hidden, after)


def stack(refs, at, size):
    if len(refs) == 1:
        return refs[0][:, at : at + size]
    return jnp.concatenate(
        [ref[:, at : at + size].astype(jnp.float32) for ref in refs], axis=0
    ).astype(jnp.bfloat16)


def adapt_kernel(count, *refs):
    arrived_refs, (a_ref, b_ref, _), change_refs = refs[:count], refs[count : count + 3], refs[count + 3 :]
    width = a_ref.shape[0]
    lines = arrived_refs[0].shape[0]
    low = jnp.zeros((count * lines, a_ref.shape[1]), jnp.float32)
    for at in range(0, width, COLUMNS_STEP):
        low += jnp.dot(
            stack(arrived_refs, at, COLUMNS_STEP),
            a_ref[at : at + COLUMNS_STEP, :],
            preferred_element_type=jnp.float32,
        )
    label = stack(arrived_refs, width, LANES).astype(jnp.float32)[:, :1].astype(jnp.int32)
    column = lax.broadcasted_iota(jnp.int32, low.shape, 1) // RANK
    low = jnp.where(column == label, low, 0.0).astype(jnp.bfloat16)
    out_width = b_ref.shape[1]
    piece = min(1024, out_width)
    for at in range(0, out_width, piece):
        change = SCALE * jnp.dot(low, b_ref[:, at : at + piece], preferred_element_type=jnp.float32)
        for i, change_ref in enumerate(change_refs):
            change_ref[:, at : at + piece] = change[i * lines : (i + 1) * lines].astype(
                change_ref.dtype
            )


def adapt(arrived, a_maps, b_maps, after):
    count = len(arrived)
    lines = arrived[0].shape[0]
    return pl.pallas_call(
        functools.partial(adapt_kernel, count),
        in_specs=[pl.BlockSpec(memory_space=pltpu.VMEM)] * (count + 2)
        + [pl.BlockSpec(memory_space=pl.ANY)],
        out_specs=[pl.BlockSpec(memory_space=pltpu.VMEM)] * count,
        out_shape=[jax.ShapeDtypeStruct((lines, b_maps.shape[1]), jnp.bfloat16)] * count,
        compiler_params=pltpu.CompilerParams(vmem_limit_bytes=16 * 2**20),
        cost_estimate=pl.CostEstimate(
            flops=2 * count * lines * (a_maps.size + b_maps.size),
            bytes_accessed=2 * (a_maps.size + b_maps.size),
            transcendentals=0,
        ),
        name="adapt",
    )(*arrived, a_maps, b_maps, after)


def tall(rows, group):
    return jnp.concatenate([rows[:, g * HEAD : (g + 1) * HEAD] for g in range(group)], axis=0)


def prep_kernel(group, context, base_ref, kv_ref, len_ref, keys_ref, values_ref, scores_ref):
    step = ROWS_STEP
    cells = step * context
    lane = lax.broadcasted_iota(jnp.int32, (group * step, cells), 1)
    line = lax.broadcasted_iota(jnp.int32, (group * step, cells), 0)
    live = (lane // context == lax.rem(line, step)) & (lax.rem(lane, context) < len_ref[...][0])
    factor = 1.0 / jnp.sqrt(jnp.float32(HEAD))
    for k in range(KVH):
        head = slice(k * HEAD, (k + 1) * HEAD)
        keys = kv_ref[:, 0, :, head].astype(jnp.float32).reshape(cells, HEAD)
        keys = jnp.transpose(keys).astype(keys_ref.dtype)
        keys_ref[k] = keys
        values_ref[k] = kv_ref[:, 1, :, head].reshape(cells, HEAD)
        base = base_ref[:, k * group * HEAD : (k + 1) * group * HEAD].astype(jnp.float32)
        scores = jnp.dot(
            tall(base, group).astype(jnp.bfloat16), keys, preferred_element_type=jnp.float32
        )
        scores_ref[k, 0] = jnp.where(live, scores * factor, -jnp.inf)


def prep(base_q, kv_cache, cache_len):
    rows, width = base_q.shape
    context = kv_cache.shape[2]
    group = width // (KVH * HEAD)
    step = ROWS_STEP
    steps = rows // step
    cells = step * context
    lens = jnp.repeat(cache_len, context).reshape(steps, 1, cells)
    return pl.pallas_call(
        functools.partial(prep_kernel, group, context),
        grid=(steps,),
        in_specs=[
            pl.BlockSpec((step, width), lambda i: (i, 0)),
            pl.BlockSpec((step, *kv_cache.shape[1:]), lambda i: (i, 0, 0, 0)),
            pl.BlockSpec((1, 1, cells), lambda i: (i, 0, 0)),
        ],
        out_specs=[
            pl.BlockSpec((KVH, HEAD, cells), lambda i: (0, 0, i)),
            pl.BlockSpec((KVH, cells, HEAD), lambda i: (0, i, 0)),
            pl.BlockSpec((KVH, 1, group * step, cells), lambda i: (0, i, 0, 0)),
        ],
        out_shape=[
            jax.ShapeDtypeStruct((KVH, HEAD, rows * context), jnp.bfloat16),
            jax.ShapeDtypeStruct((KVH, rows * context, HEAD), jnp.bfloat16),
            jax.ShapeDtypeStruct((KVH, steps, group * step, cells), jnp.float32),
        ],
        compiler_params=pltpu.CompilerParams(vmem_limit_bytes=16 * 2**20),
        cost_estimate=pl.CostEstimate(
            flops=2 * rows * width * cells, bytes_accessed=16 * 2**20, transcendentals=0
        ),
        name="prep",
    )(base_q, kv_cache, lens)


def attend_kernel(group, count, *refs):
    routed_refs, returned_refs, refs = refs[:2], refs[2 : 2 + count], refs[2 + count :]
    laid_refs, (out_ref, *held_refs, sems) = refs[:3], refs[3:]
    keys_ref, values_ref, scores_ref = held_refs
    step = ROWS_STEP
    steps, _, cells = scores_ref.shape[1:]
    span = group * HEAD
    factor = 1.0 / jnp.sqrt(jnp.float32(HEAD))
    copies = [
        [
            pltpu.make_async_copy(laid_ref.at[k], held_ref.at[k], sems.at[k, i])
            for i, (laid_ref, held_ref) in enumerate(zip(laid_refs, held_refs))
        ]
        for k in range(KVH)
    ]
    for copy in copies:
        for one in copy:
            one.start()
    routed = jnp.concatenate([ref[...].astype(jnp.float32) for ref in routed_refs], axis=0)
    routed = jnp.transpose(routed).astype(jnp.bfloat16)
    for k in range(KVH):
        delta = jnp.dot(
            routed, stack(returned_refs, k * span, span), preferred_element_type=jnp.float32
        )
        for one in copies[k]:
            one.wait()
        for i in range(steps):
            lines = slice(i * step, (i + 1) * step)
            at = slice(i * cells, (i + 1) * cells)
            change = jnp.dot(
                tall(delta[lines], group).astype(jnp.bfloat16),
                keys_ref[k, :, at],
                preferred_element_type=jnp.float32,
            )
            scores = scores_ref[k, i] + change * factor
            expo = jnp.exp(scores - jnp.max(scores, axis=1, keepdims=True))
            probs = expo * (1.0 / jnp.sum(expo, axis=1, keepdims=True))
            out = jnp.dot(
                probs.astype(jnp.bfloat16), values_ref[k, at, :], preferred_element_type=jnp.float32
            )
            for g in range(group):
                out_ref[lines, (k * group + g) * HEAD : (k * group + g + 1) * HEAD] = out[
                    g * step : (g + 1) * step
                ].astype(out_ref.dtype)


def attend(routed, returned, laid, width):
    rows = routed[0].shape[1]
    return pl.pallas_call(
        functools.partial(attend_kernel, width // (KVH * HEAD), len(returned)),
        in_specs=[pl.BlockSpec(memory_space=pltpu.VMEM)] * (2 + len(returned))
        + [pl.BlockSpec(memory_space=pl.ANY)] * len(laid),
        out_specs=pl.BlockSpec(memory_space=pltpu.VMEM),
        out_shape=jax.ShapeDtypeStruct((rows, width), jnp.bfloat16),
        scratch_shapes=[pltpu.VMEM(part.shape, part.dtype) for part in laid]
        + [pltpu.SemaphoreType.DMA((KVH, len(laid)))],
        compiler_params=pltpu.CompilerParams(vmem_limit_bytes=24 * 2**20),
        name="attend",
    )(*routed, *returned, *laid)


def on_device(hidden, adapter_id, adapter_slot, cache_len, base_q, kv_cache, a_maps, b_maps):
    owners = lax.axis_size("owner")
    quarter = owners // 4
    rows = hidden.shape[0]
    held = a_maps.shape[1] // RANK
    slot_count = max(2, 2 * ((rows + 2 * owners - 1) // (2 * owners)))
    halves = [[i for i in range(owners) if i // quarter % 2 == bit] for bit in range(2)]

    def swap(lines):
        blocks = lines.reshape(owners // 2, slot_count, lines.shape[1])
        blocks = lax.all_to_all(
            blocks, "owner", split_axis=0, concat_axis=0, tiled=True, axis_index_groups=halves
        )
        return blocks.reshape(lines.shape)

    def trade(messages):
        return [
            lax.ppermute(message, "owner", [(i, i ^ apart) for i in range(owners)])
            for message, apart in zip(messages, halves[1])
        ]

    whole = functools.partial(pack, hidden, adapter_id, adapter_slot)
    routed, lines = whole(adapter_id, False, owners, slot_count, held)
    routed_pairs, *messages = whole(routed, True, owners, slot_count, held)
    arrived = swap(lines)
    arrived_pairs = trade(messages)
    laid = prep(base_q, kv_cache, cache_len)
    (change,) = adapt([arrived], a_maps, b_maps, laid[0])
    returned = swap(change)
    changes = adapt(arrived_pairs, a_maps, b_maps, change)
    returned_pairs = trade(changes)
    return attend([routed, routed_pairs], [returned, *returned_pairs], laid, base_q.shape[1])


def solution(mesh):
    return jax.shard_map(
        on_device,
        mesh=mesh,
        in_specs=(
            P(("groups", "owner"), None),
            P(("groups", "owner")),
            P("groups"),
            P(("groups", "owner")),
            P(("groups", "owner"), None),
            P(("groups", "owner"), None, None, None),
            P(None, "owner"),
            P("owner", None),
        ),
        out_specs=P(("groups", "owner"), None),
        check_vma=False,
    )
```

```python
import functools

import jax
import jax.numpy as jnp
from jax import lax
from jax.experimental import pallas as pl
from jax.experimental.pallas import tpu as pltpu
from jax.sharding import PartitionSpec as P

HEAD = 128
KVH = 4
RANK = 64
LANES = 128
SCALE = 2.0
ROWS_STEP = 8
COLUMNS_STEP = 2048


def place_of(index, quarter):
    return lax.div(index, 2 * quarter) * quarter + lax.rem(index, quarter)


def routing(pairs, owners, slot_count, held, slots_ref, ids_ref):
    ids = ids_ref[...]
    rows = ids.shape[1]
    quarter = owners // 4

    def look(s, slot):
        return jnp.where(ids == s, slots_ref[s], slot)

    slot = lax.fori_loop(0, slots_ref.shape[0], look, jnp.zeros_like(ids), unroll=8)
    owner = lax.div(slot, held)
    local = slot - owner * held
    hits = owner == lax.broadcasted_iota(jnp.int32, (owners, rows), 0)
    earlier = lax.broadcasted_iota(jnp.int32, (rows, rows), 0) < lax.broadcasted_iota(
        jnp.int32, (rows, rows), 1
    )
    before = jnp.dot(
        hits.astype(jnp.bfloat16), earlier.astype(jnp.bfloat16), preferred_element_type=jnp.float32
    )
    place = jnp.sum(jnp.where(hits, before, 0.0), axis=0, keepdims=True).astype(jnp.int32)
    apart = owner ^ lax.axis_index("owner")
    message = place_of(apart if pairs else owner, quarter)
    meant = lax.rem(lax.div(apart, quarter), 2) == (1 if pairs else 0)
    line = lax.broadcasted_iota(jnp.int32, (owners // 2 * slot_count, rows), 0)
    routed = line == jnp.where(meant, message * slot_count + place, -1)
    label = jnp.sum(jnp.where(routed, local.astype(jnp.float32), 0.0), axis=1, keepdims=True)
    return routed.astype(jnp.bfloat16), label


def pack_kernel(
    pairs, owners, slot_count, held, slots_ref, ids_ref, hidden_ref, after_ref, routed_ref, *refs
):
    *packed_refs, rows_ref, sems = refs
    width = hidden_ref.shape[1]
    spans = [(at, min(COLUMNS_STEP, width - at)) for at in range(0, width, COLUMNS_STEP)]
    loads = [
        pltpu.make_async_copy(
            hidden_ref.at[:, pl.ds(at, size)], rows_ref.at[:, pl.ds(at, size)], sems.at[i]
        )
        for i, (at, size) in enumerate(spans)
    ]
    for load in loads:
        load.start()
    routed, label = routing(pairs, owners, slot_count, held, slots_ref, ids_ref)
    routed_ref[...] = routed
    label = jnp.broadcast_to(label, (label.shape[0], LANES))
    count = packed_refs[0].shape[0]

    def put(at, lines):
        for i, packed_ref in enumerate(packed_refs):
            packed_ref[:, at : at + lines.shape[1]] = lines[i * count : (i + 1) * count].astype(
                packed_ref.dtype
            )

    put(width, label)
    for load, (at, size) in zip(loads, spans):
        load.wait()
        put(at, jnp.dot(routed, rows_ref[:, at : at + size], preferred_element_type=jnp.float32))


def pack(hidden, adapter_id, adapter_slot, after, pairs, owners, slot_count, held):
    rows, width = hidden.shape
    lines = owners // 2 * slot_count
    messages = owners // 2 if pairs else 1
    steps = pl.cdiv(width, COLUMNS_STEP)
    return pl.pallas_call(
        functools.partial(pack_kernel, pairs, owners, slot_count, held),
        in_specs=[
            pl.BlockSpec(memory_space=pltpu.SMEM),
            pl.BlockSpec(memory_space=pltpu.VMEM),
            pl.BlockSpec(memory_space=pl.ANY),
            pl.BlockSpec(memory_space=pl.ANY),
        ],
        out_specs=[pl.BlockSpec(memory_space=pltpu.VMEM)] * (1 + messages),
        out_shape=[jax.ShapeDtypeStruct((lines, rows), jnp.bfloat16)]
        + [jax.ShapeDtypeStruct((lines // messages, width + LANES), hidden.dtype)] * messages,
        scratch_shapes=[
            pltpu.VMEM((rows, width), hidden.dtype),
            pltpu.SemaphoreType.DMA((steps,)),
        ],
        compiler_params=pltpu.CompilerParams(vmem_limit_bytes=56 * 2**20),
        name="pack_pairs" if pairs else "pack",
    )(adapter_slot, adapter_id.reshape(1, rows), hidden, after)


def stack(refs, at, size):
    if len(refs) == 1:
        return refs[0][:, at : at + size]
    return jnp.concatenate(
        [ref[:, at : at + size].astype(jnp.float32) for ref in refs], axis=0
    ).astype(jnp.bfloat16)


def adapt_kernel(count, *refs):
    arrived_refs, (a_ref, b_ref, _), change_refs = refs[:count], refs[count : count + 3], refs[count + 3 :]
    width = a_ref.shape[0]
    lines = arrived_refs[0].shape[0]
    low = jnp.zeros((count * lines, a_ref.shape[1]), jnp.float32)
    for at in range(0, width, COLUMNS_STEP):
        low += jnp.dot(
            stack(arrived_refs, at, COLUMNS_STEP),
            a_ref[at : at + COLUMNS_STEP, :],
            preferred_element_type=jnp.float32,
        )
    label = stack(arrived_refs, width, LANES).astype(jnp.float32)[:, :1].astype(jnp.int32)
    column = lax.broadcasted_iota(jnp.int32, low.shape, 1) // RANK
    low = jnp.where(column == label, low, 0.0).astype(jnp.bfloat16)
    out_width = b_ref.shape[1]
    piece = min(1024, out_width)
    for at in range(0, out_width, piece):
        change = SCALE * jnp.dot(low, b_ref[:, at : at + piece], preferred_element_type=jnp.float32)
        for i, change_ref in enumerate(change_refs):
            change_ref[:, at : at + piece] = change[i * lines : (i + 1) * lines].astype(
                change_ref.dtype
            )


def adapt(arrived, a_maps, b_maps, after):
    count = len(arrived)
    lines = arrived[0].shape[0]
    return pl.pallas_call(
        functools.partial(adapt_kernel, count),
        in_specs=[pl.BlockSpec(memory_space=pltpu.VMEM)] * (count + 2)
        + [pl.BlockSpec(memory_space=pl.ANY)],
        out_specs=[pl.BlockSpec(memory_space=pltpu.VMEM)] * count,
        out_shape=[jax.ShapeDtypeStruct((lines, b_maps.shape[1]), jnp.bfloat16)] * count,
        compiler_params=pltpu.CompilerParams(vmem_limit_bytes=16 * 2**20),
        cost_estimate=pl.CostEstimate(
            flops=2 * count * lines * (a_maps.size + b_maps.size),
            bytes_accessed=2 * (a_maps.size + b_maps.size),
            transcendentals=0,
        ),
        name="adapt",
    )(*arrived, a_maps, b_maps, after)


def tall(rows, group):
    return jnp.concatenate([rows[:, g * HEAD : (g + 1) * HEAD] for g in range(group)], axis=0)


def prep_kernel(group, context, base_ref, kv_ref, len_ref, _, keys_ref, values_ref, scores_ref):
    step = ROWS_STEP
    cells = step * context
    lane = lax.broadcasted_iota(jnp.int32, (group * step, cells), 1)
    line = lax.broadcasted_iota(jnp.int32, (group * step, cells), 0)
    live = (lane // context == lax.rem(line, step)) & (lax.rem(lane, context) < len_ref[...][0])
    factor = 1.0 / jnp.sqrt(jnp.float32(HEAD))
    for k in range(KVH):
        head = slice(k * HEAD, (k + 1) * HEAD)
        keys = kv_ref[:, 0, :, head].astype(jnp.float32).reshape(cells, HEAD)
        keys = jnp.transpose(keys).astype(keys_ref.dtype)
        keys_ref[k] = keys
        values_ref[k] = kv_ref[:, 1, :, head].reshape(cells, HEAD)
        base = base_ref[:, k * group * HEAD : (k + 1) * group * HEAD].astype(jnp.float32)
        scores = jnp.dot(
            tall(base, group).astype(jnp.bfloat16), keys, preferred_element_type=jnp.float32
        )
        scores_ref[k, 0] = jnp.where(live, scores * factor, -jnp.inf)


def prep(base_q, kv_cache, cache_len, after):
    rows, width = base_q.shape
    context = kv_cache.shape[2]
    group = width // (KVH * HEAD)
    step = ROWS_STEP
    steps = rows // step
    cells = step * context
    lens = jnp.repeat(cache_len, context).reshape(steps, 1, cells)
    return pl.pallas_call(
        functools.partial(prep_kernel, group, context),
        grid=(steps,),
        in_specs=[
            pl.BlockSpec((step, width), lambda i: (i, 0)),
            pl.BlockSpec((step, *kv_cache.shape[1:]), lambda i: (i, 0, 0, 0)),
            pl.BlockSpec((1, 1, cells), lambda i: (i, 0, 0)),
            pl.BlockSpec(memory_space=pl.ANY),
        ],
        out_specs=[
            pl.BlockSpec((KVH, HEAD, cells), lambda i: (0, 0, i)),
            pl.BlockSpec((KVH, cells, HEAD), lambda i: (0, i, 0)),
            pl.BlockSpec((KVH, 1, group * step, cells), lambda i: (0, i, 0, 0)),
        ],
        out_shape=[
            jax.ShapeDtypeStruct((KVH, HEAD, rows * context), jnp.bfloat16),
            jax.ShapeDtypeStruct((KVH, rows * context, HEAD), jnp.bfloat16),
            jax.ShapeDtypeStruct((KVH, steps, group * step, cells), jnp.float32),
        ],
        compiler_params=pltpu.CompilerParams(vmem_limit_bytes=16 * 2**20),
        cost_estimate=pl.CostEstimate(
            flops=2 * rows * width * cells, bytes_accessed=16 * 2**20, transcendentals=0
        ),
        name="prep",
    )(base_q, kv_cache, lens, after)


def attend_kernel(group, count, *refs):
    routed_refs, returned_refs, refs = refs[:2], refs[2 : 2 + count], refs[2 + count :]
    laid_refs, (out_ref, *held_refs, sems) = refs[:3], refs[3:]
    keys_ref, values_ref, scores_ref = held_refs
    step = ROWS_STEP
    steps, _, cells = scores_ref.shape[1:]
    span = group * HEAD
    factor = 1.0 / jnp.sqrt(jnp.float32(HEAD))
    copies = [
        [
            pltpu.make_async_copy(laid_ref.at[k], held_ref.at[k], sems.at[k, i])
            for i, (laid_ref, held_ref) in enumerate(zip(laid_refs, held_refs))
        ]
        for k in range(KVH)
    ]
    for copy in copies:
        for one in copy:
            one.start()
    routed = jnp.concatenate([ref[...].astype(jnp.float32) for ref in routed_refs], axis=0)
    routed = jnp.transpose(routed).astype(jnp.bfloat16)
    for k in range(KVH):
        delta = jnp.dot(
            routed, stack(returned_refs, k * span, span), preferred_element_type=jnp.float32
        )
        for one in copies[k]:
            one.wait()
        for i in range(steps):
            lines = slice(i * step, (i + 1) * step)
            at = slice(i * cells, (i + 1) * cells)
            change = jnp.dot(
                tall(delta[lines], group).astype(jnp.bfloat16),
                keys_ref[k, :, at],
                preferred_element_type=jnp.float32,
            )
            scores = scores_ref[k, i] + change * factor
            expo = jnp.exp(scores - jnp.max(scores, axis=1, keepdims=True))
            probs = expo * (1.0 / jnp.sum(expo, axis=1, keepdims=True))
            out = jnp.dot(
                probs.astype(jnp.bfloat16), values_ref[k, at, :], preferred_element_type=jnp.float32
            )
            for g in range(group):
                out_ref[lines, (k * group + g) * HEAD : (k * group + g + 1) * HEAD] = out[
                    g * step : (g + 1) * step
                ].astype(out_ref.dtype)


def attend(routed, returned, laid, width):
    rows = routed[0].shape[1]
    return pl.pallas_call(
        functools.partial(attend_kernel, width // (KVH * HEAD), len(returned)),
        in_specs=[pl.BlockSpec(memory_space=pltpu.VMEM)] * (2 + len(returned))
        + [pl.BlockSpec(memory_space=pltpu.HBM)] * len(laid),
        out_specs=pl.BlockSpec(memory_space=pltpu.VMEM),
        out_shape=jax.ShapeDtypeStruct((rows, width), jnp.bfloat16),
        scratch_shapes=[pltpu.VMEM(part.shape, part.dtype) for part in laid]
        + [pltpu.SemaphoreType.DMA((KVH, len(laid)))],
        compiler_params=pltpu.CompilerParams(vmem_limit_bytes=24 * 2**20),
        name="attend",
    )(*routed, *returned, *laid)


def on_device(hidden, adapter_id, adapter_slot, cache_len, base_q, kv_cache, a_maps, b_maps):
    owners = lax.axis_size("owner")
    quarter = owners // 4
    rows = hidden.shape[0]
    held = a_maps.shape[1] // RANK
    slot_count = max(2, 2 * ((rows + 2 * owners - 1) // (2 * owners)))
    halves = [[i for i in range(owners) if i // quarter % 2 == bit] for bit in range(2)]

    def swap(lines):
        blocks = lines.reshape(owners // 2, slot_count, lines.shape[1])
        blocks = lax.all_to_all(
            blocks, "owner", split_axis=0, concat_axis=0, tiled=True, axis_index_groups=halves
        )
        return blocks.reshape(lines.shape)

    def trade(messages, offsets):
        return [
            lax.ppermute(message, "owner", [(i, i ^ apart) for i in range(owners)])
            for message, apart in zip(messages, offsets)
        ]

    near, far = halves[1][:quarter], halves[1][quarter:]
    whole = functools.partial(pack, hidden, adapter_id, adapter_slot)
    routed, lines = whole(adapter_id, False, owners, slot_count, held)
    arrived = swap(lines)
    routed_pairs, *messages = whole(routed, True, owners, slot_count, held)
    arrived_near = trade(messages[:quarter], near)
    arrived_far = trade(messages[quarter:], far)
    laid = prep(base_q, kv_cache, cache_len, routed_pairs)
    change_near = adapt(arrived_near, a_maps, b_maps, laid[0])
    (change,) = adapt([arrived], a_maps, b_maps, change_near[0])
    returned = swap(change)
    change_far = adapt(arrived_far, a_maps, b_maps, change)
    returned_far = trade(change_far, far)
    returned_near = trade(change_near, near)
    returned = [returned, *returned_near, *returned_far]
    return attend([routed, routed_pairs], returned, laid, base_q.shape[1])


def solution(mesh):
    return jax.shard_map(
        on_device,
        mesh=mesh,
        in_specs=(
            P(("groups", "owner"), None),
            P(("groups", "owner")),
            P("groups"),
            P(("groups", "owner")),
            P(("groups", "owner"), None),
            P(("groups", "owner"), None, None, None),
            P(None, "owner"),
            P("owner", None),
        ),
        out_specs=P(("groups", "owner"), None),
        check_vma=False,
    )
```

```python
import functools

import jax
import jax.numpy as jnp
from jax import lax
from jax.experimental import pallas as pl
from jax.experimental.pallas import tpu as pltpu
from jax.sharding import PartitionSpec as P

HEAD = 128
KVH = 4
RANK = 64
LANES = 128
SCALE = 2.0
ROWS_STEP = 8
COLUMNS_STEP = 2048
FAR_GROUPS = 4


def routing(pairs, owners, slot_count, held, slots_ref, ids_ref):
    ids = ids_ref[...]
    rows = ids.shape[1]
    half = owners // 2

    def look(s, slot):
        return jnp.where(ids == s, slots_ref[s], slot)

    slot = lax.fori_loop(0, slots_ref.shape[0], look, jnp.zeros_like(ids), unroll=8)
    owner = lax.div(slot, held)
    local = slot - owner * held
    hits = owner == lax.broadcasted_iota(jnp.int32, (owners, rows), 0)
    earlier = lax.broadcasted_iota(jnp.int32, (rows, rows), 0) < lax.broadcasted_iota(
        jnp.int32, (rows, rows), 1
    )
    before = jnp.dot(
        hits.astype(jnp.bfloat16), earlier.astype(jnp.bfloat16), preferred_element_type=jnp.float32
    )
    place = jnp.sum(jnp.where(hits, before, 0.0), axis=0, keepdims=True).astype(jnp.int32)
    apart = owner ^ lax.axis_index("owner")
    message = lax.rem(apart if pairs else owner, half)
    meant = (apart >= half) == pairs
    line = lax.broadcasted_iota(jnp.int32, (half * slot_count, rows), 0)
    routed = line == jnp.where(meant, message * slot_count + place, -1)
    label = jnp.sum(jnp.where(routed, local.astype(jnp.float32), 0.0), axis=1, keepdims=True)
    return routed.astype(jnp.bfloat16), label


def pack_kernel(
    pairs, owners, slot_count, held, slots_ref, ids_ref, hidden_ref, after_ref, routed_ref, *refs
):
    *packed_refs, rows_ref, sems = refs
    width = hidden_ref.shape[1]
    spans = [(at, min(COLUMNS_STEP, width - at)) for at in range(0, width, COLUMNS_STEP)]
    loads = [
        pltpu.make_async_copy(
            hidden_ref.at[:, pl.ds(at, size)], rows_ref.at[:, pl.ds(at, size)], sems.at[i]
        )
        for i, (at, size) in enumerate(spans)
    ]
    for load in loads:
        load.start()
    routed, label = routing(pairs, owners, slot_count, held, slots_ref, ids_ref)
    routed_ref[...] = routed
    label = jnp.broadcast_to(label, (label.shape[0], LANES))
    count = packed_refs[0].shape[0]

    def put(at, lines):
        for i, packed_ref in enumerate(packed_refs):
            packed_ref[:, at : at + lines.shape[1]] = lines[i * count : (i + 1) * count].astype(
                packed_ref.dtype
            )

    put(width, label)
    for load, (at, size) in zip(loads, spans):
        load.wait()
        put(at, jnp.dot(routed, rows_ref[:, at : at + size], preferred_element_type=jnp.float32))


def pack(hidden, adapter_id, adapter_slot, after, pairs, owners, slot_count, held):
    rows, width = hidden.shape
    lines = owners // 2 * slot_count
    messages = owners // 2 if pairs else 1
    steps = pl.cdiv(width, COLUMNS_STEP)
    return pl.pallas_call(
        functools.partial(pack_kernel, pairs, owners, slot_count, held),
        in_specs=[
            pl.BlockSpec(memory_space=pltpu.SMEM),
            pl.BlockSpec(memory_space=pltpu.VMEM),
            pl.BlockSpec(memory_space=pl.ANY),
            pl.BlockSpec(memory_space=pl.ANY),
        ],
        out_specs=[pl.BlockSpec(memory_space=pltpu.VMEM)] * (1 + messages),
        out_shape=[jax.ShapeDtypeStruct((lines, rows), jnp.bfloat16)]
        + [jax.ShapeDtypeStruct((lines // messages, width + LANES), hidden.dtype)] * messages,
        scratch_shapes=[
            pltpu.VMEM((rows, width), hidden.dtype),
            pltpu.SemaphoreType.DMA((steps,)),
        ],
        compiler_params=pltpu.CompilerParams(vmem_limit_bytes=56 * 2**20),
        name="pack_pairs" if pairs else "pack",
    )(adapter_slot, adapter_id.reshape(1, rows), hidden, after)


def stack(refs, at, size):
    if len(refs) == 1:
        return refs[0][:, at : at + size]
    return jnp.concatenate(
        [ref[:, at : at + size].astype(jnp.float32) for ref in refs], axis=0
    ).astype(jnp.bfloat16)


def adapt_kernel(count, *refs):
    arrived_refs, (a_ref, b_ref, _), change_refs = refs[:count], refs[count : count + 3], refs[count + 3 :]
    width = a_ref.shape[0]
    lines = arrived_refs[0].shape[0]
    low = jnp.zeros((count * lines, a_ref.shape[1]), jnp.float32)
    for at in range(0, width, COLUMNS_STEP):
        low += jnp.dot(
            stack(arrived_refs, at, COLUMNS_STEP),
            a_ref[at : at + COLUMNS_STEP, :],
            preferred_element_type=jnp.float32,
        )
    label = stack(arrived_refs, width, LANES).astype(jnp.float32)[:, :1].astype(jnp.int32)
    column = lax.broadcasted_iota(jnp.int32, low.shape, 1) // RANK
    low = jnp.where(column == label, low, 0.0).astype(jnp.bfloat16)
    out_width = b_ref.shape[1]
    piece = min(1024, out_width)
    for at in range(0, out_width, piece):
        change = SCALE * jnp.dot(low, b_ref[:, at : at + piece], preferred_element_type=jnp.float32)
        for i, change_ref in enumerate(change_refs):
            change_ref[:, at : at + piece] = change[i * lines : (i + 1) * lines].astype(
                change_ref.dtype
            )


def adapt(arrived, a_maps, b_maps, after):
    count = len(arrived)
    lines = arrived[0].shape[0]
    return pl.pallas_call(
        functools.partial(adapt_kernel, count),
        in_specs=[pl.BlockSpec(memory_space=pltpu.VMEM)] * (count + 2)
        + [pl.BlockSpec(memory_space=pl.ANY)],
        out_specs=[pl.BlockSpec(memory_space=pltpu.VMEM)] * count,
        out_shape=[jax.ShapeDtypeStruct((lines, b_maps.shape[1]), jnp.bfloat16)] * count,
        compiler_params=pltpu.CompilerParams(vmem_limit_bytes=16 * 2**20),
        cost_estimate=pl.CostEstimate(
            flops=2 * count * lines * (a_maps.size + b_maps.size),
            bytes_accessed=2 * (a_maps.size + b_maps.size),
            transcendentals=0,
        ),
        name="adapt",
    )(*arrived, a_maps, b_maps, after)


def tall(rows, group):
    return jnp.concatenate([rows[:, g * HEAD : (g + 1) * HEAD] for g in range(group)], axis=0)


def prep_kernel(group, context, base_ref, kv_ref, len_ref, _, keys_ref, values_ref, scores_ref):
    step = ROWS_STEP
    cells = step * context
    lane = lax.broadcasted_iota(jnp.int32, (group * step, cells), 1)
    line = lax.broadcasted_iota(jnp.int32, (group * step, cells), 0)
    live = (lane // context == lax.rem(line, step)) & (lax.rem(lane, context) < len_ref[...][0])
    factor = 1.0 / jnp.sqrt(jnp.float32(HEAD))
    for k in range(KVH):
        head = slice(k * HEAD, (k + 1) * HEAD)
        keys = kv_ref[:, 0, :, head].astype(jnp.float32).reshape(cells, HEAD)
        keys = jnp.transpose(keys).astype(keys_ref.dtype)
        keys_ref[k] = keys
        values_ref[k] = kv_ref[:, 1, :, head].reshape(cells, HEAD)
        base = base_ref[:, k * group * HEAD : (k + 1) * group * HEAD].astype(jnp.float32)
        scores = jnp.dot(
            tall(base, group).astype(jnp.bfloat16), keys, preferred_element_type=jnp.float32
        )
        scores_ref[k, 0] = jnp.where(live, scores * factor, -jnp.inf)


def prep(base_q, kv_cache, cache_len, after):
    rows, width = base_q.shape
    context = kv_cache.shape[2]
    group = width // (KVH * HEAD)
    step = ROWS_STEP
    steps = rows // step
    cells = step * context
    lens = jnp.repeat(cache_len, context).reshape(steps, 1, cells)
    return pl.pallas_call(
        functools.partial(prep_kernel, group, context),
        grid=(steps,),
        in_specs=[
            pl.BlockSpec((step, width), lambda i: (i, 0)),
            pl.BlockSpec((step, *kv_cache.shape[1:]), lambda i: (i, 0, 0, 0)),
            pl.BlockSpec((1, 1, cells), lambda i: (i, 0, 0)),
            pl.BlockSpec(memory_space=pl.ANY),
        ],
        out_specs=[
            pl.BlockSpec((KVH, HEAD, cells), lambda i: (0, 0, i)),
            pl.BlockSpec((KVH, cells, HEAD), lambda i: (0, i, 0)),
            pl.BlockSpec((KVH, 1, group * step, cells), lambda i: (0, i, 0, 0)),
        ],
        out_shape=[
            jax.ShapeDtypeStruct((KVH, HEAD, rows * context), jnp.bfloat16),
            jax.ShapeDtypeStruct((KVH, rows * context, HEAD), jnp.bfloat16),
            jax.ShapeDtypeStruct((KVH, steps, group * step, cells), jnp.float32),
        ],
        compiler_params=pltpu.CompilerParams(vmem_limit_bytes=16 * 2**20),
        cost_estimate=pl.CostEstimate(
            flops=2 * rows * width * cells, bytes_accessed=16 * 2**20, transcendentals=0
        ),
        name="prep",
    )(base_q, kv_cache, lens, after)


def attend_kernel(group, count, *refs):
    routed_refs, given_refs, out_ref = refs[:2], refs[2 : 5 + count], refs[5 + count]
    *held_refs, sems, laid_sems = refs[6 + count :]
    returned_refs, (keys_ref, values_ref, scores_ref) = held_refs[:count], held_refs[count:]
    step = ROWS_STEP
    steps, _, cells = scores_ref.shape[1:]
    span = group * HEAD
    factor = 1.0 / jnp.sqrt(jnp.float32(HEAD))
    copies = [
        pltpu.make_async_copy(given_ref, held_ref, sems.at[i])
        for i, (given_ref, held_ref) in enumerate(zip(given_refs[:count], returned_refs))
    ]
    laid_copies = [
        [
            pltpu.make_async_copy(given_ref.at[k], held_ref.at[k], laid_sems.at[k, i])
            for i, (given_ref, held_ref) in enumerate(zip(given_refs[count:], held_refs[count:]))
        ]
        for k in range(KVH)
    ]
    for copy in sum(laid_copies, copies):
        copy.start()
    routed = jnp.concatenate([ref[...].astype(jnp.float32) for ref in routed_refs], axis=0)
    routed = jnp.transpose(routed).astype(jnp.bfloat16)
    for copy in copies:
        copy.wait()
    for k in range(KVH):
        delta = jnp.dot(
            routed, stack(returned_refs, k * span, span), preferred_element_type=jnp.float32
        )
        for copy in laid_copies[k]:
            copy.wait()
        for i in range(steps):
            lines = slice(i * step, (i + 1) * step)
            at = slice(i * cells, (i + 1) * cells)
            change = jnp.dot(
                tall(delta[lines], group).astype(jnp.bfloat16),
                keys_ref[k, :, at],
                preferred_element_type=jnp.float32,
            )
            scores = scores_ref[k, i] + change * factor
            expo = jnp.exp(scores - jnp.max(scores, axis=1, keepdims=True))
            probs = expo * (1.0 / jnp.sum(expo, axis=1, keepdims=True))
            out = jnp.dot(
                probs.astype(jnp.bfloat16), values_ref[k, at, :], preferred_element_type=jnp.float32
            )
            for g in range(group):
                out_ref[lines, (k * group + g) * HEAD : (k * group + g + 1) * HEAD] = out[
                    g * step : (g + 1) * step
                ].astype(out_ref.dtype)


def attend(routed, returned, laid, width):
    rows = routed[0].shape[1]
    given = [*returned, *laid]
    return pl.pallas_call(
        functools.partial(attend_kernel, width // (KVH * HEAD), len(returned)),
        in_specs=[pl.BlockSpec(memory_space=pltpu.VMEM)] * 2
        + [pl.BlockSpec(memory_space=pl.ANY)] * len(given),
        out_specs=pl.BlockSpec(memory_space=pltpu.VMEM),
        out_shape=jax.ShapeDtypeStruct((rows, width), jnp.bfloat16),
        scratch_shapes=[pltpu.VMEM(part.shape, part.dtype) for part in given]
        + [pltpu.SemaphoreType.DMA((len(returned),)), pltpu.SemaphoreType.DMA((KVH, len(laid)))],
        compiler_params=pltpu.CompilerParams(vmem_limit_bytes=56 * 2**20),
        name="attend",
    )(*routed, *given)


def on_device(hidden, adapter_id, adapter_slot, cache_len, base_q, kv_cache, a_maps, b_maps):
    owners = lax.axis_size("owner")
    half = owners // 2
    rows = hidden.shape[0]
    held = a_maps.shape[1] // RANK
    slot_count = max(2, 2 * ((rows + 2 * owners - 1) // (2 * owners)))
    halves = [list(range(half)), list(range(half, owners))]

    def swap(lines):
        blocks = lines.reshape(half, slot_count, lines.shape[1])
        blocks = lax.all_to_all(
            blocks, "owner", split_axis=0, concat_axis=0, tiled=True, axis_index_groups=halves
        )
        return blocks.reshape(lines.shape)

    def trade(messages, first):
        return [
            lax.ppermute(message, "owner", [(i, i ^ (first + j)) for i in range(owners)])
            for j, message in enumerate(messages)
        ]

    whole = functools.partial(pack, hidden, adapter_id, adapter_slot)
    routed_far, *messages = whole(adapter_id, True, owners, slot_count, held)
    size = max(1, half // FAR_GROUPS)
    starts = range(0, half, size)
    arrived_far = [trade(messages[at : at + size], half + at) for at in starts]
    routed, lines = whole(routed_far, False, owners, slot_count, held)
    arrived = swap(lines)
    laid = prep(base_q, kv_cache, cache_len, routed)
    returned, after = [], laid[0]
    for i, at in enumerate(starts):
        change_far = adapt(arrived_far[i], a_maps, b_maps, after)
        after = change_far[0]
        returned += trade(change_far, half + at)
        if i == 0:
            (after,) = adapt([arrived], a_maps, b_maps, after)
            returned.append(swap(after))
    returned = returned[:size] + returned[size + 1 :] + returned[size : size + 1]
    return attend([routed_far, routed], returned, laid, base_q.shape[1])


def solution(mesh):
    return jax.shard_map(
        on_device,
        mesh=mesh,
        in_specs=(
            P(("groups", "owner"), None),
            P(("groups", "owner")),
            P("groups"),
            P(("groups", "owner")),
            P(("groups", "owner"), None),
            P(("groups", "owner"), None, None, None),
            P(None, "owner"),
            P("owner", None),
        ),
        out_specs=P(("groups", "owner"), None),
        check_vma=False,
    )
```

```python
import functools

import jax
import jax.numpy as jnp
from jax import lax
from jax.experimental import pallas as pl
from jax.experimental.pallas import tpu as pltpu
from jax.sharding import PartitionSpec as P

HEAD = 128
KVH = 4
RANK = 64
LANES = 128
SCALE = 2.0
ROWS_STEP = 8
COLUMNS_STEP = 2048
LIGHT = pl.CostEstimate(flops=1, bytes_accessed=1, transcendentals=0)
HEAVY = pl.CostEstimate(flops=1, bytes_accessed=100_000_000, transcendentals=0)


def place_of(index, quarter):
    return lax.div(index, 2 * quarter) * quarter + lax.rem(index, quarter)


def routing(pairs, owners, slot_count, held, slots_ref, ids_ref):
    ids = ids_ref[...]
    rows = ids.shape[1]
    quarter = owners // 4

    def look(s, slot):
        return jnp.where(ids == s, slots_ref[s], slot)

    slot = lax.fori_loop(0, slots_ref.shape[0], look, jnp.zeros_like(ids), unroll=8)
    owner = lax.div(slot, held)
    local = slot - owner * held
    hits = owner == lax.broadcasted_iota(jnp.int32, (owners, rows), 0)
    earlier = lax.broadcasted_iota(jnp.int32, (rows, rows), 0) < lax.broadcasted_iota(
        jnp.int32, (rows, rows), 1
    )
    before = jnp.dot(
        hits.astype(jnp.bfloat16), earlier.astype(jnp.bfloat16), preferred_element_type=jnp.float32
    )
    place = jnp.sum(jnp.where(hits, before, 0.0), axis=0, keepdims=True).astype(jnp.int32)
    apart = owner ^ lax.axis_index("owner")
    message = place_of(apart if pairs else owner, quarter)
    meant = lax.rem(lax.div(apart, quarter), 2) == (1 if pairs else 0)
    line = lax.broadcasted_iota(jnp.int32, (owners // 2 * slot_count, rows), 0)
    routed = line == jnp.where(meant, message * slot_count + place, -1)
    label = jnp.sum(jnp.where(routed, local.astype(jnp.float32), 0.0), axis=1, keepdims=True)
    return routed.astype(jnp.bfloat16), label


def pack_kernel(
    pairs, owners, slot_count, held, slots_ref, ids_ref, hidden_ref, after_ref, routed_ref, *refs
):
    *packed_refs, rows_ref, sems = refs
    width = hidden_ref.shape[1]
    spans = [(at, min(COLUMNS_STEP, width - at)) for at in range(0, width, COLUMNS_STEP)]
    loads = [
        pltpu.make_async_copy(
            hidden_ref.at[:, pl.ds(at, size)], rows_ref.at[:, pl.ds(at, size)], sems.at[i]
        )
        for i, (at, size) in enumerate(spans)
    ]
    for load in loads:
        load.start()
    routed, label = routing(pairs, owners, slot_count, held, slots_ref, ids_ref)
    routed_ref[...] = routed
    label = jnp.broadcast_to(label, (label.shape[0], LANES))
    count = packed_refs[0].shape[0]

    def put(at, lines):
        for i, packed_ref in enumerate(packed_refs):
            packed_ref[:, at : at + lines.shape[1]] = lines[i * count : (i + 1) * count].astype(
                packed_ref.dtype
            )

    put(width, label)
    for load, (at, size) in zip(loads, spans):
        load.wait()
        put(at, jnp.dot(routed, rows_ref[:, at : at + size], preferred_element_type=jnp.float32))


def pack(hidden, adapter_id, adapter_slot, after, pairs, owners, slot_count, held):
    rows, width = hidden.shape
    lines = owners // 2 * slot_count
    messages = owners // 2 if pairs else 1
    steps = pl.cdiv(width, COLUMNS_STEP)
    return pl.pallas_call(
        functools.partial(pack_kernel, pairs, owners, slot_count, held),
        in_specs=[
            pl.BlockSpec(memory_space=pltpu.SMEM),
            pl.BlockSpec(memory_space=pltpu.VMEM),
            pl.BlockSpec(memory_space=pl.ANY),
            pl.BlockSpec(memory_space=pl.ANY),
        ],
        out_specs=[pl.BlockSpec(memory_space=pltpu.VMEM)] * (1 + messages),
        out_shape=[jax.ShapeDtypeStruct((lines, rows), jnp.bfloat16)]
        + [jax.ShapeDtypeStruct((lines // messages, width + LANES), hidden.dtype)] * messages,
        scratch_shapes=[
            pltpu.VMEM((rows, width), hidden.dtype),
            pltpu.SemaphoreType.DMA((steps,)),
        ],
        compiler_params=pltpu.CompilerParams(vmem_limit_bytes=56 * 2**20),
        cost_estimate=LIGHT,
        name="pack_pairs" if pairs else "pack",
    )(adapter_slot, adapter_id.reshape(1, rows), hidden, after)


def stack(refs, at, size):
    if len(refs) == 1:
        return refs[0][:, at : at + size]
    return jnp.concatenate(
        [ref[:, at : at + size].astype(jnp.float32) for ref in refs], axis=0
    ).astype(jnp.bfloat16)


def adapt_kernel(count, *refs):
    arrived_refs, (a_ref, b_ref, _), change_refs = refs[:count], refs[count : count + 3], refs[count + 3 :]
    width = a_ref.shape[0]
    lines = arrived_refs[0].shape[0]
    low = jnp.zeros((count * lines, a_ref.shape[1]), jnp.float32)
    for at in range(0, width, COLUMNS_STEP):
        low += jnp.dot(
            stack(arrived_refs, at, COLUMNS_STEP),
            a_ref[at : at + COLUMNS_STEP, :],
            preferred_element_type=jnp.float32,
        )
    label = stack(arrived_refs, width, LANES).astype(jnp.float32)[:, :1].astype(jnp.int32)
    column = lax.broadcasted_iota(jnp.int32, low.shape, 1) // RANK
    low = jnp.where(column == label, low, 0.0).astype(jnp.bfloat16)
    out_width = b_ref.shape[1]
    piece = min(1024, out_width)
    for at in range(0, out_width, piece):
        change = SCALE * jnp.dot(low, b_ref[:, at : at + piece], preferred_element_type=jnp.float32)
        for i, change_ref in enumerate(change_refs):
            change_ref[:, at : at + piece] = change[i * lines : (i + 1) * lines].astype(
                change_ref.dtype
            )


def adapt(arrived, a_maps, b_maps, after, weight=LIGHT):
    count = len(arrived)
    lines = arrived[0].shape[0]
    return pl.pallas_call(
        functools.partial(adapt_kernel, count),
        in_specs=[pl.BlockSpec(memory_space=pltpu.VMEM)] * (count + 2)
        + [pl.BlockSpec(memory_space=pl.ANY)],
        out_specs=[pl.BlockSpec(memory_space=pltpu.VMEM)] * count,
        out_shape=[jax.ShapeDtypeStruct((lines, b_maps.shape[1]), jnp.bfloat16)] * count,
        compiler_params=pltpu.CompilerParams(vmem_limit_bytes=16 * 2**20),
        cost_estimate=weight,
        name="adapt",
    )(*arrived, a_maps, b_maps, after)


def tall(rows, group):
    return jnp.concatenate([rows[:, g * HEAD : (g + 1) * HEAD] for g in range(group)], axis=0)


def prep_kernel(group, context, base_ref, kv_ref, len_ref, _, keys_ref, values_ref, scores_ref):
    step = ROWS_STEP
    cells = step * context
    lane = lax.broadcasted_iota(jnp.int32, (group * step, cells), 1)
    line = lax.broadcasted_iota(jnp.int32, (group * step, cells), 0)
    live = (lane // context == lax.rem(line, step)) & (lax.rem(lane, context) < len_ref[...][0])
    factor = 1.0 / jnp.sqrt(jnp.float32(HEAD))
    for k in range(KVH):
        head = slice(k * HEAD, (k + 1) * HEAD)
        keys = kv_ref[:, 0, :, head].astype(jnp.float32).reshape(cells, HEAD)
        keys = jnp.transpose(keys).astype(keys_ref.dtype)
        keys_ref[k] = keys
        values_ref[k] = kv_ref[:, 1, :, head].reshape(cells, HEAD)
        base = base_ref[:, k * group * HEAD : (k + 1) * group * HEAD].astype(jnp.float32)
        scores = jnp.dot(
            tall(base, group).astype(jnp.bfloat16), keys, preferred_element_type=jnp.float32
        )
        scores_ref[k, 0] = jnp.where(live, scores * factor, -jnp.inf)


def prep(base_q, kv_cache, cache_len, after):
    rows, width = base_q.shape
    context = kv_cache.shape[2]
    group = width // (KVH * HEAD)
    step = ROWS_STEP
    steps = rows // step
    cells = step * context
    lens = jnp.repeat(cache_len, context).reshape(steps, 1, cells)
    return pl.pallas_call(
        functools.partial(prep_kernel, group, context),
        grid=(steps,),
        in_specs=[
            pl.BlockSpec((step, width), lambda i: (i, 0)),
            pl.BlockSpec((step, *kv_cache.shape[1:]), lambda i: (i, 0, 0, 0)),
            pl.BlockSpec((1, 1, cells), lambda i: (i, 0, 0)),
            pl.BlockSpec(memory_space=pl.ANY),
        ],
        out_specs=[
            pl.BlockSpec((KVH, HEAD, cells), lambda i: (0, 0, i)),
            pl.BlockSpec((KVH, cells, HEAD), lambda i: (0, i, 0)),
            pl.BlockSpec((KVH, 1, group * step, cells), lambda i: (0, i, 0, 0)),
        ],
        out_shape=[
            jax.ShapeDtypeStruct((KVH, HEAD, rows * context), jnp.bfloat16),
            jax.ShapeDtypeStruct((KVH, rows * context, HEAD), jnp.bfloat16),
            jax.ShapeDtypeStruct((KVH, steps, group * step, cells), jnp.float32),
        ],
        compiler_params=pltpu.CompilerParams(vmem_limit_bytes=16 * 2**20),
        cost_estimate=LIGHT,
        name="prep",
    )(base_q, kv_cache, lens, after)


def attend_kernel(group, count, *refs):
    routed_refs, given_refs, out_ref = refs[:2], refs[2 : 5 + count], refs[5 + count]
    *held_refs, sems, laid_sems = refs[6 + count :]
    returned_refs, (keys_ref, values_ref, scores_ref) = held_refs[:count], held_refs[count:]
    step = ROWS_STEP
    steps, _, cells = scores_ref.shape[1:]
    span = group * HEAD
    factor = 1.0 / jnp.sqrt(jnp.float32(HEAD))
    copies = [
        pltpu.make_async_copy(given_ref, held_ref, sems.at[i])
        for i, (given_ref, held_ref) in enumerate(zip(given_refs[:count], returned_refs))
    ]
    laid_copies = [
        [
            pltpu.make_async_copy(given_ref.at[k], held_ref.at[k], laid_sems.at[k, i])
            for i, (given_ref, held_ref) in enumerate(zip(given_refs[count:], held_refs[count:]))
        ]
        for k in range(KVH)
    ]
    for copy in sum(laid_copies, copies):
        copy.start()
    routed = jnp.concatenate([ref[...].astype(jnp.float32) for ref in routed_refs], axis=0)
    routed = jnp.transpose(routed).astype(jnp.bfloat16)
    for copy in copies:
        copy.wait()
    for k in range(KVH):
        delta = jnp.dot(
            routed, stack(returned_refs, k * span, span), preferred_element_type=jnp.float32
        )
        for copy in laid_copies[k]:
            copy.wait()
        for i in range(steps):
            lines = slice(i * step, (i + 1) * step)
            at = slice(i * cells, (i + 1) * cells)
            change = jnp.dot(
                tall(delta[lines], group).astype(jnp.bfloat16),
                keys_ref[k, :, at],
                preferred_element_type=jnp.float32,
            )
            scores = scores_ref[k, i] + change * factor
            expo = jnp.exp(scores - jnp.max(scores, axis=1, keepdims=True))
            probs = expo * (1.0 / jnp.sum(expo, axis=1, keepdims=True))
            out = jnp.dot(
                probs.astype(jnp.bfloat16), values_ref[k, at, :], preferred_element_type=jnp.float32
            )
            for g in range(group):
                out_ref[lines, (k * group + g) * HEAD : (k * group + g + 1) * HEAD] = out[
                    g * step : (g + 1) * step
                ].astype(out_ref.dtype)


def attend(routed, returned, laid, width):
    rows = routed[0].shape[1]
    given = [*returned, *laid]
    return pl.pallas_call(
        functools.partial(attend_kernel, width // (KVH * HEAD), len(returned)),
        in_specs=[pl.BlockSpec(memory_space=pltpu.VMEM)] * 2
        + [pl.BlockSpec(memory_space=pl.ANY)] * len(given),
        out_specs=pl.BlockSpec(memory_space=pltpu.VMEM),
        out_shape=jax.ShapeDtypeStruct((rows, width), jnp.bfloat16),
        scratch_shapes=[pltpu.VMEM(part.shape, part.dtype) for part in given]
        + [pltpu.SemaphoreType.DMA((len(returned),)), pltpu.SemaphoreType.DMA((KVH, len(laid)))],
        compiler_params=pltpu.CompilerParams(vmem_limit_bytes=56 * 2**20),
        name="attend",
    )(*routed, *given)


def on_device(hidden, adapter_id, adapter_slot, cache_len, base_q, kv_cache, a_maps, b_maps):
    owners = lax.axis_size("owner")
    quarter = owners // 4
    rows = hidden.shape[0]
    held = a_maps.shape[1] // RANK
    slot_count = max(2, 2 * ((rows + 2 * owners - 1) // (2 * owners)))
    halves = [[i for i in range(owners) if i // quarter % 2 == bit] for bit in range(2)]

    def swap(lines):
        blocks = lines.reshape(owners // 2, slot_count, lines.shape[1])
        blocks = lax.all_to_all(
            blocks, "owner", split_axis=0, concat_axis=0, tiled=True, axis_index_groups=halves
        )
        return blocks.reshape(lines.shape)

    def trade(messages, offsets):
        return [
            lax.ppermute(message, "owner", [(i, i ^ apart) for i in range(owners)])
            for message, apart in zip(messages, offsets)
        ]

    near, far = halves[1][:quarter], halves[1][quarter:]
    whole = functools.partial(pack, hidden, adapter_id, adapter_slot)
    routed, lines = whole(adapter_id, False, owners, slot_count, held)
    arrived = swap(lines)
    routed_pairs, *messages = whole(routed, True, owners, slot_count, held)
    arrived_near = trade(messages[:quarter], near)
    arrived_far = trade(messages[quarter:], far)
    laid = prep(base_q, kv_cache, cache_len, routed_pairs)
    change_near = adapt(arrived_near, a_maps, b_maps, laid[0])
    (change,) = adapt([arrived], a_maps, b_maps, change_near[0])
    returned = swap(change)
    change_far = adapt(arrived_far, a_maps, b_maps, change, HEAVY)
    returned_far = trade(change_far, far)
    returned_near = trade(change_near, near)
    returned = [returned, *returned_near, *returned_far]
    return attend([routed, routed_pairs], returned, laid, base_q.shape[1])


def solution(mesh):
    return jax.shard_map(
        on_device,
        mesh=mesh,
        in_specs=(
            P(("groups", "owner"), None),
            P(("groups", "owner")),
            P("groups"),
            P(("groups", "owner")),
            P(("groups", "owner"), None),
            P(("groups", "owner"), None, None, None),
            P(None, "owner"),
            P("owner", None),
        ),
        out_specs=P(("groups", "owner"), None),
        check_vma=False,
    )
```

```python
import functools

import jax
import jax.numpy as jnp
from jax import lax
from jax.experimental import pallas as pl
from jax.experimental.pallas import tpu as pltpu
from jax.sharding import PartitionSpec as P

HEAD = 128
KVH = 4
RANK = 64
LANES = 128
SCALE = 2.0
ROWS_STEP = 8
COLUMNS_STEP = 2048


def routing(owners, slot_count, held, slots_ref, ids_ref):
    ids = ids_ref[...]
    rows = ids.shape[1]

    def look(s, slot):
        return jnp.where(ids == s, slots_ref[s], slot)

    slot = lax.fori_loop(0, slots_ref.shape[0], look, jnp.zeros_like(ids), unroll=8)
    owner = lax.div(slot, held)
    local = slot - owner * held
    hits = owner == lax.broadcasted_iota(jnp.int32, (owners, rows), 0)
    earlier = lax.broadcasted_iota(jnp.int32, (rows, rows), 0) < lax.broadcasted_iota(
        jnp.int32, (rows, rows), 1
    )
    before = jnp.dot(
        hits.astype(jnp.bfloat16), earlier.astype(jnp.bfloat16), preferred_element_type=jnp.float32
    )
    place = jnp.sum(jnp.where(hits, before, 0.0), axis=0, keepdims=True).astype(jnp.int32)
    bins = owner * slot_count + place
    routed = bins == lax.broadcasted_iota(jnp.int32, (owners * slot_count, rows), 0)
    label = jnp.sum(jnp.where(routed, local.astype(jnp.float32), 0.0), axis=1, keepdims=True)
    return routed.astype(jnp.bfloat16), label


def pack_kernel(
    owners, slot_count, held, slots_ref, ids_ref, hidden_ref, packed_ref, routed_ref, rows_ref, bins_ref, sems, out_sems
):
    width = hidden_ref.shape[1]
    spans = [pl.ds(at, min(COLUMNS_STEP, width - at)) for at in range(0, width, COLUMNS_STEP)]
    loads = [
        pltpu.make_async_copy(hidden_ref.at[:, span], rows_ref.at[:, span], sems.at[i])
        for i, span in enumerate(spans)
    ]
    spans[-1] = pl.ds(spans[-1].start, spans[-1].size + LANES)
    stores = [
        pltpu.make_async_copy(bins_ref.at[:, span], packed_ref.at[:, span], out_sems.at[i])
        for i, span in enumerate(spans)
    ]
    for load in loads:
        load.start()
    routed, label = routing(owners, slot_count, held, slots_ref, ids_ref)
    routed_ref[...] = jnp.transpose(routed.astype(jnp.float32)).astype(routed_ref.dtype)
    bins_ref[:, width:] = jnp.broadcast_to(label, (label.shape[0], LANES)).astype(bins_ref.dtype)
    for load, store, span in zip(loads, stores, spans):
        load.wait()
        at, end = span.start, min(span.start + span.size, width)
        bins_ref[:, at:end] = jnp.dot(
            routed, rows_ref[:, at:end], preferred_element_type=jnp.float32
        ).astype(bins_ref.dtype)
        store.start()
    for store in stores:
        store.wait()


def pack(hidden, adapter_id, adapter_slot, owners, slot_count, held):
    rows, width = hidden.shape
    bins = owners * slot_count
    steps = pl.cdiv(width, COLUMNS_STEP)
    return pl.pallas_call(
        functools.partial(pack_kernel, owners, slot_count, held),
        in_specs=[
            pl.BlockSpec(memory_space=pltpu.SMEM),
            pl.BlockSpec(memory_space=pltpu.VMEM),
            pl.BlockSpec(memory_space=pl.ANY),
        ],
        out_specs=[pl.BlockSpec(memory_space=pl.ANY), pl.BlockSpec(memory_space=pltpu.VMEM)],
        out_shape=[
            jax.ShapeDtypeStruct((bins, width + LANES), hidden.dtype),
            jax.ShapeDtypeStruct((rows, bins), jnp.bfloat16),
        ],
        scratch_shapes=[
            pltpu.VMEM((rows, width), hidden.dtype),
            pltpu.VMEM((bins, width + LANES), hidden.dtype),
            pltpu.SemaphoreType.DMA((steps,)),
            pltpu.SemaphoreType.DMA((steps,)),
        ],
        compiler_params=pltpu.CompilerParams(vmem_limit_bytes=56 * 2**20),
        name="pack",
    )(adapter_slot, adapter_id.reshape(1, rows), hidden)


def adapt_kernel(arrived_ref, a_ref, b_ref, _, change_ref):
    width = a_ref.shape[0]
    low = jnp.zeros((arrived_ref.shape[0], a_ref.shape[1]), jnp.float32)
    for at in range(0, width, COLUMNS_STEP):
        low += jnp.dot(
            arrived_ref[:, at : at + COLUMNS_STEP],
            a_ref[at : at + COLUMNS_STEP, :],
            preferred_element_type=jnp.float32,
        )
    label = arrived_ref[:, width:].astype(jnp.float32)[:, :1].astype(jnp.int32)
    column = lax.broadcasted_iota(jnp.int32, low.shape, 1) // RANK
    low = jnp.where(column == label, low, 0.0).astype(jnp.bfloat16)
    out_width = b_ref.shape[1]
    piece = min(1024, out_width)
    for at in range(0, out_width, piece):
        change_ref[:, at : at + piece] = (
            SCALE * jnp.dot(low, b_ref[:, at : at + piece], preferred_element_type=jnp.float32)
        ).astype(change_ref.dtype)


def adapt(arrived, a_maps, b_maps, after):
    return pl.pallas_call(
        adapt_kernel,
        in_specs=[pl.BlockSpec(memory_space=pltpu.VMEM)] * 3 + [pl.BlockSpec(memory_space=pl.ANY)],
        out_specs=pl.BlockSpec(memory_space=pltpu.VMEM),
        out_shape=jax.ShapeDtypeStruct((arrived.shape[0], b_maps.shape[1]), jnp.bfloat16),
        compiler_params=pltpu.CompilerParams(vmem_limit_bytes=16 * 2**20),
        name="adapt",
    )(arrived, a_maps, b_maps, after)


def tall(rows, group):
    return jnp.concatenate([rows[:, g * HEAD : (g + 1) * HEAD] for g in range(group)], axis=0)


def prep_kernel(group, base_ref, kv_ref, keys_ref, values_ref, query_ref):
    step, context = kv_ref.shape[0], kv_ref.shape[2]
    cells = step * context
    for k in range(KVH):
        head = slice(k * HEAD, (k + 1) * HEAD)
        keys = kv_ref[:, 0, :, head].astype(jnp.float32).reshape(cells, HEAD)
        keys_ref[k] = jnp.transpose(keys).astype(keys_ref.dtype)
        values_ref[k] = kv_ref[:, 1, :, head].reshape(cells, HEAD)
        base = base_ref[:, k * group * HEAD : (k + 1) * group * HEAD].astype(jnp.float32)
        query_ref[k, 0] = tall(base, group).astype(query_ref.dtype)


def prep(base_q, kv_cache):
    rows, width = base_q.shape
    context = kv_cache.shape[2]
    group = width // (KVH * HEAD)
    step = ROWS_STEP
    steps = rows // step
    cells = step * context
    return pl.pallas_call(
        functools.partial(prep_kernel, group),
        grid=(steps,),
        in_specs=[
            pl.BlockSpec((step, width), lambda i: (i, 0)),
            pl.BlockSpec((step, *kv_cache.shape[1:]), lambda i: (i, 0, 0, 0)),
        ],
        out_specs=[
            pl.BlockSpec((KVH, HEAD, cells), lambda i: (0, 0, i)),
            pl.BlockSpec((KVH, cells, HEAD), lambda i: (0, i, 0)),
            pl.BlockSpec((KVH, 1, group * step, HEAD), lambda i: (0, i, 0, 0)),
        ],
        out_shape=[
            jax.ShapeDtypeStruct((KVH, HEAD, rows * context), jnp.bfloat16),
            jax.ShapeDtypeStruct((KVH, rows * context, HEAD), jnp.bfloat16),
            jax.ShapeDtypeStruct((KVH, steps, group * step, HEAD), jnp.bfloat16),
        ],
        compiler_params=pltpu.CompilerParams(vmem_limit_bytes=16 * 2**20),
        name="prep",
    )(base_q, kv_cache)


def attend_kernel(
    group,
    context,
    routed_ref,
    returned_ref,
    keys_ref,
    lens_ref,
    values_hbm,
    query_hbm,
    out_hbm,
    values_ref,
    query_ref,
    bias_ref,
    out_ref,
    sems,
):
    step = ROWS_STEP
    steps, lines = query_ref.shape[1:3]
    cells = step * context
    span = group * HEAD
    factor = 1.0 / jnp.sqrt(jnp.float32(HEAD))
    loads = [
        [
            pltpu.make_async_copy(query_hbm.at[k], query_ref.at[k], sems.at[k, 0]),
            pltpu.make_async_copy(values_hbm.at[k], values_ref.at[k], sems.at[k, 1]),
        ]
        for k in range(KVH)
    ]
    stores = [
        pltpu.make_async_copy(
            out_ref.at[:, pl.ds(k * span, span)], out_hbm.at[:, pl.ds(k * span, span)], sems.at[k, 2]
        )
        for k in range(KVH)
    ]
    for load in loads:
        for copy in load:
            copy.start()
    lane = lax.broadcasted_iota(jnp.int32, (lines, cells), 1)
    line = lax.broadcasted_iota(jnp.int32, (lines, cells), 0)
    own = lax.div(lane, context) == lax.rem(line, step)
    position = lax.rem(lane, context)
    for i in range(steps):
        bias_ref[i] = jnp.where(own & (position < lens_ref[i]), 0.0, -jnp.inf)
    for k in range(KVH):
        delta = jnp.dot(
            routed_ref[...],
            returned_ref[:, k * span : (k + 1) * span],
            preferred_element_type=jnp.float32,
        )
        for copy in loads[k]:
            copy.wait()
        for i in range(steps):
            rows = slice(i * step, (i + 1) * step)
            at = slice(i * cells, (i + 1) * cells)
            keys = keys_ref[k, :, at]
            change = tall(delta[rows], group).astype(jnp.bfloat16)
            scores = jnp.dot(
                jnp.concatenate([query_ref[k, i], change], axis=1),
                jnp.concatenate([keys, keys], axis=0),
                preferred_element_type=jnp.float32,
            )
            scores = scores * factor + bias_ref[i]
            expo = jnp.exp(scores - jnp.max(scores, axis=1, keepdims=True))
            probs = expo * (1.0 / jnp.sum(expo, axis=1, keepdims=True))
            out = jnp.dot(
                probs.astype(jnp.bfloat16), values_ref[k, at, :], preferred_element_type=jnp.float32
            )
            for g in range(group):
                out_ref[rows, (k * group + g) * HEAD : (k * group + g + 1) * HEAD] = out[
                    g * step : (g + 1) * step
                ].astype(out_ref.dtype)
        stores[k].start()
    for store in stores:
        store.wait()


def attend(routed, returned, cache_len, laid, context):
    keys, values, query = laid
    rows, width = routed.shape[0], returned.shape[1]
    steps = query.shape[1]
    cells = ROWS_STEP * context
    lens = jnp.repeat(cache_len, context).reshape(steps, 1, cells)
    return pl.pallas_call(
        functools.partial(attend_kernel, width // (KVH * HEAD), context),
        in_specs=[pl.BlockSpec(memory_space=pltpu.VMEM)] * 4
        + [pl.BlockSpec(memory_space=pl.ANY)] * 2,
        out_specs=pl.BlockSpec(memory_space=pl.ANY),
        out_shape=jax.ShapeDtypeStruct((rows, width), jnp.bfloat16),
        scratch_shapes=[
            pltpu.VMEM(values.shape, values.dtype),
            pltpu.VMEM(query.shape, query.dtype),
            pltpu.VMEM((steps, query.shape[2], cells), jnp.float32),
            pltpu.VMEM((rows, width), jnp.bfloat16),
            pltpu.SemaphoreType.DMA((KVH, 3)),
        ],
        compiler_params=pltpu.CompilerParams(vmem_limit_bytes=60 * 2**20),
        name="attend",
    )(routed, returned, keys, lens, values, query)


def on_device(hidden, adapter_id, adapter_slot, cache_len, base_q, kv_cache, a_maps, b_maps):
    owners = lax.axis_size("owner")
    rows = hidden.shape[0]
    held = a_maps.shape[1] // RANK
    slot_count = max(2, 2 * ((rows + 2 * owners - 1) // (2 * owners)))
    bins = owners * slot_count
    packed, routed = pack(hidden, adapter_id, adapter_slot, owners, slot_count, held)
    packed = packed.reshape(owners, slot_count, packed.shape[1])
    arrived = lax.all_to_all(packed, "owner", split_axis=0, concat_axis=0, tiled=True)
    laid = prep(base_q, kv_cache)
    change = adapt(arrived.reshape(bins, arrived.shape[2]), a_maps, b_maps, laid[0])
    change = change.reshape(owners, slot_count, change.shape[1])
    returned = lax.all_to_all(change, "owner", split_axis=0, concat_axis=0, tiled=True)
    returned = returned.reshape(bins, returned.shape[2])
    return attend(routed, returned, cache_len, laid, kv_cache.shape[2])


def solution(mesh):
    return jax.shard_map(
        on_device,
        mesh=mesh,
        in_specs=(
            P(("groups", "owner"), None),
            P(("groups", "owner")),
            P("groups"),
            P(("groups", "owner")),
            P(("groups", "owner"), None),
            P(("groups", "owner"), None, None, None),
            P(None, "owner"),
            P("owner", None),
        ),
        out_specs=P(("groups", "owner"), None),
        check_vma=False,
    )
```

```python
import functools

import jax
import jax.numpy as jnp
from jax import lax
from jax.experimental import pallas as pl
from jax.experimental.pallas import tpu as pltpu
from jax.sharding import PartitionSpec as P

HEAD = 128
KVH = 4
RANK = 64
LANES = 128
SCALE = 2.0
ROWS_STEP = 8
COLUMNS_STEP = 1024
GRANT = 48 * 2**20
TALL_BYTES = 17 * 2**20


def routing(owners, slot_count, held, slots, ids):
    rows = ids.shape[1]
    named = lax.broadcasted_iota(jnp.int32, (slots.shape[1], rows), 0) == ids
    slot = jnp.dot(
        slots.astype(jnp.float32).astype(jnp.bfloat16),
        named.astype(jnp.bfloat16),
        preferred_element_type=jnp.float32,
    ).astype(jnp.int32)
    owner = lax.div(slot, held)
    local = slot - owner * held
    hits = owner == lax.broadcasted_iota(jnp.int32, (owners, rows), 0)
    earlier = lax.broadcasted_iota(jnp.int32, (rows, rows), 0) < lax.broadcasted_iota(
        jnp.int32, (rows, rows), 1
    )
    before = jnp.dot(
        hits.astype(jnp.bfloat16), earlier.astype(jnp.bfloat16), preferred_element_type=jnp.float32
    )
    place = jnp.sum(jnp.where(hits, before, 0.0), axis=0, keepdims=True).astype(jnp.int32)
    bins = owner * slot_count + place
    routed = bins == lax.broadcasted_iota(jnp.int32, (owners * slot_count, rows), 0)
    label = jnp.sum(jnp.where(routed, local.astype(jnp.float32), 0.0), axis=1, keepdims=True)
    return routed.astype(jnp.bfloat16), label


def pack_kernel(owners, slot_count, held, slots_hbm, ids_hbm, hidden_hbm, packed_hbm, routed_hbm, *scratch):
    slots_ref, ids_ref, rows_ref, bins_ref, routed_ref, small_sems, sems, out_sems = scratch
    width = rows_ref.shape[1]
    spans = [(at, min(COLUMNS_STEP, width - at)) for at in range(0, width, COLUMNS_STEP)]
    small = [
        pltpu.make_async_copy(slots_hbm, slots_ref, small_sems.at[0]),
        pltpu.make_async_copy(ids_hbm, ids_ref, small_sems.at[1]),
    ]
    loads = [
        pltpu.make_async_copy(
            hidden_hbm.at[:, pl.ds(at, size)], rows_ref.at[:, pl.ds(at, size)], sems.at[i]
        )
        for i, (at, size) in enumerate(spans)
    ]
    stores = [
        pltpu.make_async_copy(
            bins_ref.at[:, pl.ds(at, size)], packed_hbm.at[:, pl.ds(at, size)], out_sems.at[i]
        )
        for i, (at, size) in enumerate([*spans, (width, LANES)])
    ]
    routed_store = pltpu.make_async_copy(routed_ref, routed_hbm, small_sems.at[2])
    for copy in [*small, *loads]:
        copy.start()
    for copy in small:
        copy.wait()
    routed, label = routing(owners, slot_count, held, slots_ref[...], ids_ref[...])
    for load, store, (at, size) in zip(loads, stores, spans):
        load.wait()
        bins_ref[:, at : at + size] = jnp.dot(
            routed, rows_ref[:, at : at + size], preferred_element_type=jnp.float32
        ).astype(bins_ref.dtype)
        store.start()
        if at == 0:
            bins_ref[:, width:] = jnp.broadcast_to(label, (label.shape[0], LANES)).astype(
                bins_ref.dtype
            )
            stores[-1].start()
            routed_ref[...] = jnp.transpose(routed.astype(jnp.float32)).astype(routed_ref.dtype)
            routed_store.start()
    for store in stores:
        store.wait()
    routed_store.wait()


def pack(hidden, adapter_id, adapter_slot, owners, slot_count, held):
    rows, width = hidden.shape
    bins = owners * slot_count
    steps = pl.cdiv(width, COLUMNS_STEP)
    slots = adapter_slot.reshape(1, -1)
    return pl.pallas_call(
        functools.partial(pack_kernel, owners, slot_count, held),
        in_specs=[pl.BlockSpec(memory_space=pl.ANY)] * 3,
        out_specs=[pl.BlockSpec(memory_space=pl.ANY)] * 2,
        out_shape=[
            jax.ShapeDtypeStruct((bins, width + LANES), hidden.dtype),
            jax.ShapeDtypeStruct((rows, bins), jnp.bfloat16),
        ],
        scratch_shapes=[
            pltpu.VMEM(slots.shape, jnp.int32),
            pltpu.VMEM((1, rows), jnp.int32),
            pltpu.VMEM((rows, width), hidden.dtype),
            pltpu.VMEM((bins, width + LANES), hidden.dtype),
            pltpu.VMEM((rows, bins), jnp.bfloat16),
            pltpu.SemaphoreType.DMA((3,)),
            pltpu.SemaphoreType.DMA((steps,)),
            pltpu.SemaphoreType.DMA((steps + 1,)),
        ],
        compiler_params=pltpu.CompilerParams(vmem_limit_bytes=56 * 2**20),
        name="pack",
    )(slots, adapter_id.reshape(1, rows), hidden)


def adapt_kernel(arrived_ref, a_ref, b_ref, _, change_ref):
    width = a_ref.shape[0]
    low = jnp.zeros((arrived_ref.shape[0], a_ref.shape[1]), jnp.float32)
    for at in range(0, width, COLUMNS_STEP):
        low += jnp.dot(
            arrived_ref[:, at : at + COLUMNS_STEP],
            a_ref[at : at + COLUMNS_STEP, :],
            preferred_element_type=jnp.float32,
        )
    label = arrived_ref[:, width:].astype(jnp.float32)[:, :1].astype(jnp.int32)
    column = lax.broadcasted_iota(jnp.int32, low.shape, 1) // RANK
    low = jnp.where(column == label, low, 0.0).astype(jnp.bfloat16)
    out_width = b_ref.shape[1]
    piece = min(1024, out_width)
    for at in range(0, out_width, piece):
        change_ref[:, at : at + piece] = (
            SCALE * jnp.dot(low, b_ref[:, at : at + piece], preferred_element_type=jnp.float32)
        ).astype(change_ref.dtype)


def adapt(arrived, a_maps, b_maps, after):
    return pl.pallas_call(
        adapt_kernel,
        in_specs=[pl.BlockSpec(memory_space=pltpu.VMEM)] * 3 + [pl.BlockSpec(memory_space=pl.ANY)],
        out_specs=pl.BlockSpec(memory_space=pltpu.VMEM),
        out_shape=jax.ShapeDtypeStruct((arrived.shape[0], b_maps.shape[1]), jnp.bfloat16),
        compiler_params=pltpu.CompilerParams(vmem_limit_bytes=GRANT),
        name="adapt",
    )(arrived, a_maps, b_maps, after)


def tall(rows, group):
    return jnp.concatenate([rows[:, g * HEAD : (g + 1) * HEAD] for g in range(group)], axis=0)


def prep_kernel(group, base_ref, kv_ref, keys_ref, rest_ref):
    step, context = kv_ref.shape[0], kv_ref.shape[2]
    cells = step * context
    for k in range(KVH):
        head = slice(k * HEAD, (k + 1) * HEAD)
        keys = kv_ref[:, 0, :, head].astype(jnp.float32).reshape(cells, HEAD)
        keys_ref[k] = jnp.transpose(keys).astype(keys_ref.dtype)
        rest_ref[k, :cells] = kv_ref[:, 1, :, head].reshape(cells, HEAD)
        base = base_ref[:, k * group * HEAD : (k + 1) * group * HEAD].astype(jnp.float32)
        rest_ref[k, cells:] = tall(base, group).astype(rest_ref.dtype)


def prep(base_q, kv_cache):
    rows, width = base_q.shape
    context = kv_cache.shape[2]
    group = width // (KVH * HEAD)
    step = ROWS_STEP
    steps = rows // step
    cells = step * context
    lines = cells + group * step
    length = pl.cdiv(max(TALL_BYTES // (2 * KVH * HEAD), steps * lines), lines) * lines
    return pl.pallas_call(
        functools.partial(prep_kernel, group),
        grid=(steps,),
        in_specs=[
            pl.BlockSpec((step, width), lambda i: (i, 0)),
            pl.BlockSpec((step, *kv_cache.shape[1:]), lambda i: (i, 0, 0, 0)),
        ],
        out_specs=[
            pl.BlockSpec((KVH, HEAD, cells), lambda i: (0, 0, i)),
            pl.BlockSpec((KVH, lines, HEAD), lambda i: (0, i, 0)),
        ],
        out_shape=[
            jax.ShapeDtypeStruct((KVH, HEAD, rows * context), jnp.bfloat16),
            jax.ShapeDtypeStruct((KVH, length, HEAD), jnp.bfloat16),
        ],
        compiler_params=pltpu.CompilerParams(vmem_limit_bytes=GRANT),
        name="prep",
    )(base_q, kv_cache)


def attend_kernel(
    group, context, routed_ref, returned_ref, keys_ref, lens_ref, rest_hbm, out_hbm, rest_ref, bias_ref, out_ref, sems
):
    step = ROWS_STEP
    steps, lines, cells = bias_ref.shape
    block = cells + lines
    span = group * HEAD
    factor = 1.0 / jnp.sqrt(jnp.float32(HEAD))
    loads = [
        pltpu.make_async_copy(
            rest_hbm.at[k, pl.ds(0, steps * block)], rest_ref.at[k], sems.at[k, 0]
        )
        for k in range(KVH)
    ]
    stores = [
        pltpu.make_async_copy(
            out_ref.at[:, pl.ds(k * span, span)], out_hbm.at[:, pl.ds(k * span, span)], sems.at[k, 1]
        )
        for k in range(KVH)
    ]
    for load in loads:
        load.start()
    lane = lax.broadcasted_iota(jnp.int32, (lines, cells), 1)
    line = lax.broadcasted_iota(jnp.int32, (lines, cells), 0)
    own = lax.div(lane, context) == lax.rem(line, step)
    position = lax.rem(lane, context)
    for i in range(steps):
        bias_ref[i] = jnp.where(own & (position < lens_ref[i]), 0.0, -jnp.inf)
    for k in range(KVH):
        delta = jnp.dot(
            routed_ref[...],
            returned_ref[:, k * span : (k + 1) * span],
            preferred_element_type=jnp.float32,
        )
        loads[k].wait()
        for i in range(steps):
            rows = slice(i * step, (i + 1) * step)
            keys = keys_ref[k, :, i * cells : (i + 1) * cells]
            values = rest_ref[k, i * block : i * block + cells, :]
            query = rest_ref[k, i * block + cells : (i + 1) * block, :]
            change = tall(delta[rows], group).astype(jnp.bfloat16)
            scores = jnp.dot(
                jnp.concatenate([query, change], axis=1),
                jnp.concatenate([keys, keys], axis=0),
                preferred_element_type=jnp.float32,
            )
            scores = scores * factor + bias_ref[i]
            expo = jnp.exp(scores - jnp.max(scores, axis=1, keepdims=True))
            probs = expo * (1.0 / jnp.sum(expo, axis=1, keepdims=True))
            out = jnp.dot(probs.astype(jnp.bfloat16), values, preferred_element_type=jnp.float32)
            for g in range(group):
                out_ref[rows, (k * group + g) * HEAD : (k * group + g + 1) * HEAD] = out[
                    g * step : (g + 1) * step
                ].astype(out_ref.dtype)
        stores[k].start()
    for store in stores:
        store.wait()


def attend(routed, returned, cache_len, keys, rest, context):
    rows, width = routed.shape[0], returned.shape[1]
    group = width // (KVH * HEAD)
    step = ROWS_STEP
    steps = rows // step
    cells = step * context
    lens = jnp.repeat(cache_len, context).reshape(steps, 1, cells)
    return pl.pallas_call(
        functools.partial(attend_kernel, group, context),
        in_specs=[pl.BlockSpec(memory_space=pltpu.VMEM)] * 4 + [pl.BlockSpec(memory_space=pl.ANY)],
        out_specs=pl.BlockSpec(memory_space=pl.ANY),
        out_shape=jax.ShapeDtypeStruct((rows, width), jnp.bfloat16),
        scratch_shapes=[
            pltpu.VMEM((KVH, steps * (cells + group * step), HEAD), rest.dtype),
            pltpu.VMEM((steps, group * step, cells), jnp.float32),
            pltpu.VMEM((rows, width), jnp.bfloat16),
            pltpu.SemaphoreType.DMA((KVH, 2)),
        ],
        compiler_params=pltpu.CompilerParams(vmem_limit_bytes=GRANT),
        name="attend",
    )(routed, returned, keys, lens, rest)


def on_device(hidden, adapter_id, adapter_slot, cache_len, base_q, kv_cache, a_maps, b_maps):
    owners = lax.axis_size("owner")
    rows = hidden.shape[0]
    held = a_maps.shape[1] // RANK
    slot_count = max(2, 2 * ((rows + 2 * owners - 1) // (2 * owners)))
    bins = owners * slot_count
    packed, routed = pack(hidden, adapter_id, adapter_slot, owners, slot_count, held)
    packed = packed.reshape(owners, slot_count, packed.shape[1])
    arrived = lax.all_to_all(packed, "owner", split_axis=0, concat_axis=0, tiled=True)
    keys, rest = prep(base_q, kv_cache)
    change = adapt(arrived.reshape(bins, arrived.shape[2]), a_maps, b_maps, rest)
    change = change.reshape(owners, slot_count, change.shape[1])
    returned = lax.all_to_all(change, "owner", split_axis=0, concat_axis=0, tiled=True)
    returned = returned.reshape(bins, returned.shape[2])
    return attend(routed, returned, cache_len, keys, rest, kv_cache.shape[2])


def solution(mesh):
    return jax.shard_map(
        on_device,
        mesh=mesh,
        in_specs=(
            P(("groups", "owner"), None),
            P(("groups", "owner")),
            P("groups"),
            P(("groups", "owner")),
            P(("groups", "owner"), None),
            P(("groups", "owner"), None, None, None),
            P(None, "owner"),
            P("owner", None),
        ),
        out_specs=P(("groups", "owner"), None),
        check_vma=False,
    )
```

```python
import functools

import jax
import jax.numpy as jnp
from jax import lax
from jax.experimental import pallas as pl
from jax.experimental.pallas import tpu as pltpu
from jax.sharding import PartitionSpec as P

HEAD = 128
KVH = 4
RANK = 64
LANES = 128
SCALE = 2.0
ROWS_STEP = 8
COLUMNS_STEP = 2048
FAR_GROUPS = 2
GRANT = 48 * 2**20
TALL_BYTES = 17 * 2**20


def routing(pairs, owners, slot_count, held, slots_ref, ids_ref):
    ids = ids_ref[...]
    rows = ids.shape[1]
    half = owners // 2
    named = lax.broadcasted_iota(jnp.int32, (slots_ref.shape[1], rows), 0) == ids
    slot = jnp.dot(
        slots_ref[...].astype(jnp.float32).astype(jnp.bfloat16),
        named.astype(jnp.bfloat16),
        preferred_element_type=jnp.float32,
    ).astype(jnp.int32)
    owner = lax.div(slot, held)
    local = slot - owner * held
    hits = owner == lax.broadcasted_iota(jnp.int32, (owners, rows), 0)
    earlier = lax.broadcasted_iota(jnp.int32, (rows, rows), 0) < lax.broadcasted_iota(
        jnp.int32, (rows, rows), 1
    )
    before = jnp.dot(
        hits.astype(jnp.bfloat16), earlier.astype(jnp.bfloat16), preferred_element_type=jnp.float32
    )
    place = jnp.sum(jnp.where(hits, before, 0.0), axis=0, keepdims=True).astype(jnp.int32)
    apart = owner ^ lax.axis_index("owner")
    message = lax.rem(apart if pairs else owner, half)
    meant = (apart >= half) == pairs
    line = lax.broadcasted_iota(jnp.int32, (half * slot_count, rows), 0)
    routed = line == jnp.where(meant, message * slot_count + place, -1)
    label = jnp.sum(jnp.where(routed, local.astype(jnp.float32), 0.0), axis=1, keepdims=True)
    return routed.astype(jnp.bfloat16), label


def pack_kernel(
    pairs, owners, slot_count, held, slots_ref, ids_ref, hidden_ref, after_ref, routed_ref, *refs
):
    *packed_refs, rows_ref, sems = refs
    width = hidden_ref.shape[1]
    spans = [(at, min(COLUMNS_STEP, width - at)) for at in range(0, width, COLUMNS_STEP)]
    loads = [
        pltpu.make_async_copy(
            hidden_ref.at[:, pl.ds(at, size)], rows_ref.at[:, pl.ds(at, size)], sems.at[i]
        )
        for i, (at, size) in enumerate(spans)
    ]
    for load in loads:
        load.start()
    routed, label = routing(pairs, owners, slot_count, held, slots_ref, ids_ref)
    routed_ref[...] = routed
    label = jnp.broadcast_to(label, (label.shape[0], LANES))
    count = packed_refs[0].shape[0]

    def put(at, lines):
        for i, packed_ref in enumerate(packed_refs):
            packed_ref[:, at : at + lines.shape[1]] = lines[i * count : (i + 1) * count].astype(
                packed_ref.dtype
            )

    put(width, label)
    for load, (at, size) in zip(loads, spans):
        load.wait()
        put(at, jnp.dot(routed, rows_ref[:, at : at + size], preferred_element_type=jnp.float32))


def pack(hidden, adapter_id, adapter_slot, after, pairs, owners, slot_count, held):
    rows, width = hidden.shape
    lines = owners // 2 * slot_count
    messages = owners // 2 if pairs else 1
    steps = pl.cdiv(width, COLUMNS_STEP)
    return pl.pallas_call(
        functools.partial(pack_kernel, pairs, owners, slot_count, held),
        in_specs=[
            pl.BlockSpec(memory_space=pltpu.VMEM),
            pl.BlockSpec(memory_space=pltpu.VMEM),
            pl.BlockSpec(memory_space=pl.ANY),
            pl.BlockSpec(memory_space=pl.ANY),
        ],
        out_specs=[pl.BlockSpec(memory_space=pltpu.VMEM)] * (1 + messages),
        out_shape=[jax.ShapeDtypeStruct((lines, rows), jnp.bfloat16)]
        + [jax.ShapeDtypeStruct((lines // messages, width + LANES), hidden.dtype)] * messages,
        scratch_shapes=[
            pltpu.VMEM((rows, width), hidden.dtype),
            pltpu.SemaphoreType.DMA((steps,)),
        ],
        compiler_params=pltpu.CompilerParams(vmem_limit_bytes=56 * 2**20),
        name="pack_pairs" if pairs else "pack",
    )(adapter_slot.reshape(1, -1), adapter_id.reshape(1, rows), hidden, after)


def stack(refs, at, size):
    if len(refs) == 1:
        return refs[0][:, at : at + size]
    return jnp.concatenate(
        [ref[:, at : at + size].astype(jnp.float32) for ref in refs], axis=0
    ).astype(jnp.bfloat16)


def adapt_kernel(count, *refs):
    arrived_refs, (a_ref, b_ref, _), change_refs = refs[:count], refs[count : count + 3], refs[count + 3 :]
    width = a_ref.shape[0]
    lines = arrived_refs[0].shape[0]
    low = jnp.zeros((count * lines, a_ref.shape[1]), jnp.float32)
    for at in range(0, width, COLUMNS_STEP):
        low += jnp.dot(
            stack(arrived_refs, at, COLUMNS_STEP),
            a_ref[at : at + COLUMNS_STEP, :],
            preferred_element_type=jnp.float32,
        )
    label = stack(arrived_refs, width, LANES).astype(jnp.float32)[:, :1].astype(jnp.int32)
    column = lax.broadcasted_iota(jnp.int32, low.shape, 1) // RANK
    low = jnp.where(column == label, low, 0.0).astype(jnp.bfloat16)
    out_width = b_ref.shape[1]
    piece = min(1024, out_width)
    for at in range(0, out_width, piece):
        change = SCALE * jnp.dot(low, b_ref[:, at : at + piece], preferred_element_type=jnp.float32)
        for i, change_ref in enumerate(change_refs):
            change_ref[:, at : at + piece] = change[i * lines : (i + 1) * lines].astype(
                change_ref.dtype
            )


def adapt(arrived, a_maps, b_maps, after):
    count = len(arrived)
    lines = arrived[0].shape[0]
    return pl.pallas_call(
        functools.partial(adapt_kernel, count),
        in_specs=[pl.BlockSpec(memory_space=pltpu.VMEM)] * (count + 2)
        + [pl.BlockSpec(memory_space=pl.ANY)],
        out_specs=[pl.BlockSpec(memory_space=pltpu.VMEM)] * count,
        out_shape=[jax.ShapeDtypeStruct((lines, b_maps.shape[1]), jnp.bfloat16)] * count,
        compiler_params=pltpu.CompilerParams(vmem_limit_bytes=GRANT),
        name="adapt",
    )(*arrived, a_maps, b_maps, after)


def tall(rows, group):
    return jnp.concatenate([rows[:, g * HEAD : (g + 1) * HEAD] for g in range(group)], axis=0)


def prep_kernel(group, base_ref, kv_ref, _, keys_ref, rest_ref):
    step, context = kv_ref.shape[0], kv_ref.shape[2]
    cells = step * context
    for k in range(KVH):
        head = slice(k * HEAD, (k + 1) * HEAD)
        keys = kv_ref[:, 0, :, head].astype(jnp.float32).reshape(cells, HEAD)
        keys_ref[k] = jnp.transpose(keys).astype(keys_ref.dtype)
        rest_ref[k, :cells] = kv_ref[:, 1, :, head].reshape(cells, HEAD)
        base = base_ref[:, k * group * HEAD : (k + 1) * group * HEAD].astype(jnp.float32)
        rest_ref[k, cells:] = tall(base, group).astype(rest_ref.dtype)


def prep(base_q, kv_cache, after):
    rows, width = base_q.shape
    context = kv_cache.shape[2]
    group = width // (KVH * HEAD)
    step = ROWS_STEP
    steps = rows // step
    cells = step * context
    lines = cells + group * step
    length = pl.cdiv(max(TALL_BYTES // (2 * KVH * HEAD), steps * lines), lines) * lines
    return pl.pallas_call(
        functools.partial(prep_kernel, group),
        grid=(steps,),
        in_specs=[
            pl.BlockSpec((step, width), lambda i: (i, 0)),
            pl.BlockSpec((step, *kv_cache.shape[1:]), lambda i: (i, 0, 0, 0)),
            pl.BlockSpec(memory_space=pl.ANY),
        ],
        out_specs=[
            pl.BlockSpec((KVH, HEAD, cells), lambda i: (0, 0, i)),
            pl.BlockSpec((KVH, lines, HEAD), lambda i: (0, i, 0)),
        ],
        out_shape=[
            jax.ShapeDtypeStruct((KVH, HEAD, rows * context), jnp.bfloat16),
            jax.ShapeDtypeStruct((KVH, length, HEAD), jnp.bfloat16),
        ],
        compiler_params=pltpu.CompilerParams(vmem_limit_bytes=GRANT),
        name="prep",
    )(base_q, kv_cache, after)


def attend_kernel(group, context, count, *refs):
    routed_refs, returned_refs, refs = refs[:2], refs[2 : 2 + count], refs[2 + count :]
    keys_ref, lens_ref, rest_hbm, out_hbm, rest_ref, bias_ref, out_ref, sems = refs
    step = ROWS_STEP
    steps, lines, cells = bias_ref.shape
    block = cells + lines
    span = group * HEAD
    factor = 1.0 / jnp.sqrt(jnp.float32(HEAD))
    loads = [
        pltpu.make_async_copy(
            rest_hbm.at[k, pl.ds(0, steps * block)], rest_ref.at[k], sems.at[k, 0]
        )
        for k in range(KVH)
    ]
    stores = [
        pltpu.make_async_copy(
            out_ref.at[:, pl.ds(k * span, span)], out_hbm.at[:, pl.ds(k * span, span)], sems.at[k, 1]
        )
        for k in range(KVH)
    ]
    for load in loads:
        load.start()
    lane = lax.broadcasted_iota(jnp.int32, (lines, cells), 1)
    line = lax.broadcasted_iota(jnp.int32, (lines, cells), 0)
    own = lax.div(lane, context) == lax.rem(line, step)
    position = lax.rem(lane, context)
    for i in range(steps):
        bias_ref[i] = jnp.where(own & (position < lens_ref[i]), 0.0, -jnp.inf)
    routed = jnp.concatenate([ref[...].astype(jnp.float32) for ref in routed_refs], axis=0)
    routed = jnp.transpose(routed).astype(jnp.bfloat16)
    for k in range(KVH):
        delta = jnp.dot(
            routed, stack(returned_refs, k * span, span), preferred_element_type=jnp.float32
        )
        loads[k].wait()
        for i in range(steps):
            rows = slice(i * step, (i + 1) * step)
            keys = keys_ref[k, :, i * cells : (i + 1) * cells]
            values = rest_ref[k, i * block : i * block + cells, :]
            query = rest_ref[k, i * block + cells : (i + 1) * block, :]
            change = tall(delta[rows], group).astype(jnp.bfloat16)
            scores = jnp.dot(
                jnp.concatenate([query, change], axis=1),
                jnp.concatenate([keys, keys], axis=0),
                preferred_element_type=jnp.float32,
            )
            scores = scores * factor + bias_ref[i]
            expo = jnp.exp(scores - jnp.max(scores, axis=1, keepdims=True))
            probs = expo * (1.0 / jnp.sum(expo, axis=1, keepdims=True))
            out = jnp.dot(probs.astype(jnp.bfloat16), values, preferred_element_type=jnp.float32)
            for g in range(group):
                out_ref[rows, (k * group + g) * HEAD : (k * group + g + 1) * HEAD] = out[
                    g * step : (g + 1) * step
                ].astype(out_ref.dtype)
        stores[k].start()
    for store in stores:
        store.wait()


def attend(routed, returned, cache_len, keys, rest, context):
    rows, width = routed[0].shape[1], returned[0].shape[1]
    group = width // (KVH * HEAD)
    step = ROWS_STEP
    steps = rows // step
    cells = step * context
    lens = jnp.repeat(cache_len, context).reshape(steps, 1, cells)
    return pl.pallas_call(
        functools.partial(attend_kernel, group, context, len(returned)),
        in_specs=[pl.BlockSpec(memory_space=pltpu.VMEM)] * (4 + len(returned)) + [pl.BlockSpec(memory_space=pl.ANY)],
        out_specs=pl.BlockSpec(memory_space=pl.ANY),
        out_shape=jax.ShapeDtypeStruct((rows, width), jnp.bfloat16),
        scratch_shapes=[
            pltpu.VMEM((KVH, steps * (cells + group * step), HEAD), rest.dtype),
            pltpu.VMEM((steps, group * step, cells), jnp.float32),
            pltpu.VMEM((rows, width), jnp.bfloat16),
            pltpu.SemaphoreType.DMA((KVH, 2)),
        ],
        compiler_params=pltpu.CompilerParams(vmem_limit_bytes=GRANT),
        name="attend",
    )(*routed, *returned, keys, lens, rest)


def on_device(hidden, adapter_id, adapter_slot, cache_len, base_q, kv_cache, a_maps, b_maps):
    owners = lax.axis_size("owner")
    half = owners // 2
    rows = hidden.shape[0]
    held = a_maps.shape[1] // RANK
    slot_count = max(2, 2 * ((rows + 2 * owners - 1) // (2 * owners)))
    halves = [list(range(half)), list(range(half, owners))]

    def swap(lines):
        blocks = lines.reshape(half, slot_count, lines.shape[1])
        blocks = lax.all_to_all(
            blocks, "owner", split_axis=0, concat_axis=0, tiled=True, axis_index_groups=halves
        )
        return blocks.reshape(lines.shape)

    def trade(messages, first):
        return [
            lax.ppermute(message, "owner", [(i, i ^ (first + j)) for i in range(owners)])
            for j, message in enumerate(messages)
        ]

    whole = functools.partial(pack, hidden, adapter_id, adapter_slot)
    routed_far, *messages = whole(adapter_id, True, owners, slot_count, held)
    size = max(1, half // FAR_GROUPS)
    starts = range(0, half, size)
    arrived_far = [trade(messages[at : at + size], half + at) for at in starts]
    routed, lines = whole(arrived_far[0][0], False, owners, slot_count, held)
    arrived = swap(lines)
    keys, rest = prep(base_q, kv_cache, routed)
    returned, after = [], rest
    for group, at in zip(arrived_far, starts):
        change = adapt(group, a_maps, b_maps, after)
        after = change[0]
        returned += trade(change, half + at)
    (change,) = adapt([arrived], a_maps, b_maps, returned[0])
    returned.append(swap(change))
    return attend([routed_far, routed], returned, cache_len, keys, rest, kv_cache.shape[2])


def solution(mesh):
    return jax.shard_map(
        on_device,
        mesh=mesh,
        in_specs=(
            P(("groups", "owner"), None),
            P(("groups", "owner")),
            P("groups"),
            P(("groups", "owner")),
            P(("groups", "owner"), None),
            P(("groups", "owner"), None, None, None),
            P(None, "owner"),
            P("owner", None),
        ),
        out_specs=P(("groups", "owner"), None),
        check_vma=False,
    )
```

```python
import functools

import jax
import jax.numpy as jnp
from jax import lax
from jax.experimental import pallas as pl
from jax.experimental.pallas import tpu as pltpu
from jax.sharding import PartitionSpec as P

HEAD = 128
KVH = 4
RANK = 64
LANES = 128
SCALE = 2.0
ROWS_STEP = 8
COLUMNS_STEP = 1024
GRANT = 48 * 2**20
TALL_BYTES = 17 * 2**20


def routing(owners, slot_count, held, slots, ids):
    rows = ids.shape[1]
    named = lax.broadcasted_iota(jnp.int32, (slots.shape[1], rows), 0) == ids
    slot = jnp.dot(
        slots.astype(jnp.float32).astype(jnp.bfloat16),
        named.astype(jnp.bfloat16),
        preferred_element_type=jnp.float32,
    ).astype(jnp.int32)
    owner = lax.div(slot, held)
    local = slot - owner * held
    hits = owner == lax.broadcasted_iota(jnp.int32, (owners, rows), 0)
    earlier = lax.broadcasted_iota(jnp.int32, (rows, rows), 0) < lax.broadcasted_iota(
        jnp.int32, (rows, rows), 1
    )
    before = jnp.dot(
        hits.astype(jnp.bfloat16), earlier.astype(jnp.bfloat16), preferred_element_type=jnp.float32
    )
    place = jnp.sum(jnp.where(hits, before, 0.0), axis=0, keepdims=True).astype(jnp.int32)
    bins = owner * slot_count + place
    routed = bins == lax.broadcasted_iota(jnp.int32, (owners * slot_count, rows), 0)
    label = jnp.sum(jnp.where(routed, local.astype(jnp.float32), 0.0), axis=1, keepdims=True)
    return routed.astype(jnp.bfloat16), label


def pack_kernel(owners, slot_count, held, slots_hbm, ids_hbm, hidden_hbm, packed_hbm, routed_hbm, *scratch):
    slots_ref, ids_ref, rows_ref, bins_ref, routed_ref, small_sems, sems, out_sems = scratch
    width = rows_ref.shape[1]
    spans = [(at, min(COLUMNS_STEP, width - at)) for at in range(0, width, COLUMNS_STEP)]
    small = [
        pltpu.make_async_copy(slots_hbm, slots_ref, small_sems.at[0]),
        pltpu.make_async_copy(ids_hbm, ids_ref, small_sems.at[1]),
    ]
    loads = [
        pltpu.make_async_copy(
            hidden_hbm.at[:, pl.ds(at, size)], rows_ref.at[:, pl.ds(at, size)], sems.at[i]
        )
        for i, (at, size) in enumerate(spans)
    ]
    stores = [
        pltpu.make_async_copy(
            bins_ref.at[:, pl.ds(at, size)], packed_hbm.at[:, pl.ds(at, size)], out_sems.at[i]
        )
        for i, (at, size) in enumerate([*spans, (width, LANES)])
    ]
    routed_store = pltpu.make_async_copy(routed_ref, routed_hbm, small_sems.at[2])
    for copy in [*small, *loads]:
        copy.start()
    for copy in small:
        copy.wait()
    routed, label = routing(owners, slot_count, held, slots_ref[...], ids_ref[...])
    for load, store, (at, size) in zip(loads, stores, spans):
        load.wait()
        bins_ref[:, at : at + size] = jnp.dot(
            routed, rows_ref[:, at : at + size], preferred_element_type=jnp.float32
        ).astype(bins_ref.dtype)
        store.start()
        if at == 0:
            bins_ref[:, width:] = jnp.broadcast_to(label, (label.shape[0], LANES)).astype(
                bins_ref.dtype
            )
            stores[-1].start()
            routed_ref[...] = jnp.transpose(routed.astype(jnp.float32)).astype(routed_ref.dtype)
            routed_store.start()
    for store in stores:
        store.wait()
    routed_store.wait()


def pack(hidden, adapter_id, adapter_slot, owners, slot_count, held):
    rows, width = hidden.shape
    bins = owners * slot_count
    steps = pl.cdiv(width, COLUMNS_STEP)
    slots = adapter_slot.reshape(1, -1)
    return pl.pallas_call(
        functools.partial(pack_kernel, owners, slot_count, held),
        in_specs=[pl.BlockSpec(memory_space=pl.ANY)] * 3,
        out_specs=[pl.BlockSpec(memory_space=pl.ANY)] * 2,
        out_shape=[
            jax.ShapeDtypeStruct((bins, width + LANES), hidden.dtype),
            jax.ShapeDtypeStruct((rows, bins), jnp.bfloat16),
        ],
        scratch_shapes=[
            pltpu.VMEM(slots.shape, jnp.int32),
            pltpu.VMEM((1, rows), jnp.int32),
            pltpu.VMEM((rows, width), hidden.dtype),
            pltpu.VMEM((bins, width + LANES), hidden.dtype),
            pltpu.VMEM((rows, bins), jnp.bfloat16),
            pltpu.SemaphoreType.DMA((3,)),
            pltpu.SemaphoreType.DMA((steps,)),
            pltpu.SemaphoreType.DMA((steps + 1,)),
        ],
        compiler_params=pltpu.CompilerParams(vmem_limit_bytes=56 * 2**20),
        name="pack",
    )(slots, adapter_id.reshape(1, rows), hidden)


def adapt_kernel(arrived_ref, a_ref, b_ref, _, change_ref):
    width = a_ref.shape[0]
    low = jnp.zeros((arrived_ref.shape[0], a_ref.shape[1]), jnp.float32)
    for at in range(0, width, COLUMNS_STEP):
        low += jnp.dot(
            arrived_ref[:, at : at + COLUMNS_STEP],
            a_ref[at : at + COLUMNS_STEP, :],
            preferred_element_type=jnp.float32,
        )
    label = arrived_ref[:, width:].astype(jnp.float32)[:, :1].astype(jnp.int32)
    column = lax.broadcasted_iota(jnp.int32, low.shape, 1) // RANK
    low = jnp.where(column == label, low, 0.0).astype(jnp.bfloat16)
    out_width = b_ref.shape[1]
    piece = min(1024, out_width)
    for at in range(0, out_width, piece):
        change_ref[:, at : at + piece] = (
            SCALE * jnp.dot(low, b_ref[:, at : at + piece], preferred_element_type=jnp.float32)
        ).astype(change_ref.dtype)


def adapt(arrived, a_maps, b_maps, after):
    return pl.pallas_call(
        adapt_kernel,
        in_specs=[pl.BlockSpec(memory_space=pltpu.VMEM)] * 3 + [pl.BlockSpec(memory_space=pl.ANY)],
        out_specs=pl.BlockSpec(memory_space=pltpu.VMEM),
        out_shape=jax.ShapeDtypeStruct((arrived.shape[0], b_maps.shape[1]), jnp.bfloat16),
        compiler_params=pltpu.CompilerParams(vmem_limit_bytes=16 * 2**20),
        name="adapt",
    )(arrived, a_maps, b_maps, after)


def tall(rows, group):
    return jnp.concatenate([rows[:, g * HEAD : (g + 1) * HEAD] for g in range(group)], axis=0)


def prep_kernel(group, base_ref, kv_ref, keys_ref, rest_ref, token_ref):
    token_ref[...] = jnp.zeros_like(token_ref)
    step, context = kv_ref.shape[0], kv_ref.shape[2]
    cells = step * context
    for k in range(KVH):
        head = slice(k * HEAD, (k + 1) * HEAD)
        keys = kv_ref[:, 0, :, head].astype(jnp.float32).reshape(cells, HEAD)
        keys_ref[k] = jnp.transpose(keys).astype(keys_ref.dtype)
        rest_ref[k, :cells] = kv_ref[:, 1, :, head].reshape(cells, HEAD)
        base = base_ref[:, k * group * HEAD : (k + 1) * group * HEAD].astype(jnp.float32)
        rest_ref[k, cells:] = tall(base, group).astype(rest_ref.dtype)


def prep(base_q, kv_cache):
    rows, width = base_q.shape
    context = kv_cache.shape[2]
    group = width // (KVH * HEAD)
    step = ROWS_STEP
    steps = rows // step
    cells = step * context
    lines = cells + group * step
    length = pl.cdiv(max(TALL_BYTES // (2 * KVH * HEAD), steps * lines), lines) * lines
    return pl.pallas_call(
        functools.partial(prep_kernel, group),
        grid=(steps,),
        in_specs=[
            pl.BlockSpec((step, width), lambda i: (i, 0)),
            pl.BlockSpec((step, *kv_cache.shape[1:]), lambda i: (i, 0, 0, 0)),
        ],
        out_specs=[
            pl.BlockSpec((KVH, HEAD, cells), lambda i: (0, 0, i)),
            pl.BlockSpec((KVH, lines, HEAD), lambda i: (0, i, 0)),
            pl.BlockSpec((8, LANES), lambda i: (0, 0)),
        ],
        out_shape=[
            jax.ShapeDtypeStruct((KVH, HEAD, rows * context), jnp.bfloat16),
            jax.ShapeDtypeStruct((KVH, length, HEAD), jnp.bfloat16),
            jax.ShapeDtypeStruct((8, LANES), jnp.float32),
        ],
        compiler_params=pltpu.CompilerParams(vmem_limit_bytes=60 * 2**20),
        name="prep",
    )(base_q, kv_cache)


def attend_kernel(
    group, context, routed_ref, returned_ref, keys_ref, lens_ref, rest_hbm, out_hbm, rest_ref, bias_ref, out_ref, sems
):
    step = ROWS_STEP
    steps, lines, cells = bias_ref.shape
    block = cells + lines
    span = group * HEAD
    factor = 1.0 / jnp.sqrt(jnp.float32(HEAD))
    loads = [
        pltpu.make_async_copy(
            rest_hbm.at[k, pl.ds(0, steps * block)], rest_ref.at[k], sems.at[k, 0]
        )
        for k in range(KVH)
    ]
    stores = [
        pltpu.make_async_copy(
            out_ref.at[:, pl.ds(k * span, span)], out_hbm.at[:, pl.ds(k * span, span)], sems.at[k, 1]
        )
        for k in range(KVH)
    ]
    for load in loads:
        load.start()
    lane = lax.broadcasted_iota(jnp.int32, (lines, cells), 1)
    line = lax.broadcasted_iota(jnp.int32, (lines, cells), 0)
    own = lax.div(lane, context) == lax.rem(line, step)
    position = lax.rem(lane, context)
    for i in range(steps):
        bias_ref[i] = jnp.where(own & (position < lens_ref[i]), 0.0, -jnp.inf)
    for k in range(KVH):
        delta = jnp.dot(
            routed_ref[...],
            returned_ref[:, k * span : (k + 1) * span],
            preferred_element_type=jnp.float32,
        )
        loads[k].wait()
        for i in range(steps):
            rows = slice(i * step, (i + 1) * step)
            keys = keys_ref[k, :, i * cells : (i + 1) * cells]
            values = rest_ref[k, i * block : i * block + cells, :]
            query = rest_ref[k, i * block + cells : (i + 1) * block, :]
            change = tall(delta[rows], group).astype(jnp.bfloat16)
            scores = jnp.dot(
                jnp.concatenate([query, change], axis=1),
                jnp.concatenate([keys, keys], axis=0),
                preferred_element_type=jnp.float32,
            )
            scores = scores * factor + bias_ref[i]
            expo = jnp.exp(scores - jnp.max(scores, axis=1, keepdims=True))
            probs = expo * (1.0 / jnp.sum(expo, axis=1, keepdims=True))
            out = jnp.dot(probs.astype(jnp.bfloat16), values, preferred_element_type=jnp.float32)
            for g in range(group):
                out_ref[rows, (k * group + g) * HEAD : (k * group + g + 1) * HEAD] = out[
                    g * step : (g + 1) * step
                ].astype(out_ref.dtype)
        stores[k].start()
    for store in stores:
        store.wait()


def attend(routed, returned, cache_len, keys, rest, context):
    rows, width = routed.shape[0], returned.shape[1]
    group = width // (KVH * HEAD)
    step = ROWS_STEP
    steps = rows // step
    cells = step * context
    lens = jnp.repeat(cache_len, context).reshape(steps, 1, cells)
    return pl.pallas_call(
        functools.partial(attend_kernel, group, context),
        in_specs=[pl.BlockSpec(memory_space=pltpu.VMEM)] * 4 + [pl.BlockSpec(memory_space=pl.ANY)],
        out_specs=pl.BlockSpec(memory_space=pl.ANY),
        out_shape=jax.ShapeDtypeStruct((rows, width), jnp.bfloat16),
        scratch_shapes=[
            pltpu.VMEM((KVH, steps * (cells + group * step), HEAD), rest.dtype),
            pltpu.VMEM((steps, group * step, cells), jnp.float32),
            pltpu.VMEM((rows, width), jnp.bfloat16),
            pltpu.SemaphoreType.DMA((KVH, 2)),
        ],
        compiler_params=pltpu.CompilerParams(vmem_limit_bytes=GRANT),
        name="attend",
    )(routed, returned, keys, lens, rest)


def on_device(hidden, adapter_id, adapter_slot, cache_len, base_q, kv_cache, a_maps, b_maps):
    owners = lax.axis_size("owner")
    rows = hidden.shape[0]
    held = a_maps.shape[1] // RANK
    slot_count = max(2, 2 * ((rows + 2 * owners - 1) // (2 * owners)))
    bins = owners * slot_count
    packed, routed = pack(hidden, adapter_id, adapter_slot, owners, slot_count, held)
    packed = packed.reshape(owners, slot_count, packed.shape[1])
    arrived = lax.all_to_all(packed, "owner", split_axis=0, concat_axis=0, tiled=True)
    keys, rest, token = prep(base_q, kv_cache)
    change = adapt(arrived.reshape(bins, arrived.shape[2]), a_maps, b_maps, token)
    change = change.reshape(owners, slot_count, change.shape[1])
    returned = lax.all_to_all(change, "owner", split_axis=0, concat_axis=0, tiled=True)
    returned = returned.reshape(bins, returned.shape[2])
    return attend(routed, returned, cache_len, keys, rest, kv_cache.shape[2])


def solution(mesh):
    return jax.shard_map(
        on_device,
        mesh=mesh,
        in_specs=(
            P(("groups", "owner"), None),
            P(("groups", "owner")),
            P("groups"),
            P(("groups", "owner")),
            P(("groups", "owner"), None),
            P(("groups", "owner"), None, None, None),
            P(None, "owner"),
            P("owner", None),
        ),
        out_specs=P(("groups", "owner"), None),
        check_vma=False,
    )
```

```python
import functools

import jax
import jax.numpy as jnp
from jax import lax
from jax.experimental import pallas as pl
from jax.experimental.pallas import tpu as pltpu
from jax.sharding import PartitionSpec as P

HEAD = 128
KVH = 4
RANK = 64
SCALE = 2.0
ROWS_STEP = 8
COLUMNS_STEP = 1024
GRANT = 48 * 2**20
TALL_BYTES = 17 * 2**20


def routing(owners, slot_count, held, slots, ids):
    rows = ids.shape[1]
    named = lax.broadcasted_iota(jnp.int32, (slots.shape[1], rows), 0) == ids
    slot = jnp.dot(
        slots.astype(jnp.float32).astype(jnp.bfloat16),
        named.astype(jnp.bfloat16),
        preferred_element_type=jnp.float32,
    ).astype(jnp.int32)
    owner = lax.div(slot, held)
    local = slot - owner * held
    hits = owner == lax.broadcasted_iota(jnp.int32, (owners, rows), 0)
    earlier = lax.broadcasted_iota(jnp.int32, (rows, rows), 0) < lax.broadcasted_iota(
        jnp.int32, (rows, rows), 1
    )
    before = jnp.dot(
        hits.astype(jnp.bfloat16), earlier.astype(jnp.bfloat16), preferred_element_type=jnp.float32
    )
    place = jnp.sum(jnp.where(hits, before, 0.0), axis=0, keepdims=True).astype(jnp.int32)
    bins = owner * slot_count + place
    routed = bins == lax.broadcasted_iota(jnp.int32, (owners * slot_count, rows), 0)
    return routed.astype(jnp.bfloat16), local.astype(jnp.float32).astype(jnp.bfloat16)


def pack_kernel(
    owners, slot_count, held, slots_hbm, ids_hbm, hidden_hbm, packed_hbm, routed_hbm, labels_hbm, *scratch
):
    slots_ref, ids_ref, rows_ref, bins_ref, routed_ref, labels_ref, small_sems, sems, out_sems = scratch
    width = rows_ref.shape[1]
    spans = [(at, min(COLUMNS_STEP, width - at)) for at in range(0, width, COLUMNS_STEP)]
    small = [
        pltpu.make_async_copy(slots_hbm, slots_ref, small_sems.at[0]),
        pltpu.make_async_copy(ids_hbm, ids_ref, small_sems.at[1]),
    ]
    loads = [
        pltpu.make_async_copy(
            hidden_hbm.at[:, pl.ds(at, size)], rows_ref.at[:, pl.ds(at, size)], sems.at[i]
        )
        for i, (at, size) in enumerate(spans)
    ]
    stores = [
        pltpu.make_async_copy(
            bins_ref.at[:, pl.ds(at, size)], packed_hbm.at[:, pl.ds(at, size)], out_sems.at[i]
        )
        for i, (at, size) in enumerate(spans)
    ]
    small_stores = [
        pltpu.make_async_copy(routed_ref, routed_hbm, small_sems.at[2]),
        pltpu.make_async_copy(labels_ref, labels_hbm, small_sems.at[3]),
    ]
    for copy in [*small, *loads]:
        copy.start()
    for copy in small:
        copy.wait()
    routed, local = routing(owners, slot_count, held, slots_ref[...], ids_ref[...])
    for load, store, (at, size) in zip(loads, stores, spans):
        load.wait()
        bins_ref[:, at : at + size] = jnp.dot(
            routed, rows_ref[:, at : at + size], preferred_element_type=jnp.float32
        ).astype(bins_ref.dtype)
        store.start()
        if at == 0:
            turned = jnp.transpose(routed.astype(jnp.float32)).astype(routed_ref.dtype)
            routed_ref[...] = turned
            labels_ref[...] = jnp.dot(local, turned, preferred_element_type=jnp.float32)
            for copy in small_stores:
                copy.start()
    for copy in [*stores, *small_stores]:
        copy.wait()


def pack(hidden, adapter_id, adapter_slot, owners, slot_count, held):
    rows, width = hidden.shape
    bins = owners * slot_count
    steps = pl.cdiv(width, COLUMNS_STEP)
    slots = adapter_slot.reshape(1, -1)
    return pl.pallas_call(
        functools.partial(pack_kernel, owners, slot_count, held),
        in_specs=[pl.BlockSpec(memory_space=pl.ANY)] * 3,
        out_specs=[pl.BlockSpec(memory_space=pl.ANY)] * 3,
        out_shape=[
            jax.ShapeDtypeStruct((bins, width), hidden.dtype),
            jax.ShapeDtypeStruct((rows, bins), jnp.bfloat16),
            jax.ShapeDtypeStruct((1, bins), jnp.float32),
        ],
        scratch_shapes=[
            pltpu.VMEM(slots.shape, jnp.int32),
            pltpu.VMEM((1, rows), jnp.int32),
            pltpu.VMEM((rows, width), hidden.dtype),
            pltpu.VMEM((bins, width), hidden.dtype),
            pltpu.VMEM((rows, bins), jnp.bfloat16),
            pltpu.VMEM((1, bins), jnp.float32),
            pltpu.SemaphoreType.DMA((4,)),
            pltpu.SemaphoreType.DMA((steps,)),
            pltpu.SemaphoreType.DMA((steps,)),
        ],
        compiler_params=pltpu.CompilerParams(vmem_limit_bytes=56 * 2**20),
        name="pack",
    )(slots, adapter_id.reshape(1, rows), hidden)


def adapt_kernel(slot_count, arrived_ref, labels_ref, a_ref, b_ref, change_ref):
    width = a_ref.shape[0]
    bins = arrived_ref.shape[0]
    owners = labels_ref.shape[0]
    source = lax.broadcasted_iota(jnp.int32, (bins, owners), 0) // slot_count
    named = source == lax.broadcasted_iota(jnp.int32, (bins, owners), 1)
    labels = jnp.dot(
        named.astype(jnp.bfloat16),
        labels_ref[...].astype(jnp.bfloat16),
        preferred_element_type=jnp.float32,
    )
    line = lax.broadcasted_iota(jnp.int32, (bins, bins), 0)
    mine = lax.rem(line, slot_count) + lax.axis_index("owner") * slot_count
    mine = mine == lax.broadcasted_iota(jnp.int32, (bins, bins), 1)
    label = jnp.sum(jnp.where(mine, labels, 0.0), axis=1, keepdims=True).astype(jnp.int32)
    low = jnp.zeros((bins, a_ref.shape[1]), jnp.float32)
    for at in range(0, width, COLUMNS_STEP):
        low += jnp.dot(
            arrived_ref[:, at : at + COLUMNS_STEP],
            a_ref[at : at + COLUMNS_STEP, :],
            preferred_element_type=jnp.float32,
        )
    column = lax.broadcasted_iota(jnp.int32, low.shape, 1) // RANK
    low = jnp.where(column == label, low, 0.0).astype(jnp.bfloat16)
    out_width = b_ref.shape[1]
    piece = min(1024, out_width)
    for at in range(0, out_width, piece):
        change_ref[:, at : at + piece] = (
            SCALE * jnp.dot(low, b_ref[:, at : at + piece], preferred_element_type=jnp.float32)
        ).astype(change_ref.dtype)


def adapt(arrived, labels, a_maps, b_maps, slot_count):
    return pl.pallas_call(
        functools.partial(adapt_kernel, slot_count),
        in_specs=[pl.BlockSpec(memory_space=pltpu.VMEM)] * 4,
        out_specs=pl.BlockSpec(memory_space=pltpu.VMEM),
        out_shape=jax.ShapeDtypeStruct((arrived.shape[0], b_maps.shape[1]), jnp.bfloat16),
        compiler_params=pltpu.CompilerParams(vmem_limit_bytes=16 * 2**20),
        name="adapt",
    )(arrived, labels, a_maps, b_maps)


def tall(rows, group):
    return jnp.concatenate([rows[:, g * HEAD : (g + 1) * HEAD] for g in range(group)], axis=0)


def prep_kernel(group, base_ref, kv_ref, keys_ref, rest_ref):
    step, context = kv_ref.shape[0], kv_ref.shape[2]
    cells = step * context
    for k in range(KVH):
        head = slice(k * HEAD, (k + 1) * HEAD)
        keys = kv_ref[:, 0, :, head].astype(jnp.float32).reshape(cells, HEAD)
        keys_ref[k] = jnp.transpose(keys).astype(keys_ref.dtype)
        rest_ref[k, :cells] = kv_ref[:, 1, :, head].reshape(cells, HEAD)
        base = base_ref[:, k * group * HEAD : (k + 1) * group * HEAD].astype(jnp.float32)
        rest_ref[k, cells:] = tall(base, group).astype(rest_ref.dtype)


def prep(base_q, kv_cache):
    rows, width = base_q.shape
    context = kv_cache.shape[2]
    group = width // (KVH * HEAD)
    step = ROWS_STEP
    steps = rows // step
    cells = step * context
    lines = cells + group * step
    length = pl.cdiv(max(TALL_BYTES // (2 * KVH * HEAD), steps * lines), lines) * lines
    return pl.pallas_call(
        functools.partial(prep_kernel, group),
        grid=(steps,),
        in_specs=[
            pl.BlockSpec((step, width), lambda i: (i, 0)),
            pl.BlockSpec((step, *kv_cache.shape[1:]), lambda i: (i, 0, 0, 0)),
        ],
        out_specs=[
            pl.BlockSpec((KVH, HEAD, cells), lambda i: (0, 0, i)),
            pl.BlockSpec((KVH, lines, HEAD), lambda i: (0, i, 0)),
        ],
        out_shape=[
            jax.ShapeDtypeStruct((KVH, HEAD, rows * context), jnp.bfloat16),
            jax.ShapeDtypeStruct((KVH, length, HEAD), jnp.bfloat16),
        ],
        compiler_params=pltpu.CompilerParams(vmem_limit_bytes=60 * 2**20),
        name="prep",
    )(base_q, kv_cache)


def attend_kernel(
    group, context, routed_ref, returned_ref, keys_ref, lens_ref, rest_hbm, out_hbm, rest_ref, bias_ref, out_ref, sems
):
    step = ROWS_STEP
    steps, lines, cells = bias_ref.shape
    block = cells + lines
    span = group * HEAD
    factor = 1.0 / jnp.sqrt(jnp.float32(HEAD))
    loads = [
        pltpu.make_async_copy(
            rest_hbm.at[k, pl.ds(0, steps * block)], rest_ref.at[k], sems.at[k, 0]
        )
        for k in range(KVH)
    ]
    stores = [
        pltpu.make_async_copy(
            out_ref.at[:, pl.ds(k * span, span)], out_hbm.at[:, pl.ds(k * span, span)], sems.at[k, 1]
        )
        for k in range(KVH)
    ]
    for load in loads:
        load.start()
    lane = lax.broadcasted_iota(jnp.int32, (lines, cells), 1)
    line = lax.broadcasted_iota(jnp.int32, (lines, cells), 0)
    own = lax.div(lane, context) == lax.rem(line, step)
    position = lax.rem(lane, context)
    for i in range(steps):
        bias_ref[i] = jnp.where(own & (position < lens_ref[i]), 0.0, -jnp.inf)
    for k in range(KVH):
        delta = jnp.dot(
            routed_ref[...],
            returned_ref[:, k * span : (k + 1) * span],
            preferred_element_type=jnp.float32,
        )
        loads[k].wait()
        for i in range(steps):
            rows = slice(i * step, (i + 1) * step)
            keys = keys_ref[k, :, i * cells : (i + 1) * cells]
            values = rest_ref[k, i * block : i * block + cells, :]
            query = rest_ref[k, i * block + cells : (i + 1) * block, :]
            change = tall(delta[rows], group).astype(jnp.bfloat16)
            scores = jnp.dot(
                jnp.concatenate([query, change], axis=1),
                jnp.concatenate([keys, keys], axis=0),
                preferred_element_type=jnp.float32,
            )
            scores = scores * factor + bias_ref[i]
            expo = jnp.exp(scores - jnp.max(scores, axis=1, keepdims=True))
            probs = expo * (1.0 / jnp.sum(expo, axis=1, keepdims=True))
            out = jnp.dot(probs.astype(jnp.bfloat16), values, preferred_element_type=jnp.float32)
            for g in range(group):
                out_ref[rows, (k * group + g) * HEAD : (k * group + g + 1) * HEAD] = out[
                    g * step : (g + 1) * step
                ].astype(out_ref.dtype)
        stores[k].start()
    for store in stores:
        store.wait()


def attend(routed, returned, cache_len, keys, rest, context):
    rows, width = routed.shape[0], returned.shape[1]
    group = width // (KVH * HEAD)
    step = ROWS_STEP
    steps = rows // step
    cells = step * context
    lens = jnp.repeat(cache_len, context).reshape(steps, 1, cells)
    return pl.pallas_call(
        functools.partial(attend_kernel, group, context),
        in_specs=[pl.BlockSpec(memory_space=pltpu.VMEM)] * 4 + [pl.BlockSpec(memory_space=pl.ANY)],
        out_specs=pl.BlockSpec(memory_space=pl.ANY),
        out_shape=jax.ShapeDtypeStruct((rows, width), jnp.bfloat16),
        scratch_shapes=[
            pltpu.VMEM((KVH, steps * (cells + group * step), HEAD), rest.dtype),
            pltpu.VMEM((steps, group * step, cells), jnp.float32),
            pltpu.VMEM((rows, width), jnp.bfloat16),
            pltpu.SemaphoreType.DMA((KVH, 2)),
        ],
        compiler_params=pltpu.CompilerParams(vmem_limit_bytes=GRANT),
        name="attend",
    )(routed, returned, keys, lens, rest)


def on_device(hidden, adapter_id, adapter_slot, cache_len, base_q, kv_cache, a_maps, b_maps):
    owners = lax.axis_size("owner")
    rows = hidden.shape[0]
    held = a_maps.shape[1] // RANK
    slot_count = max(2, 2 * ((rows + 2 * owners - 1) // (2 * owners)))
    bins = owners * slot_count
    packed, routed, labels = pack(hidden, adapter_id, adapter_slot, owners, slot_count, held)
    packed = packed.reshape(owners, slot_count, packed.shape[1])
    arrived = lax.all_to_all(packed, "owner", split_axis=0, concat_axis=0, tiled=True)
    labels = lax.all_gather(labels, "owner", axis=0, tiled=True)
    keys, rest = prep(base_q, kv_cache)
    change = adapt(arrived.reshape(bins, arrived.shape[2]), labels, a_maps, b_maps, slot_count)
    change = change.reshape(owners, slot_count, change.shape[1])
    returned = lax.all_to_all(change, "owner", split_axis=0, concat_axis=0, tiled=True)
    returned = returned.reshape(bins, returned.shape[2])
    return attend(routed, returned, cache_len, keys, rest, kv_cache.shape[2])


def solution(mesh):
    return jax.shard_map(
        on_device,
        mesh=mesh,
        in_specs=(
            P(("groups", "owner"), None),
            P(("groups", "owner")),
            P("groups"),
            P(("groups", "owner")),
            P(("groups", "owner"), None),
            P(("groups", "owner"), None, None, None),
            P(None, "owner"),
            P("owner", None),
        ),
        out_specs=P(("groups", "owner"), None),
        check_vma=False,
    )
```

```python
import functools

import jax
import jax.numpy as jnp
from jax import lax
from jax.experimental import pallas as pl
from jax.experimental.pallas import tpu as pltpu
from jax.sharding import PartitionSpec as P

HEAD = 128
KVH = 4
RANK = 64
LANES = 128
SCALE = 2.0
ROWS_STEP = 8
COLUMNS_STEP = 1024
ADAPT_STEP = 1024
OUT_STEP = 1024
GRANT = 48 * 2**20
TALL_BYTES = 17 * 2**20


def routing(owners, slot_count, held, slots, ids):
    rows = ids.shape[1]
    named = lax.broadcasted_iota(jnp.int32, (slots.shape[1], rows), 0) == ids
    slot = jnp.dot(
        slots.astype(jnp.float32).astype(jnp.bfloat16),
        named.astype(jnp.bfloat16),
        preferred_element_type=jnp.float32,
    ).astype(jnp.int32)
    owner = lax.div(slot, held)
    local = slot - owner * held
    hits = owner == lax.broadcasted_iota(jnp.int32, (owners, rows), 0)
    earlier = lax.broadcasted_iota(jnp.int32, (rows, rows), 0) < lax.broadcasted_iota(
        jnp.int32, (rows, rows), 1
    )
    before = jnp.dot(
        hits.astype(jnp.bfloat16), earlier.astype(jnp.bfloat16), preferred_element_type=jnp.float32
    )
    place = jnp.sum(jnp.where(hits, before, 0.0), axis=0, keepdims=True).astype(jnp.int32)
    bins = owner * slot_count + place
    routed = bins == lax.broadcasted_iota(jnp.int32, (owners * slot_count, rows), 0)
    label = jnp.sum(jnp.where(routed, local.astype(jnp.float32), 0.0), axis=1, keepdims=True)
    return routed.astype(jnp.bfloat16), label


def pack_kernel(owners, slot_count, held, slots_hbm, ids_hbm, hidden_hbm, packed_hbm, routed_hbm, *scratch):
    slots_ref, ids_ref, rows_ref, bins_ref, routed_ref, small_sems, sems, out_sems = scratch
    width = rows_ref.shape[1]
    spans = [(at, min(COLUMNS_STEP, width - at)) for at in range(0, width, COLUMNS_STEP)]
    small = [
        pltpu.make_async_copy(slots_hbm, slots_ref, small_sems.at[0]),
        pltpu.make_async_copy(ids_hbm, ids_ref, small_sems.at[1]),
    ]
    loads = [
        pltpu.make_async_copy(
            hidden_hbm.at[:, pl.ds(at, size)], rows_ref.at[:, pl.ds(at, size)], sems.at[i]
        )
        for i, (at, size) in enumerate(spans)
    ]
    stores = [
        pltpu.make_async_copy(
            bins_ref.at[:, pl.ds(at, size)], packed_hbm.at[:, pl.ds(at, size)], out_sems.at[i]
        )
        for i, (at, size) in enumerate([*spans, (width, LANES)])
    ]
    routed_store = pltpu.make_async_copy(routed_ref, routed_hbm, small_sems.at[2])
    for copy in [*small, *loads]:
        copy.start()
    for copy in small:
        copy.wait()
    routed, label = routing(owners, slot_count, held, slots_ref[...], ids_ref[...])
    for load, store, (at, size) in zip(loads, stores, spans):
        load.wait()
        bins_ref[:, at : at + size] = jnp.dot(
            routed, rows_ref[:, at : at + size], preferred_element_type=jnp.float32
        ).astype(bins_ref.dtype)
        store.start()
        if at == 0:
            bins_ref[:, width:] = jnp.broadcast_to(label, (label.shape[0], LANES)).astype(
                bins_ref.dtype
            )
            stores[-1].start()
            routed_ref[...] = jnp.transpose(routed.astype(jnp.float32)).astype(routed_ref.dtype)
            routed_store.start()
    for store in stores:
        store.wait()
    routed_store.wait()


def pack(hidden, adapter_id, adapter_slot, owners, slot_count, held):
    rows, width = hidden.shape
    bins = owners * slot_count
    steps = pl.cdiv(width, COLUMNS_STEP)
    slots = adapter_slot.reshape(1, -1)
    return pl.pallas_call(
        functools.partial(pack_kernel, owners, slot_count, held),
        in_specs=[pl.BlockSpec(memory_space=pl.ANY)] * 3,
        out_specs=[pl.BlockSpec(memory_space=pl.ANY)] * 2,
        out_shape=[
            jax.ShapeDtypeStruct((bins, width + LANES), hidden.dtype),
            jax.ShapeDtypeStruct((rows, bins), jnp.bfloat16),
        ],
        scratch_shapes=[
            pltpu.VMEM(slots.shape, jnp.int32),
            pltpu.VMEM((1, rows), jnp.int32),
            pltpu.VMEM((rows, width), hidden.dtype),
            pltpu.VMEM((bins, width + LANES), hidden.dtype),
            pltpu.VMEM((rows, bins), jnp.bfloat16),
            pltpu.SemaphoreType.DMA((3,)),
            pltpu.SemaphoreType.DMA((steps,)),
            pltpu.SemaphoreType.DMA((steps + 1,)),
        ],
        compiler_params=pltpu.CompilerParams(vmem_limit_bytes=56 * 2**20),
        name="pack",
    )(slots, adapter_id.reshape(1, rows), hidden)


def adapt_kernel(arrived_hbm, a_ref, b_ref, _, change_hbm, arrived_ref, change_ref, sems, out_sems):
    width = a_ref.shape[0]
    spans = [(at, min(ADAPT_STEP, width - at)) for at in range(0, width, ADAPT_STEP)]
    spans[-1] = (spans[-1][0], spans[-1][1] + LANES)
    loads = [
        pltpu.make_async_copy(
            arrived_hbm.at[:, pl.ds(at, size)], arrived_ref.at[:, pl.ds(at, size)], sems.at[i]
        )
        for i, (at, size) in enumerate(spans)
    ]
    for load in loads:
        load.start()
    low = jnp.zeros((arrived_ref.shape[0], a_ref.shape[1]), jnp.float32)
    for load, (at, size) in zip(loads, spans):
        load.wait()
        end = min(at + size, width)
        low += jnp.dot(
            arrived_ref[:, at:end], a_ref[at:end, :], preferred_element_type=jnp.float32
        )
    label = arrived_ref[:, width:].astype(jnp.float32)[:, :1].astype(jnp.int32)
    column = lax.broadcasted_iota(jnp.int32, low.shape, 1) // RANK
    low = jnp.where(column == label, low, 0.0).astype(jnp.bfloat16)
    stores = []
    for i, at in enumerate(range(0, b_ref.shape[1], OUT_STEP)):
        span = pl.ds(at, OUT_STEP)
        change_ref[:, at : at + OUT_STEP] = (
            SCALE * jnp.dot(low, b_ref[:, at : at + OUT_STEP], preferred_element_type=jnp.float32)
        ).astype(change_ref.dtype)
        stores.append(
            pltpu.make_async_copy(change_ref.at[:, span], change_hbm.at[:, span], out_sems.at[i])
        )
        stores[-1].start()
    for store in stores:
        store.wait()


def adapt(arrived, a_maps, b_maps, after):
    change = jax.ShapeDtypeStruct((arrived.shape[0], b_maps.shape[1]), jnp.bfloat16)
    return pl.pallas_call(
        adapt_kernel,
        in_specs=[
            pl.BlockSpec(memory_space=pl.ANY),
            pl.BlockSpec(memory_space=pltpu.VMEM),
            pl.BlockSpec(memory_space=pltpu.VMEM),
            pl.BlockSpec(memory_space=pl.ANY),
        ],
        out_specs=pl.BlockSpec(memory_space=pl.ANY),
        out_shape=change,
        scratch_shapes=[
            pltpu.VMEM(arrived.shape, arrived.dtype),
            pltpu.VMEM(change.shape, change.dtype),
            pltpu.SemaphoreType.DMA((pl.cdiv(a_maps.shape[0], ADAPT_STEP),)),
            pltpu.SemaphoreType.DMA((pl.cdiv(b_maps.shape[1], OUT_STEP),)),
        ],
        compiler_params=pltpu.CompilerParams(vmem_limit_bytes=GRANT),
        name="adapt",
    )(arrived, a_maps, b_maps, after)


def tall(rows, group):
    return jnp.concatenate([rows[:, g * HEAD : (g + 1) * HEAD] for g in range(group)], axis=0)


def prep_kernel(group, base_ref, kv_ref, keys_ref, rest_ref):
    step, context = kv_ref.shape[0], kv_ref.shape[2]
    cells = step * context
    for k in range(KVH):
        head = slice(k * HEAD, (k + 1) * HEAD)
        keys = kv_ref[:, 0, :, head].astype(jnp.float32).reshape(cells, HEAD)
        keys_ref[k] = jnp.transpose(keys).astype(keys_ref.dtype)
        rest_ref[k, 0, :cells] = kv_ref[:, 1, :, head].reshape(cells, HEAD)
        base = base_ref[:, k * group * HEAD : (k + 1) * group * HEAD].astype(jnp.float32)
        rest_ref[k, 0, cells:] = tall(base, group).astype(rest_ref.dtype)


def prep(base_q, kv_cache):
    rows, width = base_q.shape
    context = kv_cache.shape[2]
    group = width // (KVH * HEAD)
    step = ROWS_STEP
    steps = rows // step
    cells = step * context
    lines = cells + group * step
    length = max(pl.cdiv(TALL_BYTES, 2 * KVH * lines * HEAD), steps)
    return pl.pallas_call(
        functools.partial(prep_kernel, group),
        grid=(steps,),
        in_specs=[
            pl.BlockSpec((step, width), lambda i: (i, 0)),
            pl.BlockSpec((step, *kv_cache.shape[1:]), lambda i: (i, 0, 0, 0)),
        ],
        out_specs=[
            pl.BlockSpec((KVH, HEAD, cells), lambda i: (0, 0, i)),
            pl.BlockSpec((KVH, 1, lines, HEAD), lambda i: (0, i, 0, 0)),
        ],
        out_shape=[
            jax.ShapeDtypeStruct((KVH, HEAD, rows * context), jnp.bfloat16),
            jax.ShapeDtypeStruct((KVH, length, lines, HEAD), jnp.bfloat16),
        ],
        compiler_params=pltpu.CompilerParams(vmem_limit_bytes=60 * 2**20),
        name="prep",
    )(base_q, kv_cache)


def attend_kernel(
    group, context, routed_ref, returned_ref, keys_ref, lens_ref, rest_hbm, out_hbm, *scratch
):
    query_ref, values_ref, bias_ref, out_ref, sems = scratch
    step = ROWS_STEP
    steps, lines, cells = bias_ref.shape
    span = group * HEAD
    factor = 1.0 / jnp.sqrt(jnp.float32(HEAD))
    loads = [
        [
            pltpu.make_async_copy(
                rest_hbm.at[k, pl.ds(0, steps), pl.ds(cells, lines)], query_ref.at[k], sems.at[k, 1]
            ),
            pltpu.make_async_copy(
                rest_hbm.at[k, pl.ds(0, steps), pl.ds(0, cells)], values_ref.at[k], sems.at[k, 2]
            ),
        ]
        for k in range(KVH)
    ]
    stores = [
        pltpu.make_async_copy(
            out_ref.at[:, pl.ds(k * span, span)], out_hbm.at[:, pl.ds(k * span, span)], sems.at[k, 0]
        )
        for k in range(KVH)
    ]
    for load in loads:
        for copy in load:
            copy.start()
    lane = lax.broadcasted_iota(jnp.int32, (lines, cells), 1)
    line = lax.broadcasted_iota(jnp.int32, (lines, cells), 0)
    own = lax.div(lane, context) == lax.rem(line, step)
    position = lax.rem(lane, context)
    for i in range(steps):
        bias_ref[i] = jnp.where(own & (position < lens_ref[i]), 0.0, -jnp.inf)
    for k in range(KVH):
        delta = jnp.dot(
            routed_ref[...],
            returned_ref[:, k * span : (k + 1) * span],
            preferred_element_type=jnp.float32,
        )
        for copy in loads[k]:
            copy.wait()
        for i in range(steps):
            rows = slice(i * step, (i + 1) * step)
            keys = keys_ref[k, :, i * cells : (i + 1) * cells]
            change = tall(delta[rows], group).astype(jnp.bfloat16)
            scores = jnp.dot(
                jnp.concatenate([query_ref[k, i], change], axis=1),
                jnp.concatenate([keys, keys], axis=0),
                preferred_element_type=jnp.float32,
            )
            scores = scores * factor + bias_ref[i]
            expo = jnp.exp(scores - jnp.max(scores, axis=1, keepdims=True))
            probs = expo * (1.0 / jnp.sum(expo, axis=1, keepdims=True))
            out = jnp.dot(
                probs.astype(jnp.bfloat16), values_ref[k, i], preferred_element_type=jnp.float32
            )
            for g in range(group):
                out_ref[rows, (k * group + g) * HEAD : (k * group + g + 1) * HEAD] = out[
                    g * step : (g + 1) * step
                ].astype(out_ref.dtype)
        stores[k].start()
    for store in stores:
        store.wait()


def attend(routed, returned, cache_len, keys, rest, context):
    rows, width = routed.shape[0], returned.shape[1]
    group = width // (KVH * HEAD)
    step = ROWS_STEP
    steps = rows // step
    cells = step * context
    lens = jnp.repeat(cache_len, context).reshape(steps, 1, cells)
    return pl.pallas_call(
        functools.partial(attend_kernel, group, context),
        in_specs=[pl.BlockSpec(memory_space=pltpu.VMEM)] * 4 + [pl.BlockSpec(memory_space=pl.ANY)],
        out_specs=pl.BlockSpec(memory_space=pl.ANY),
        out_shape=jax.ShapeDtypeStruct((rows, width), jnp.bfloat16),
        scratch_shapes=[
            pltpu.VMEM((KVH, steps, group * step, HEAD), rest.dtype),
            pltpu.VMEM((KVH, steps, cells, HEAD), rest.dtype),
            pltpu.VMEM((steps, group * step, cells), jnp.float32),
            pltpu.VMEM((rows, width), jnp.bfloat16),
            pltpu.SemaphoreType.DMA((KVH, 3)),
        ],
        compiler_params=pltpu.CompilerParams(vmem_limit_bytes=GRANT),
        name="attend",
    )(routed, returned, keys, lens, rest)


def on_device(hidden, adapter_id, adapter_slot, cache_len, base_q, kv_cache, a_maps, b_maps):
    owners = lax.axis_size("owner")
    rows = hidden.shape[0]
    held = a_maps.shape[1] // RANK
    slot_count = max(2, 2 * ((rows + 2 * owners - 1) // (2 * owners)))
    bins = owners * slot_count
    packed, routed = pack(hidden, adapter_id, adapter_slot, owners, slot_count, held)
    packed = packed.reshape(owners, slot_count, packed.shape[1])
    arrived = lax.all_to_all(packed, "owner", split_axis=0, concat_axis=0, tiled=True)
    keys, rest = prep(base_q, kv_cache)
    change = adapt(arrived.reshape(bins, arrived.shape[2]), a_maps, b_maps, rest)
    change = change.reshape(owners, slot_count, change.shape[1])
    returned = lax.all_to_all(change, "owner", split_axis=0, concat_axis=0, tiled=True)
    returned = returned.reshape(bins, returned.shape[2])
    return attend(routed, returned, cache_len, keys, rest, kv_cache.shape[2])


def solution(mesh):
    return jax.shard_map(
        on_device,
        mesh=mesh,
        in_specs=(
            P(("groups", "owner"), None),
            P(("groups", "owner")),
            P("groups"),
            P(("groups", "owner")),
            P(("groups", "owner"), None),
            P(("groups", "owner"), None, None, None),
            P(None, "owner"),
            P("owner", None),
        ),
        out_specs=P(("groups", "owner"), None),
        check_vma=False,
    )
```

```python
import functools

import jax
import jax.numpy as jnp
from jax import lax
from jax.experimental import pallas as pl
from jax.experimental.pallas import tpu as pltpu
from jax.sharding import PartitionSpec as P

HEAD = 128
KVH = 4
RANK = 64
LANES = 128
SCALE = 2.0
ROWS_STEP = 8
COLUMNS_STEP = 1024
ADAPT_STEP = 2048
GRANT = 48 * 2**20
TALL_BYTES = 17 * 2**20


def routing(owners, slot_count, held, slots, ids):
    rows = ids.shape[1]
    named = lax.broadcasted_iota(jnp.int32, (slots.shape[1], rows), 0) == ids
    slot = jnp.dot(
        slots.astype(jnp.float32).astype(jnp.bfloat16),
        named.astype(jnp.bfloat16),
        preferred_element_type=jnp.float32,
    ).astype(jnp.int32)
    owner = lax.div(slot, held)
    local = slot - owner * held
    hits = owner == lax.broadcasted_iota(jnp.int32, (owners, rows), 0)
    earlier = lax.broadcasted_iota(jnp.int32, (rows, rows), 0) < lax.broadcasted_iota(
        jnp.int32, (rows, rows), 1
    )
    before = jnp.dot(
        hits.astype(jnp.bfloat16), earlier.astype(jnp.bfloat16), preferred_element_type=jnp.float32
    )
    place = jnp.sum(jnp.where(hits, before, 0.0), axis=0, keepdims=True).astype(jnp.int32)
    bins = owner * slot_count + place
    routed = bins == lax.broadcasted_iota(jnp.int32, (owners * slot_count, rows), 0)
    label = jnp.sum(jnp.where(routed, local.astype(jnp.float32), 0.0), axis=1, keepdims=True)
    return routed.astype(jnp.bfloat16), label


def pack_kernel(owners, slot_count, held, slots_hbm, ids_hbm, hidden_hbm, packed_hbm, routed_hbm, *scratch):
    slots_ref, ids_ref, rows_ref, bins_ref, routed_ref, small_sems, sems, out_sems = scratch
    width = rows_ref.shape[1]
    spans = [(at, min(COLUMNS_STEP, width - at)) for at in range(0, width, COLUMNS_STEP)]
    small = [
        pltpu.make_async_copy(slots_hbm, slots_ref, small_sems.at[0]),
        pltpu.make_async_copy(ids_hbm, ids_ref, small_sems.at[1]),
    ]
    loads = [
        pltpu.make_async_copy(
            hidden_hbm.at[:, pl.ds(at, size)], rows_ref.at[:, pl.ds(at, size)], sems.at[i]
        )
        for i, (at, size) in enumerate(spans)
    ]
    stores = [
        pltpu.make_async_copy(
            bins_ref.at[:, pl.ds(at, size)], packed_hbm.at[:, pl.ds(at, size)], out_sems.at[i]
        )
        for i, (at, size) in enumerate([*spans, (width, LANES)])
    ]
    routed_store = pltpu.make_async_copy(routed_ref, routed_hbm, small_sems.at[2])
    for copy in [*small, *loads]:
        copy.start()
    for copy in small:
        copy.wait()
    routed, label = routing(owners, slot_count, held, slots_ref[...], ids_ref[...])
    for load, store, (at, size) in zip(loads, stores, spans):
        load.wait()
        bins_ref[:, at : at + size] = jnp.dot(
            routed, rows_ref[:, at : at + size], preferred_element_type=jnp.float32
        ).astype(bins_ref.dtype)
        store.start()
        if at == 0:
            bins_ref[:, width:] = jnp.broadcast_to(label, (label.shape[0], LANES)).astype(
                bins_ref.dtype
            )
            stores[-1].start()
            routed_ref[...] = jnp.transpose(routed.astype(jnp.float32)).astype(routed_ref.dtype)
            routed_store.start()
    for store in stores:
        store.wait()
    routed_store.wait()


def pack(hidden, adapter_id, adapter_slot, owners, slot_count, held):
    rows, width = hidden.shape
    bins = owners * slot_count
    steps = pl.cdiv(width, COLUMNS_STEP)
    slots = adapter_slot.reshape(1, -1)
    return pl.pallas_call(
        functools.partial(pack_kernel, owners, slot_count, held),
        in_specs=[pl.BlockSpec(memory_space=pl.ANY)] * 3,
        out_specs=[pl.BlockSpec(memory_space=pl.ANY)] * 2,
        out_shape=[
            jax.ShapeDtypeStruct((bins, width + LANES), hidden.dtype),
            jax.ShapeDtypeStruct((rows, bins), jnp.bfloat16),
        ],
        scratch_shapes=[
            pltpu.VMEM(slots.shape, jnp.int32),
            pltpu.VMEM((1, rows), jnp.int32),
            pltpu.VMEM((rows, width), hidden.dtype),
            pltpu.VMEM((bins, width + LANES), hidden.dtype),
            pltpu.VMEM((rows, bins), jnp.bfloat16),
            pltpu.SemaphoreType.DMA((3,)),
            pltpu.SemaphoreType.DMA((steps,)),
            pltpu.SemaphoreType.DMA((steps + 1,)),
        ],
        compiler_params=pltpu.CompilerParams(vmem_limit_bytes=56 * 2**20),
        name="pack",
    )(slots, adapter_id.reshape(1, rows), hidden)


def adapt_kernel(arrived_ref, a_ref, b_ref, change_ref):
    width = a_ref.shape[0]
    low = jnp.zeros((arrived_ref.shape[0], a_ref.shape[1]), jnp.float32)
    for at in range(0, width, ADAPT_STEP):
        low += jnp.dot(
            arrived_ref[:, at : at + ADAPT_STEP],
            a_ref[at : at + ADAPT_STEP, :],
            preferred_element_type=jnp.float32,
        )
    label = arrived_ref[:, width:].astype(jnp.float32)[:, :1].astype(jnp.int32)
    column = lax.broadcasted_iota(jnp.int32, low.shape, 1) // RANK
    low = jnp.where(column == label, low, 0.0).astype(jnp.bfloat16)
    out_width = b_ref.shape[1]
    piece = min(1024, out_width)
    for at in range(0, out_width, piece):
        change_ref[:, at : at + piece] = (
            SCALE * jnp.dot(low, b_ref[:, at : at + piece], preferred_element_type=jnp.float32)
        ).astype(change_ref.dtype)


def adapt(arrived, a_maps, b_maps):
    return pl.pallas_call(
        adapt_kernel,
        in_specs=[pl.BlockSpec(memory_space=pltpu.VMEM)] * 3,
        out_specs=pl.BlockSpec(memory_space=pltpu.VMEM),
        out_shape=jax.ShapeDtypeStruct((arrived.shape[0], b_maps.shape[1]), jnp.bfloat16),
        compiler_params=pltpu.CompilerParams(vmem_limit_bytes=16 * 2**20),
        name="adapt",
    )(arrived, a_maps, b_maps)


def tall(rows, group):
    return jnp.concatenate([rows[:, g * HEAD : (g + 1) * HEAD] for g in range(group)], axis=0)


def prep_kernel(group, base_ref, kv_ref, keys_ref, rest_ref):
    step, context = kv_ref.shape[0], kv_ref.shape[2]
    cells = step * context
    for k in range(KVH):
        head = slice(k * HEAD, (k + 1) * HEAD)
        keys = kv_ref[:, 0, :, head].astype(jnp.float32).reshape(cells, HEAD)
        keys_ref[k] = jnp.transpose(keys).astype(keys_ref.dtype)
        rest_ref[k, 0, :cells] = kv_ref[:, 1, :, head].reshape(cells, HEAD)
        base = base_ref[:, k * group * HEAD : (k + 1) * group * HEAD].astype(jnp.float32)
        rest_ref[k, 0, cells:] = tall(base, group).astype(rest_ref.dtype)


def prep(base_q, kv_cache):
    rows, width = base_q.shape
    context = kv_cache.shape[2]
    group = width // (KVH * HEAD)
    step = ROWS_STEP
    steps = rows // step
    cells = step * context
    lines = cells + group * step
    length = max(pl.cdiv(TALL_BYTES, 2 * KVH * lines * HEAD), steps)
    return pl.pallas_call(
        functools.partial(prep_kernel, group),
        grid=(steps,),
        in_specs=[
            pl.BlockSpec((step, width), lambda i: (i, 0)),
            pl.BlockSpec((step, *kv_cache.shape[1:]), lambda i: (i, 0, 0, 0)),
        ],
        out_specs=[
            pl.BlockSpec((KVH, HEAD, cells), lambda i: (0, 0, i)),
            pl.BlockSpec((KVH, 1, lines, HEAD), lambda i: (0, i, 0, 0)),
        ],
        out_shape=[
            jax.ShapeDtypeStruct((KVH, HEAD, rows * context), jnp.bfloat16),
            jax.ShapeDtypeStruct((KVH, length, lines, HEAD), jnp.bfloat16),
        ],
        compiler_params=pltpu.CompilerParams(vmem_limit_bytes=GRANT),
        name="prep",
    )(base_q, kv_cache)


def attend_kernel(
    group, context, routed_ref, returned_ref, keys_ref, lens_ref, rest_hbm, out_hbm, *scratch
):
    query_ref, values_ref, bias_ref, scores_ref, probs_ref, out_ref, sems = scratch
    step = ROWS_STEP
    steps, lines, cells = bias_ref.shape
    span = group * HEAD
    factor = 1.0 / jnp.sqrt(jnp.float32(HEAD))
    loads = [
        [
            pltpu.make_async_copy(
                rest_hbm.at[k, pl.ds(0, steps), pl.ds(cells, lines)], query_ref.at[k], sems.at[k, 1]
            ),
            pltpu.make_async_copy(
                rest_hbm.at[k, pl.ds(0, steps), pl.ds(0, cells)], values_ref.at[k], sems.at[k, 2]
            ),
        ]
        for k in range(KVH)
    ]
    stores = [
        pltpu.make_async_copy(
            out_ref.at[:, pl.ds(k * span, span)], out_hbm.at[:, pl.ds(k * span, span)], sems.at[k, 0]
        )
        for k in range(KVH)
    ]
    for load in loads:
        for copy in load:
            copy.start()
    lane = lax.broadcasted_iota(jnp.int32, (lines, cells), 1)
    line = lax.broadcasted_iota(jnp.int32, (lines, cells), 0)
    own = lax.div(lane, context) == lax.rem(line, step)
    position = lax.rem(lane, context)
    for i in range(steps):
        bias_ref[i] = jnp.where(own & (position < lens_ref[i]), 0.0, -jnp.inf)
    for k in range(KVH):
        delta = jnp.dot(
            routed_ref[...],
            returned_ref[:, k * span : (k + 1) * span],
            preferred_element_type=jnp.float32,
        )
        for copy in loads[k]:
            copy.wait()
        for i in range(steps):
            keys = keys_ref[k, :, i * cells : (i + 1) * cells]
            change = tall(delta[i * step : (i + 1) * step], group).astype(jnp.bfloat16)
            scores = jnp.dot(
                jnp.concatenate([query_ref[k, i], change], axis=1),
                jnp.concatenate([keys, keys], axis=0),
                preferred_element_type=jnp.float32,
            )
            scores_ref[k, i] = scores * factor + bias_ref[i]
        for i in range(steps):
            scores = scores_ref[k, i]
            expo = jnp.exp(scores - jnp.max(scores, axis=1, keepdims=True))
            probs = expo * (1.0 / jnp.sum(expo, axis=1, keepdims=True))
            probs_ref[k, i] = probs.astype(probs_ref.dtype)
        for i in range(steps):
            rows = slice(i * step, (i + 1) * step)
            out = jnp.dot(probs_ref[k, i], values_ref[k, i], preferred_element_type=jnp.float32)
            for g in range(group):
                out_ref[rows, (k * group + g) * HEAD : (k * group + g + 1) * HEAD] = out[
                    g * step : (g + 1) * step
                ].astype(out_ref.dtype)
        stores[k].start()
    for store in stores:
        store.wait()


def attend(routed, returned, cache_len, keys, rest, context):
    rows, width = routed.shape[0], returned.shape[1]
    group = width // (KVH * HEAD)
    step = ROWS_STEP
    steps = rows // step
    cells = step * context
    lens = jnp.repeat(cache_len, context).reshape(steps, 1, cells)
    return pl.pallas_call(
        functools.partial(attend_kernel, group, context),
        in_specs=[pl.BlockSpec(memory_space=pltpu.VMEM)] * 4 + [pl.BlockSpec(memory_space=pl.ANY)],
        out_specs=pl.BlockSpec(memory_space=pl.ANY),
        out_shape=jax.ShapeDtypeStruct((rows, width), jnp.bfloat16),
        scratch_shapes=[
            pltpu.VMEM((KVH, steps, group * step, HEAD), rest.dtype),
            pltpu.VMEM((KVH, steps, cells, HEAD), rest.dtype),
            pltpu.VMEM((steps, group * step, cells), jnp.float32),
            pltpu.VMEM((KVH, steps, group * step, cells), jnp.float32),
            pltpu.VMEM((KVH, steps, group * step, cells), jnp.bfloat16),
            pltpu.VMEM((rows, width), jnp.bfloat16),
            pltpu.SemaphoreType.DMA((KVH, 3)),
        ],
        compiler_params=pltpu.CompilerParams(vmem_limit_bytes=GRANT),
        name="attend",
    )(routed, returned, keys, lens, rest)


def on_device(hidden, adapter_id, adapter_slot, cache_len, base_q, kv_cache, a_maps, b_maps):
    owners = lax.axis_size("owner")
    rows = hidden.shape[0]
    held = a_maps.shape[1] // RANK
    slot_count = max(2, 2 * ((rows + 2 * owners - 1) // (2 * owners)))
    bins = owners * slot_count
    packed, routed = pack(hidden, adapter_id, adapter_slot, owners, slot_count, held)
    packed = packed.reshape(owners, slot_count, packed.shape[1])
    arrived = lax.all_to_all(packed, "owner", split_axis=0, concat_axis=0, tiled=True)
    keys, rest = prep(base_q, kv_cache)
    change = adapt(arrived.reshape(bins, arrived.shape[2]), a_maps, b_maps)
    change = change.reshape(owners, slot_count, change.shape[1])
    returned = lax.all_to_all(change, "owner", split_axis=0, concat_axis=0, tiled=True)
    returned = returned.reshape(bins, returned.shape[2])
    return attend(routed, returned, cache_len, keys, rest, kv_cache.shape[2])


def solution(mesh):
    return jax.shard_map(
        on_device,
        mesh=mesh,
        in_specs=(
            P(("groups", "owner"), None),
            P(("groups", "owner")),
            P("groups"),
            P(("groups", "owner")),
            P(("groups", "owner"), None),
            P(("groups", "owner"), None, None, None),
            P(None, "owner"),
            P("owner", None),
        ),
        out_specs=P(("groups", "owner"), None),
        check_vma=False,
    )
```

```python
import functools

import jax
import jax.numpy as jnp
from jax import lax
from jax.experimental import pallas as pl
from jax.experimental.pallas import tpu as pltpu
from jax.sharding import PartitionSpec as P

HEAD = 128
KVH = 4
RANK = 64
LANES = 128
SCALE = 2.0
ROWS_STEP = 8
COLUMNS_STEP = 1024
ADAPT_STEP = 2048
GRANT = 48 * 2**20
TALL_BYTES = 17 * 2**20


def routing(owners, slot_count, held, slots, ids):
    rows = ids.shape[1]
    named = lax.broadcasted_iota(jnp.int32, (slots.shape[1], rows), 0) == ids
    slot = jnp.dot(
        slots.astype(jnp.float32).astype(jnp.bfloat16),
        named.astype(jnp.bfloat16),
        preferred_element_type=jnp.float32,
    ).astype(jnp.int32)
    owner = lax.div(slot, held)
    local = slot - owner * held
    hits = owner == lax.broadcasted_iota(jnp.int32, (owners, rows), 0)
    earlier = lax.broadcasted_iota(jnp.int32, (rows, rows), 0) < lax.broadcasted_iota(
        jnp.int32, (rows, rows), 1
    )
    before = jnp.dot(
        hits.astype(jnp.bfloat16), earlier.astype(jnp.bfloat16), preferred_element_type=jnp.float32
    )
    place = jnp.sum(jnp.where(hits, before, 0.0), axis=0, keepdims=True).astype(jnp.int32)
    bins = owner * slot_count + place
    routed = bins == lax.broadcasted_iota(jnp.int32, (owners * slot_count, rows), 0)
    label = jnp.sum(jnp.where(routed, local.astype(jnp.float32), 0.0), axis=1, keepdims=True)
    return routed.astype(jnp.bfloat16), label


def pack_kernel(owners, slot_count, held, slots_hbm, ids_hbm, hidden_hbm, packed_hbm, routed_hbm, *scratch):
    slots_ref, ids_ref, rows_ref, bins_ref, routed_ref, small_sems, sems, out_sems = scratch
    width = rows_ref.shape[1]
    spans = [(at, min(COLUMNS_STEP, width - at)) for at in range(0, width, COLUMNS_STEP)]
    small = [
        pltpu.make_async_copy(slots_hbm, slots_ref, small_sems.at[0]),
        pltpu.make_async_copy(ids_hbm, ids_ref, small_sems.at[1]),
    ]
    loads = [
        pltpu.make_async_copy(
            hidden_hbm.at[:, pl.ds(at, size)], rows_ref.at[:, pl.ds(at, size)], sems.at[i]
        )
        for i, (at, size) in enumerate(spans)
    ]
    stores = [
        pltpu.make_async_copy(
            bins_ref.at[:, pl.ds(at, size)], packed_hbm.at[:, pl.ds(at, size)], out_sems.at[i]
        )
        for i, (at, size) in enumerate([*spans, (width, LANES)])
    ]
    routed_store = pltpu.make_async_copy(routed_ref, routed_hbm, small_sems.at[2])
    for copy in [*small, *loads]:
        copy.start()
    for copy in small:
        copy.wait()
    routed, label = routing(owners, slot_count, held, slots_ref[...], ids_ref[...])
    for load, store, (at, size) in zip(loads, stores, spans):
        load.wait()
        bins_ref[:, at : at + size] = jnp.dot(
            routed, rows_ref[:, at : at + size], preferred_element_type=jnp.float32
        ).astype(bins_ref.dtype)
        store.start()
        if at == 0:
            bins_ref[:, width:] = jnp.broadcast_to(label, (label.shape[0], LANES)).astype(
                bins_ref.dtype
            )
            stores[-1].start()
            routed_ref[...] = jnp.transpose(routed.astype(jnp.float32)).astype(routed_ref.dtype)
            routed_store.start()
    for store in stores:
        store.wait()
    routed_store.wait()


def pack(hidden, adapter_id, adapter_slot, owners, slot_count, held):
    rows, width = hidden.shape
    bins = owners * slot_count
    steps = pl.cdiv(width, COLUMNS_STEP)
    slots = adapter_slot.reshape(1, -1)
    return pl.pallas_call(
        functools.partial(pack_kernel, owners, slot_count, held),
        in_specs=[pl.BlockSpec(memory_space=pl.ANY)] * 3,
        out_specs=[pl.BlockSpec(memory_space=pl.ANY)] * 2,
        out_shape=[
            jax.ShapeDtypeStruct((bins, width + LANES), hidden.dtype),
            jax.ShapeDtypeStruct((rows, bins), jnp.bfloat16),
        ],
        scratch_shapes=[
            pltpu.VMEM(slots.shape, jnp.int32),
            pltpu.VMEM((1, rows), jnp.int32),
            pltpu.VMEM((rows, width), hidden.dtype),
            pltpu.VMEM((bins, width + LANES), hidden.dtype),
            pltpu.VMEM((rows, bins), jnp.bfloat16),
            pltpu.SemaphoreType.DMA((3,)),
            pltpu.SemaphoreType.DMA((steps,)),
            pltpu.SemaphoreType.DMA((steps + 1,)),
        ],
        compiler_params=pltpu.CompilerParams(vmem_limit_bytes=56 * 2**20),
        name="pack",
    )(slots, adapter_id.reshape(1, rows), hidden)


def adapt_kernel(arrived_ref, a_ref, b_ref, change_ref):
    width = a_ref.shape[0]
    low = jnp.zeros((arrived_ref.shape[0], a_ref.shape[1]), jnp.float32)
    for at in range(0, width, ADAPT_STEP):
        low += jnp.dot(
            arrived_ref[:, at : at + ADAPT_STEP],
            a_ref[at : at + ADAPT_STEP, :],
            preferred_element_type=jnp.float32,
        )
    label = arrived_ref[:, width:].astype(jnp.float32)[:, :1].astype(jnp.int32)
    column = lax.broadcasted_iota(jnp.int32, low.shape, 1) // RANK
    low = jnp.where(column == label, low, 0.0).astype(jnp.bfloat16)
    out_width = b_ref.shape[1]
    piece = min(1024, out_width)
    for at in range(0, out_width, piece):
        change_ref[:, at : at + piece] = (
            SCALE * jnp.dot(low, b_ref[:, at : at + piece], preferred_element_type=jnp.float32)
        ).astype(change_ref.dtype)


def adapt(arrived, a_maps, b_maps):
    return pl.pallas_call(
        adapt_kernel,
        in_specs=[pl.BlockSpec(memory_space=pltpu.VMEM)] * 3,
        out_specs=pl.BlockSpec(memory_space=pltpu.VMEM),
        out_shape=jax.ShapeDtypeStruct((arrived.shape[0], b_maps.shape[1]), jnp.bfloat16),
        compiler_params=pltpu.CompilerParams(vmem_limit_bytes=16 * 2**20),
        name="adapt",
    )(arrived, a_maps, b_maps)


def tall(rows, group):
    return jnp.concatenate([rows[:, g * HEAD : (g + 1) * HEAD] for g in range(group)], axis=0)


def prep_kernel(group, base_ref, kv_ref, keys_ref, query_ref, rest_ref):
    step, context = kv_ref.shape[0], kv_ref.shape[2]
    cells = step * context
    for k in range(KVH):
        head = slice(k * HEAD, (k + 1) * HEAD)
        keys = kv_ref[:, 0, :, head].astype(jnp.float32).reshape(cells, HEAD)
        keys = jnp.transpose(keys).astype(keys_ref.dtype)
        base = base_ref[:, k * group * HEAD : (k + 1) * group * HEAD].astype(jnp.float32)
        query = tall(base, group).astype(query_ref.dtype)
        if k == 0:
            keys_ref[0] = keys
            query_ref[0] = query
        rest_ref[k, 0, :cells] = kv_ref[:, 1, :, head].reshape(cells, HEAD)
        rest_ref[k, 0, cells : cells + HEAD] = keys
        rest_ref[k, 0, cells + HEAD :] = query


def prep(base_q, kv_cache):
    rows, width = base_q.shape
    context = kv_cache.shape[2]
    group = width // (KVH * HEAD)
    step = ROWS_STEP
    steps = rows // step
    cells = step * context
    lines = group * step
    block = cells + HEAD + lines
    length = max(pl.cdiv(TALL_BYTES, 2 * KVH * block * HEAD), steps)
    return pl.pallas_call(
        functools.partial(prep_kernel, group),
        grid=(steps,),
        in_specs=[
            pl.BlockSpec((step, width), lambda i: (i, 0)),
            pl.BlockSpec((step, *kv_cache.shape[1:]), lambda i: (i, 0, 0, 0)),
        ],
        out_specs=[
            pl.BlockSpec((1, HEAD, cells), lambda i: (i, 0, 0)),
            pl.BlockSpec((1, lines, HEAD), lambda i: (i, 0, 0)),
            pl.BlockSpec((KVH, 1, block, HEAD), lambda i: (0, i, 0, 0)),
        ],
        out_shape=[
            jax.ShapeDtypeStruct((steps, HEAD, cells), jnp.bfloat16),
            jax.ShapeDtypeStruct((steps, lines, HEAD), jnp.bfloat16),
            jax.ShapeDtypeStruct((KVH, length, block, HEAD), jnp.bfloat16),
        ],
        compiler_params=pltpu.CompilerParams(vmem_limit_bytes=GRANT),
        name="prep",
    )(base_q, kv_cache)


def attend_kernel(
    group, context, routed_ref, returned_ref, keys_ref, query_ref, lens_ref, rest_hbm, out_hbm, *scratch
):
    values_ref, later_ref, bias_ref, scores_ref, probs_ref, out_ref, sems = scratch
    step = ROWS_STEP
    steps, lines, cells = bias_ref.shape
    span = group * HEAD
    factor = 1.0 / jnp.sqrt(jnp.float32(HEAD))
    values_loads = [
        pltpu.make_async_copy(
            rest_hbm.at[k, pl.ds(0, steps), pl.ds(0, cells)], values_ref.at[k], sems.at[k, 1]
        )
        for k in range(KVH)
    ]
    later_loads = [
        pltpu.make_async_copy(
            rest_hbm.at[k, pl.ds(0, steps), pl.ds(cells, HEAD + lines)],
            later_ref.at[k - 1],
            sems.at[k, 2],
        )
        for k in range(1, KVH)
    ]
    stores = [
        pltpu.make_async_copy(
            out_ref.at[:, pl.ds(k * span, span)], out_hbm.at[:, pl.ds(k * span, span)], sems.at[k, 0]
        )
        for k in range(KVH)
    ]
    for k in range(KVH):
        values_loads[k].start()
        if k < KVH - 1:
            later_loads[k].start()
    lane = lax.broadcasted_iota(jnp.int32, (lines, cells), 1)
    line = lax.broadcasted_iota(jnp.int32, (lines, cells), 0)
    own = lax.div(lane, context) == lax.rem(line, step)
    position = lax.rem(lane, context)
    for i in range(steps):
        bias_ref[i] = jnp.where(own & (position < lens_ref[i]), 0.0, -jnp.inf)
    for k in range(KVH):
        delta = jnp.dot(
            routed_ref[...],
            returned_ref[:, k * span : (k + 1) * span],
            preferred_element_type=jnp.float32,
        )
        if k > 0:
            later_loads[k - 1].wait()
        for i in range(steps):
            keys = keys_ref[i] if k == 0 else later_ref[k - 1, i, :HEAD]
            query = query_ref[i] if k == 0 else later_ref[k - 1, i, HEAD:]
            change = tall(delta[i * step : (i + 1) * step], group).astype(jnp.bfloat16)
            scores = jnp.dot(
                jnp.concatenate([query, change], axis=1),
                jnp.concatenate([keys, keys], axis=0),
                preferred_element_type=jnp.float32,
            )
            scores_ref[k, i] = scores * factor + bias_ref[i]
        for i in range(steps):
            scores = scores_ref[k, i]
            expo = jnp.exp(scores - jnp.max(scores, axis=1, keepdims=True))
            probs = expo * (1.0 / jnp.sum(expo, axis=1, keepdims=True))
            probs_ref[k, i] = probs.astype(probs_ref.dtype)
        values_loads[k].wait()
        for i in range(steps):
            rows = slice(i * step, (i + 1) * step)
            out = jnp.dot(probs_ref[k, i], values_ref[k, i], preferred_element_type=jnp.float32)
            for g in range(group):
                out_ref[rows, (k * group + g) * HEAD : (k * group + g + 1) * HEAD] = out[
                    g * step : (g + 1) * step
                ].astype(out_ref.dtype)
        stores[k].start()
    for store in stores:
        store.wait()


def attend(routed, returned, cache_len, keys, query, rest, context):
    rows, width = routed.shape[0], returned.shape[1]
    group = width // (KVH * HEAD)
    step = ROWS_STEP
    steps = rows // step
    cells = step * context
    lens = jnp.repeat(cache_len, context).reshape(steps, 1, cells)
    return pl.pallas_call(
        functools.partial(attend_kernel, group, context),
        in_specs=[pl.BlockSpec(memory_space=pltpu.VMEM)] * 5 + [pl.BlockSpec(memory_space=pl.ANY)],
        out_specs=pl.BlockSpec(memory_space=pl.ANY),
        out_shape=jax.ShapeDtypeStruct((rows, width), jnp.bfloat16),
        scratch_shapes=[
            pltpu.VMEM((KVH, steps, cells, HEAD), rest.dtype),
            pltpu.VMEM((KVH - 1, steps, HEAD + group * step, HEAD), rest.dtype),
            pltpu.VMEM((steps, group * step, cells), jnp.float32),
            pltpu.VMEM((KVH, steps, group * step, cells), jnp.float32),
            pltpu.VMEM((KVH, steps, group * step, cells), jnp.bfloat16),
            pltpu.VMEM((rows, width), jnp.bfloat16),
            pltpu.SemaphoreType.DMA((KVH, 3)),
        ],
        compiler_params=pltpu.CompilerParams(vmem_limit_bytes=GRANT),
        name="attend",
    )(routed, returned, keys, query, lens, rest)


def on_device(hidden, adapter_id, adapter_slot, cache_len, base_q, kv_cache, a_maps, b_maps):
    owners = lax.axis_size("owner")
    rows = hidden.shape[0]
    held = a_maps.shape[1] // RANK
    slot_count = max(2, 2 * ((rows + 2 * owners - 1) // (2 * owners)))
    bins = owners * slot_count
    packed, routed = pack(hidden, adapter_id, adapter_slot, owners, slot_count, held)
    packed = packed.reshape(owners, slot_count, packed.shape[1])
    arrived = lax.all_to_all(packed, "owner", split_axis=0, concat_axis=0, tiled=True)
    keys, query, rest = prep(base_q, kv_cache)
    change = adapt(arrived.reshape(bins, arrived.shape[2]), a_maps, b_maps)
    change = change.reshape(owners, slot_count, change.shape[1])
    returned = lax.all_to_all(change, "owner", split_axis=0, concat_axis=0, tiled=True)
    returned = returned.reshape(bins, returned.shape[2])
    return attend(routed, returned, cache_len, keys, query, rest, kv_cache.shape[2])


def solution(mesh):
    return jax.shard_map(
        on_device,
        mesh=mesh,
        in_specs=(
            P(("groups", "owner"), None),
            P(("groups", "owner")),
            P("groups"),
            P(("groups", "owner")),
            P(("groups", "owner"), None),
            P(("groups", "owner"), None, None, None),
            P(None, "owner"),
            P("owner", None),
        ),
        out_specs=P(("groups", "owner"), None),
        check_vma=False,
    )
```

```python
import functools

import jax
import jax.numpy as jnp
from jax import lax
from jax.experimental import pallas as pl
from jax.experimental.pallas import tpu as pltpu
from jax.sharding import PartitionSpec as P

HEAD = 128
KVH = 4
RANK = 64
LANES = 128
SCALE = 2.0
ROWS_STEP = 8
COLUMNS_STEP = 1024
ADAPT_STEP = 2048
OUT_STEP = 1024
GRANT = 48 * 2**20
LOG2E = 1.4426950408889634
TALL_BYTES = 17 * 2**20


def routing(owners, slot_count, held, slots, ids):
    rows = ids.shape[1]
    named = lax.broadcasted_iota(jnp.int32, (slots.shape[1], rows), 0) == ids
    slot = jnp.dot(
        slots.astype(jnp.float32).astype(jnp.bfloat16),
        named.astype(jnp.bfloat16),
        preferred_element_type=jnp.float32,
    ).astype(jnp.int32)
    owner = lax.div(slot, held)
    local = slot - owner * held
    hits = owner == lax.broadcasted_iota(jnp.int32, (owners, rows), 0)
    earlier = lax.broadcasted_iota(jnp.int32, (rows, rows), 0) < lax.broadcasted_iota(
        jnp.int32, (rows, rows), 1
    )
    before = jnp.dot(
        hits.astype(jnp.bfloat16), earlier.astype(jnp.bfloat16), preferred_element_type=jnp.float32
    )
    place = jnp.sum(jnp.where(hits, before, 0.0), axis=0, keepdims=True).astype(jnp.int32)
    bins = owner * slot_count + place
    routed = bins == lax.broadcasted_iota(jnp.int32, (owners * slot_count, rows), 0)
    label = jnp.sum(jnp.where(routed, local.astype(jnp.float32), 0.0), axis=1, keepdims=True)
    return routed.astype(jnp.bfloat16), label


def pack_kernel(owners, slot_count, held, slots_hbm, ids_hbm, hidden_hbm, packed_hbm, routed_hbm, *scratch):
    slots_ref, ids_ref, rows_ref, bins_ref, routed_ref, small_sems, sems, out_sems = scratch
    width = rows_ref.shape[1]
    spans = [(at, min(COLUMNS_STEP, width - at)) for at in range(0, width, COLUMNS_STEP)]
    small = [
        pltpu.make_async_copy(slots_hbm, slots_ref, small_sems.at[0]),
        pltpu.make_async_copy(ids_hbm, ids_ref, small_sems.at[1]),
    ]
    loads = [
        pltpu.make_async_copy(
            hidden_hbm.at[:, pl.ds(at, size)], rows_ref.at[:, pl.ds(at, size)], sems.at[i]
        )
        for i, (at, size) in enumerate(spans)
    ]
    stores = [
        pltpu.make_async_copy(
            bins_ref.at[:, pl.ds(at, size)], packed_hbm.at[:, pl.ds(at, size)], out_sems.at[i]
        )
        for i, (at, size) in enumerate([*spans, (width, LANES)])
    ]
    routed_store = pltpu.make_async_copy(routed_ref, routed_hbm, small_sems.at[2])
    for copy in [*small, *loads]:
        copy.start()
    for copy in small:
        copy.wait()
    routed, label = routing(owners, slot_count, held, slots_ref[...], ids_ref[...])
    for load, store, (at, size) in zip(loads, stores, spans):
        load.wait()
        bins_ref[:, at : at + size] = jnp.dot(
            routed, rows_ref[:, at : at + size], preferred_element_type=jnp.float32
        ).astype(bins_ref.dtype)
        store.start()
        if at == 0:
            bins_ref[:, width:] = jnp.broadcast_to(label, (label.shape[0], LANES)).astype(
                bins_ref.dtype
            )
            stores[-1].start()
            routed_ref[...] = jnp.transpose(routed.astype(jnp.float32)).astype(routed_ref.dtype)
            routed_store.start()
    for store in stores:
        store.wait()
    routed_store.wait()


def pack(hidden, adapter_id, adapter_slot, owners, slot_count, held):
    rows, width = hidden.shape
    bins = owners * slot_count
    steps = pl.cdiv(width, COLUMNS_STEP)
    slots = adapter_slot.reshape(1, -1)
    return pl.pallas_call(
        functools.partial(pack_kernel, owners, slot_count, held),
        in_specs=[pl.BlockSpec(memory_space=pl.ANY)] * 3,
        out_specs=[pl.BlockSpec(memory_space=pl.ANY)] * 2,
        out_shape=[
            jax.ShapeDtypeStruct((bins, width + LANES), hidden.dtype),
            jax.ShapeDtypeStruct((rows, bins), jnp.bfloat16),
        ],
        scratch_shapes=[
            pltpu.VMEM(slots.shape, jnp.int32),
            pltpu.VMEM((1, rows), jnp.int32),
            pltpu.VMEM((rows, width), hidden.dtype),
            pltpu.VMEM((bins, width + LANES), hidden.dtype),
            pltpu.VMEM((rows, bins), jnp.bfloat16),
            pltpu.SemaphoreType.DMA((3,)),
            pltpu.SemaphoreType.DMA((steps,)),
            pltpu.SemaphoreType.DMA((steps + 1,)),
        ],
        compiler_params=pltpu.CompilerParams(vmem_limit_bytes=56 * 2**20),
        name="pack",
    )(slots, adapter_id.reshape(1, rows), hidden)


def adapt_kernel(arrived_ref, a_ref, b_ref, change_hbm, change_ref, sems):
    width = a_ref.shape[0]
    low = jnp.zeros((arrived_ref.shape[0], a_ref.shape[1]), jnp.float32)
    for at in range(0, width, ADAPT_STEP):
        low += jnp.dot(
            arrived_ref[:, at : at + ADAPT_STEP],
            a_ref[at : at + ADAPT_STEP, :],
            preferred_element_type=jnp.float32,
        )
    label = arrived_ref[:, width:].astype(jnp.float32)[:, :1].astype(jnp.int32)
    column = lax.broadcasted_iota(jnp.int32, low.shape, 1) // RANK
    low = jnp.where(column == label, low, 0.0).astype(jnp.bfloat16)
    stores = []
    for i, at in enumerate(range(0, b_ref.shape[1], OUT_STEP)):
        span = pl.ds(at, OUT_STEP)
        change_ref[:, at : at + OUT_STEP] = (
            SCALE * jnp.dot(low, b_ref[:, at : at + OUT_STEP], preferred_element_type=jnp.float32)
        ).astype(change_ref.dtype)
        stores.append(
            pltpu.make_async_copy(change_ref.at[:, span], change_hbm.at[:, span], sems.at[i])
        )
        stores[-1].start()
    for store in stores:
        store.wait()


def adapt(arrived, a_maps, b_maps):
    change = jax.ShapeDtypeStruct((arrived.shape[0], b_maps.shape[1]), jnp.bfloat16)
    return pl.pallas_call(
        adapt_kernel,
        in_specs=[pl.BlockSpec(memory_space=pltpu.VMEM)] * 3,
        out_specs=pl.BlockSpec(memory_space=pl.ANY),
        out_shape=change,
        scratch_shapes=[
            pltpu.VMEM(change.shape, change.dtype),
            pltpu.SemaphoreType.DMA((pl.cdiv(b_maps.shape[1], OUT_STEP),)),
        ],
        compiler_params=pltpu.CompilerParams(vmem_limit_bytes=16 * 2**20),
        name="adapt",
    )(arrived, a_maps, b_maps)


def tall(rows, group):
    return jnp.concatenate([rows[:, g * HEAD : (g + 1) * HEAD] for g in range(group)], axis=0)


def prep_kernel(group, base_ref, kv_ref, keys_ref, rest_ref):
    step, context = kv_ref.shape[0], kv_ref.shape[2]
    cells = step * context
    for k in range(KVH):
        head = slice(k * HEAD, (k + 1) * HEAD)
        keys = kv_ref[:, 0, :, head].astype(jnp.float32).reshape(cells, HEAD)
        keys_ref[k] = jnp.transpose(keys).astype(keys_ref.dtype)
        rest_ref[k, 0, :cells] = kv_ref[:, 1, :, head].reshape(cells, HEAD)
        base = base_ref[:, k * group * HEAD : (k + 1) * group * HEAD].astype(jnp.float32)
        rest_ref[k, 0, cells:] = tall(base, group).astype(rest_ref.dtype)


def prep(base_q, kv_cache):
    rows, width = base_q.shape
    context = kv_cache.shape[2]
    group = width // (KVH * HEAD)
    step = ROWS_STEP
    steps = rows // step
    cells = step * context
    lines = cells + group * step
    length = max(pl.cdiv(TALL_BYTES, 2 * KVH * lines * HEAD), steps)
    return pl.pallas_call(
        functools.partial(prep_kernel, group),
        grid=(steps,),
        in_specs=[
            pl.BlockSpec((step, width), lambda i: (i, 0)),
            pl.BlockSpec((step, *kv_cache.shape[1:]), lambda i: (i, 0, 0, 0)),
        ],
        out_specs=[
            pl.BlockSpec((KVH, HEAD, cells), lambda i: (0, 0, i)),
            pl.BlockSpec((KVH, 1, lines, HEAD), lambda i: (0, i, 0, 0)),
        ],
        out_shape=[
            jax.ShapeDtypeStruct((KVH, HEAD, rows * context), jnp.bfloat16),
            jax.ShapeDtypeStruct((KVH, length, lines, HEAD), jnp.bfloat16),
        ],
        compiler_params=pltpu.CompilerParams(vmem_limit_bytes=GRANT),
        name="prep",
    )(base_q, kv_cache)


def attend_kernel(
    group, context, routed_ref, returned_ref, keys_ref, lens_ref, rest_hbm, out_hbm, *scratch
):
    query_ref, values_ref, bias_ref, scores_ref, expo_ref, out_ref, sems = scratch
    step = ROWS_STEP
    steps, lines, cells = bias_ref.shape
    span = group * HEAD
    factor = LOG2E / jnp.sqrt(jnp.float32(HEAD))
    loads = [
        [
            pltpu.make_async_copy(
                rest_hbm.at[k, pl.ds(0, steps), pl.ds(cells, lines)], query_ref.at[k], sems.at[k, 1]
            ),
            pltpu.make_async_copy(
                rest_hbm.at[k, pl.ds(0, steps), pl.ds(0, cells)], values_ref.at[k], sems.at[k, 2]
            ),
        ]
        for k in range(KVH)
    ]
    stores = [
        pltpu.make_async_copy(
            out_ref.at[:, pl.ds(k * span, span)], out_hbm.at[:, pl.ds(k * span, span)], sems.at[k, 0]
        )
        for k in range(KVH)
    ]
    for load in loads:
        for copy in load:
            copy.start()
    lane = lax.broadcasted_iota(jnp.int32, (lines, cells), 1)
    line = lax.broadcasted_iota(jnp.int32, (lines, cells), 0)
    own = lax.div(lane, context) == lax.rem(line, step)
    position = lax.rem(lane, context)
    ones = jnp.ones((cells, HEAD), expo_ref.dtype)
    for i in range(steps):
        bias_ref[i] = jnp.where(own & (position < lens_ref[i]), 0.0, -jnp.inf)
    for k in range(KVH):
        delta = jnp.dot(
            routed_ref[...],
            returned_ref[:, k * span : (k + 1) * span],
            preferred_element_type=jnp.float32,
        )
        for copy in loads[k]:
            copy.wait()
        for i in range(steps):
            keys = keys_ref[k, :, i * cells : (i + 1) * cells]
            change = tall(delta[i * step : (i + 1) * step], group).astype(jnp.bfloat16)
            scores = jnp.dot(
                jnp.concatenate([query_ref[k, i], change], axis=1),
                jnp.concatenate([keys, keys], axis=0),
                preferred_element_type=jnp.float32,
            )
            scores_ref[k, i] = scores * factor + bias_ref[i]
        for i in range(steps):
            scores = scores_ref[k, i]
            expo = jnp.exp2(scores - jnp.max(scores, axis=1, keepdims=True))
            expo_ref[k, i] = expo.astype(expo_ref.dtype)
        for i in range(steps):
            rows = slice(i * step, (i + 1) * step)
            out = jnp.dot(
                expo_ref[k, i],
                jnp.concatenate([values_ref[k, i], ones], axis=1),
                preferred_element_type=jnp.float32,
            )
            out = out[:, :HEAD] * (1.0 / out[:, HEAD:])
            for g in range(group):
                out_ref[rows, (k * group + g) * HEAD : (k * group + g + 1) * HEAD] = out[
                    g * step : (g + 1) * step
                ].astype(out_ref.dtype)
        stores[k].start()
    for store in stores:
        store.wait()


def attend(routed, returned, cache_len, keys, rest, context):
    rows, width = routed.shape[0], returned.shape[1]
    group = width // (KVH * HEAD)
    step = ROWS_STEP
    steps = rows // step
    cells = step * context
    lens = jnp.repeat(cache_len, context).reshape(steps, 1, cells)
    return pl.pallas_call(
        functools.partial(attend_kernel, group, context),
        in_specs=[pl.BlockSpec(memory_space=pltpu.VMEM)] * 4 + [pl.BlockSpec(memory_space=pl.ANY)],
        out_specs=pl.BlockSpec(memory_space=pl.ANY),
        out_shape=jax.ShapeDtypeStruct((rows, width), jnp.bfloat16),
        scratch_shapes=[
            pltpu.VMEM((KVH, steps, group * step, HEAD), rest.dtype),
            pltpu.VMEM((KVH, steps, cells, HEAD), rest.dtype),
            pltpu.VMEM((steps, group * step, cells), jnp.float32),
            pltpu.VMEM((KVH, steps, group * step, cells), jnp.float32),
            pltpu.VMEM((KVH, steps, group * step, cells), jnp.bfloat16),
            pltpu.VMEM((rows, width), jnp.bfloat16),
            pltpu.SemaphoreType.DMA((KVH, 3)),
        ],
        compiler_params=pltpu.CompilerParams(vmem_limit_bytes=GRANT),
        name="attend",
    )(routed, returned, keys, lens, rest)


def on_device(hidden, adapter_id, adapter_slot, cache_len, base_q, kv_cache, a_maps, b_maps):
    owners = lax.axis_size("owner")
    rows = hidden.shape[0]
    held = a_maps.shape[1] // RANK
    slot_count = max(2, 2 * ((rows + 2 * owners - 1) // (2 * owners)))
    bins = owners * slot_count
    packed, routed = pack(hidden, adapter_id, adapter_slot, owners, slot_count, held)
    packed = packed.reshape(owners, slot_count, packed.shape[1])
    arrived = lax.all_to_all(packed, "owner", split_axis=0, concat_axis=0, tiled=True)
    keys, rest = prep(base_q, kv_cache)
    change = adapt(arrived.reshape(bins, arrived.shape[2]), a_maps, b_maps)
    change = change.reshape(owners, slot_count, change.shape[1])
    returned = lax.all_to_all(change, "owner", split_axis=0, concat_axis=0, tiled=True)
    returned = returned.reshape(bins, returned.shape[2])
    return attend(routed, returned, cache_len, keys, rest, kv_cache.shape[2])


def solution(mesh):
    return jax.shard_map(
        on_device,
        mesh=mesh,
        in_specs=(
            P(("groups", "owner"), None),
            P(("groups", "owner")),
            P("groups"),
            P(("groups", "owner")),
            P(("groups", "owner"), None),
            P(("groups", "owner"), None, None, None),
            P(None, "owner"),
            P("owner", None),
        ),
        out_specs=P(("groups", "owner"), None),
        check_vma=False,
    )
```

```python
import functools

import jax
import jax.numpy as jnp
from jax import lax
from jax.experimental import pallas as pl
from jax.experimental.pallas import tpu as pltpu
from jax.sharding import PartitionSpec as P

HEAD = 128
KVH = 4
RANK = 64
LANES = 128
SCALE = 2.0
ROWS_STEP = 8
COLUMNS_STEP = 1024
ADAPT_STEP = 2048
OUT_STEP = 1024
GRANT = 48 * 2**20
LOG2E = 1.4426950408889634
TALL_BYTES = 17 * 2**20


def routing(owners, slot_count, held, slots, ids):
    rows = ids.shape[1]
    named = lax.broadcasted_iota(jnp.int32, (slots.shape[1], rows), 0) == ids
    slot = jnp.dot(
        slots.astype(jnp.float32).astype(jnp.bfloat16),
        named.astype(jnp.bfloat16),
        preferred_element_type=jnp.float32,
    ).astype(jnp.int32)
    owner = lax.div(slot, held)
    local = slot - owner * held
    hits = owner == lax.broadcasted_iota(jnp.int32, (owners, rows), 0)
    earlier = lax.broadcasted_iota(jnp.int32, (rows, rows), 0) < lax.broadcasted_iota(
        jnp.int32, (rows, rows), 1
    )
    before = jnp.dot(
        hits.astype(jnp.bfloat16), earlier.astype(jnp.bfloat16), preferred_element_type=jnp.float32
    )
    place = jnp.sum(jnp.where(hits, before, 0.0), axis=0, keepdims=True).astype(jnp.int32)
    line = lax.broadcasted_iota(jnp.int32, (owners * slot_count, rows), 0)
    apart = owner ^ lax.axis_index("owner")
    sent = line == apart * slot_count + place
    label = jnp.sum(jnp.where(sent, local.astype(jnp.float32), 0.0), axis=1, keepdims=True)
    return sent, line == owner * slot_count + place, label


def pack_kernel(owners, slot_count, held, slots_hbm, ids_hbm, hidden_hbm, routed_ref, *refs):
    message_refs, (slots_ref, ids_ref, rows_ref, small_sems, sems) = refs[:owners], refs[owners:]
    width = rows_ref.shape[1]
    spans = [(at, min(COLUMNS_STEP, width - at)) for at in range(0, width, COLUMNS_STEP)]
    small = [
        pltpu.make_async_copy(slots_hbm, slots_ref, small_sems.at[0]),
        pltpu.make_async_copy(ids_hbm, ids_ref, small_sems.at[1]),
    ]
    loads = [
        pltpu.make_async_copy(
            hidden_hbm.at[:, pl.ds(at, size)], rows_ref.at[:, pl.ds(at, size)], sems.at[i]
        )
        for i, (at, size) in enumerate(spans)
    ]
    for copy in [*small, *loads]:
        copy.start()
    for copy in small:
        copy.wait()
    sent, routed, label = routing(owners, slot_count, held, slots_ref[...], ids_ref[...])
    sent = sent.astype(jnp.bfloat16)
    routed_ref[...] = jnp.transpose(routed.astype(jnp.float32)).astype(routed_ref.dtype)

    def put(at, lines):
        for i, message_ref in enumerate(message_refs):
            message_ref[:, at : at + lines.shape[1]] = lines[
                i * slot_count : (i + 1) * slot_count
            ].astype(message_ref.dtype)

    put(width, jnp.broadcast_to(label, (label.shape[0], LANES)))
    for load, (at, size) in zip(loads, spans):
        load.wait()
        put(at, jnp.dot(sent, rows_ref[:, at : at + size], preferred_element_type=jnp.float32))


def pack(hidden, adapter_id, adapter_slot, owners, slot_count, held):
    rows, width = hidden.shape
    bins = owners * slot_count
    steps = pl.cdiv(width, COLUMNS_STEP)
    slots = adapter_slot.reshape(1, -1)
    return pl.pallas_call(
        functools.partial(pack_kernel, owners, slot_count, held),
        in_specs=[pl.BlockSpec(memory_space=pl.ANY)] * 3,
        out_specs=[pl.BlockSpec(memory_space=pltpu.VMEM)] * (1 + owners),
        out_shape=[jax.ShapeDtypeStruct((rows, bins), jnp.bfloat16)]
        + [jax.ShapeDtypeStruct((slot_count, width + LANES), hidden.dtype)] * owners,
        scratch_shapes=[
            pltpu.VMEM(slots.shape, jnp.int32),
            pltpu.VMEM((1, rows), jnp.int32),
            pltpu.VMEM((rows, width), hidden.dtype),
            pltpu.SemaphoreType.DMA((2,)),
            pltpu.SemaphoreType.DMA((steps,)),
        ],
        compiler_params=pltpu.CompilerParams(vmem_limit_bytes=56 * 2**20),
        name="pack",
    )(slots, adapter_id.reshape(1, rows), hidden)


def stack(refs, at, size):
    return jnp.concatenate(
        [ref[:, at : at + size].astype(jnp.float32) for ref in refs], axis=0
    ).astype(jnp.bfloat16)


def adapt_kernel(order, *refs):
    owners = len(order)
    arrived_refs, (a_ref, b_ref, change_hbm, change_ref, sems) = refs[:owners], refs[owners:]
    width = a_ref.shape[0]
    slot_count = arrived_refs[0].shape[0]
    me = lax.axis_index("owner")
    low = jnp.zeros((owners * slot_count, a_ref.shape[1]), jnp.float32)
    for at in range(0, width, ADAPT_STEP):
        low += jnp.dot(
            stack(arrived_refs, at, ADAPT_STEP),
            a_ref[at : at + ADAPT_STEP, :],
            preferred_element_type=jnp.float32,
        )
    label = stack(arrived_refs, width, LANES).astype(jnp.float32)[:, :1].astype(jnp.int32)
    column = lax.broadcasted_iota(jnp.int32, low.shape, 1) // RANK
    low = jnp.where(column == label, low, 0.0).astype(jnp.bfloat16)
    stores = []
    for i, at in enumerate(range(0, b_ref.shape[1], OUT_STEP)):
        span = pl.ds(at, OUT_STEP)
        change = SCALE * jnp.dot(low, b_ref[:, at : at + OUT_STEP], preferred_element_type=jnp.float32)
        for j, s in enumerate(order):
            change_ref[me ^ s, :, at : at + OUT_STEP] = change[
                j * slot_count : (j + 1) * slot_count
            ].astype(change_ref.dtype)
        stores.append(
            pltpu.make_async_copy(change_ref.at[:, :, span], change_hbm.at[:, :, span], sems.at[i])
        )
        stores[-1].start()
    for store in stores:
        store.wait()


def adapt(arrived, order, a_maps, b_maps):
    owners = len(order)
    change = jax.ShapeDtypeStruct((owners, arrived[0].shape[0], b_maps.shape[1]), jnp.bfloat16)
    return pl.pallas_call(
        functools.partial(adapt_kernel, order),
        in_specs=[pl.BlockSpec(memory_space=pltpu.VMEM)] * (owners + 2),
        out_specs=pl.BlockSpec(memory_space=pl.ANY),
        out_shape=change,
        scratch_shapes=[
            pltpu.VMEM(change.shape, change.dtype),
            pltpu.SemaphoreType.DMA((pl.cdiv(b_maps.shape[1], OUT_STEP),)),
        ],
        compiler_params=pltpu.CompilerParams(vmem_limit_bytes=16 * 2**20),
        name="adapt",
    )(*arrived, a_maps, b_maps)


def tall(rows, group):
    return jnp.concatenate([rows[:, g * HEAD : (g + 1) * HEAD] for g in range(group)], axis=0)


def prep_kernel(group, base_ref, kv_ref, keys_ref, rest_ref):
    step, context = kv_ref.shape[0], kv_ref.shape[2]
    cells = step * context
    for k in range(KVH):
        head = slice(k * HEAD, (k + 1) * HEAD)
        keys = kv_ref[:, 0, :, head].astype(jnp.float32).reshape(cells, HEAD)
        keys_ref[k] = jnp.transpose(keys).astype(keys_ref.dtype)
        rest_ref[k, 0, :cells] = kv_ref[:, 1, :, head].reshape(cells, HEAD)
        base = base_ref[:, k * group * HEAD : (k + 1) * group * HEAD].astype(jnp.float32)
        rest_ref[k, 0, cells:] = tall(base, group).astype(rest_ref.dtype)


def prep(base_q, kv_cache):
    rows, width = base_q.shape
    context = kv_cache.shape[2]
    group = width // (KVH * HEAD)
    step = ROWS_STEP
    steps = rows // step
    cells = step * context
    lines = cells + group * step
    length = max(pl.cdiv(TALL_BYTES, 2 * KVH * lines * HEAD), steps)
    return pl.pallas_call(
        functools.partial(prep_kernel, group),
        grid=(steps,),
        in_specs=[
            pl.BlockSpec((step, width), lambda i: (i, 0)),
            pl.BlockSpec((step, *kv_cache.shape[1:]), lambda i: (i, 0, 0, 0)),
        ],
        out_specs=[
            pl.BlockSpec((KVH, HEAD, cells), lambda i: (0, 0, i)),
            pl.BlockSpec((KVH, 1, lines, HEAD), lambda i: (0, i, 0, 0)),
        ],
        out_shape=[
            jax.ShapeDtypeStruct((KVH, HEAD, rows * context), jnp.bfloat16),
            jax.ShapeDtypeStruct((KVH, length, lines, HEAD), jnp.bfloat16),
        ],
        compiler_params=pltpu.CompilerParams(vmem_limit_bytes=GRANT),
        name="prep",
    )(base_q, kv_cache)


def attend_kernel(
    group, context, routed_ref, returned_ref, keys_ref, lens_ref, rest_hbm, out_hbm, *scratch
):
    query_ref, values_ref, bias_ref, scores_ref, expo_ref, out_ref, sems = scratch
    step = ROWS_STEP
    steps, lines, cells = bias_ref.shape
    span = group * HEAD
    factor = LOG2E / jnp.sqrt(jnp.float32(HEAD))
    loads = [
        [
            pltpu.make_async_copy(
                rest_hbm.at[k, pl.ds(0, steps), pl.ds(cells, lines)], query_ref.at[k], sems.at[k, 1]
            ),
            pltpu.make_async_copy(
                rest_hbm.at[k, pl.ds(0, steps), pl.ds(0, cells)], values_ref.at[k], sems.at[k, 2]
            ),
        ]
        for k in range(KVH)
    ]
    stores = [
        pltpu.make_async_copy(
            out_ref.at[:, pl.ds(k * span, span)], out_hbm.at[:, pl.ds(k * span, span)], sems.at[k, 0]
        )
        for k in range(KVH)
    ]
    for load in loads:
        for copy in load:
            copy.start()
    lane = lax.broadcasted_iota(jnp.int32, (lines, cells), 1)
    line = lax.broadcasted_iota(jnp.int32, (lines, cells), 0)
    own = lax.div(lane, context) == lax.rem(line, step)
    position = lax.rem(lane, context)
    ones = jnp.ones((cells, HEAD), expo_ref.dtype)
    for i in range(steps):
        bias_ref[i] = jnp.where(own & (position < lens_ref[i]), 0.0, -jnp.inf)
    for k in range(KVH):
        delta = jnp.dot(
            routed_ref[...],
            returned_ref[:, k * span : (k + 1) * span],
            preferred_element_type=jnp.float32,
        )
        for copy in loads[k]:
            copy.wait()
        for i in range(steps):
            keys = keys_ref[k, :, i * cells : (i + 1) * cells]
            change = tall(delta[i * step : (i + 1) * step], group).astype(jnp.bfloat16)
            scores = jnp.dot(
                jnp.concatenate([query_ref[k, i], change], axis=1),
                jnp.concatenate([keys, keys], axis=0),
                preferred_element_type=jnp.float32,
            )
            scores_ref[k, i] = scores * factor + bias_ref[i]
        for i in range(steps):
            scores = scores_ref[k, i]
            expo = jnp.exp2(scores - jnp.max(scores, axis=1, keepdims=True))
            expo_ref[k, i] = expo.astype(expo_ref.dtype)
        for i in range(steps):
            rows = slice(i * step, (i + 1) * step)
            out = jnp.dot(
                expo_ref[k, i],
                jnp.concatenate([values_ref[k, i], ones], axis=1),
                preferred_element_type=jnp.float32,
            )
            out = out[:, :HEAD] * (1.0 / out[:, HEAD:])
            for g in range(group):
                out_ref[rows, (k * group + g) * HEAD : (k * group + g + 1) * HEAD] = out[
                    g * step : (g + 1) * step
                ].astype(out_ref.dtype)
        stores[k].start()
    for store in stores:
        store.wait()


def attend(routed, returned, cache_len, keys, rest, context):
    rows, width = routed.shape[0], returned.shape[1]
    group = width // (KVH * HEAD)
    step = ROWS_STEP
    steps = rows // step
    cells = step * context
    lens = jnp.repeat(cache_len, context).reshape(steps, 1, cells)
    return pl.pallas_call(
        functools.partial(attend_kernel, group, context),
        in_specs=[pl.BlockSpec(memory_space=pltpu.VMEM)] * 4 + [pl.BlockSpec(memory_space=pl.ANY)],
        out_specs=pl.BlockSpec(memory_space=pl.ANY),
        out_shape=jax.ShapeDtypeStruct((rows, width), jnp.bfloat16),
        scratch_shapes=[
            pltpu.VMEM((KVH, steps, group * step, HEAD), rest.dtype),
            pltpu.VMEM((KVH, steps, cells, HEAD), rest.dtype),
            pltpu.VMEM((steps, group * step, cells), jnp.float32),
            pltpu.VMEM((KVH, steps, group * step, cells), jnp.float32),
            pltpu.VMEM((KVH, steps, group * step, cells), jnp.bfloat16),
            pltpu.VMEM((rows, width), jnp.bfloat16),
            pltpu.SemaphoreType.DMA((KVH, 3)),
        ],
        compiler_params=pltpu.CompilerParams(vmem_limit_bytes=GRANT),
        name="attend",
    )(routed, returned, keys, lens, rest)


def on_device(hidden, adapter_id, adapter_slot, cache_len, base_q, kv_cache, a_maps, b_maps):
    owners = lax.axis_size("owner")
    rows = hidden.shape[0]
    held = a_maps.shape[1] // RANK
    slot_count = max(2, 2 * ((rows + 2 * owners - 1) // (2 * owners)))
    bins = owners * slot_count
    routed, *messages = pack(hidden, adapter_id, adapter_slot, owners, slot_count, held)
    half = owners // 2
    near = [*range(half // 2, half), *range(1, half // 2)]
    order = [s for pair in zip(range(half, owners), [*near, 0]) for s in pair]
    arrived = [
        lax.ppermute(messages[s], "owner", [(i, i ^ s) for i in range(owners)]) if s else messages[s]
        for s in order
    ]
    keys, rest = prep(base_q, kv_cache)
    change = adapt(arrived, order, a_maps, b_maps)
    returned = lax.all_to_all(change, "owner", split_axis=0, concat_axis=0, tiled=True)
    returned = returned.reshape(bins, returned.shape[2])
    return attend(routed, returned, cache_len, keys, rest, kv_cache.shape[2])


def solution(mesh):
    return jax.shard_map(
        on_device,
        mesh=mesh,
        in_specs=(
            P(("groups", "owner"), None),
            P(("groups", "owner")),
            P("groups"),
            P(("groups", "owner")),
            P(("groups", "owner"), None),
            P(("groups", "owner"), None, None, None),
            P(None, "owner"),
            P("owner", None),
        ),
        out_specs=P(("groups", "owner"), None),
        check_vma=False,
    )
```

```python
import functools

import jax
import jax.numpy as jnp
from jax import lax
from jax.experimental import pallas as pl
from jax.experimental.pallas import tpu as pltpu
from jax.sharding import PartitionSpec as P

HEAD = 128
KVH = 4
RANK = 64
LANES = 128
SCALE = 2.0
ROWS_STEP = 8
PREP_STEPS = 2
GROUPS = 4
MOST_PERMUTES = 32
COLUMNS_STEP = 1024
ADAPT_STEP = 2048
OUT_STEP = 1024
GRANT = 48 * 2**20
LOG2E = 1.4426950408889634
TALL_BYTES = 17 * 2**20


def routing(owners, slot_count, held, slots, ids):
    rows = ids.shape[1]
    named = lax.broadcasted_iota(jnp.int32, (slots.shape[1], rows), 0) == ids
    slot = jnp.dot(
        slots.astype(jnp.float32).astype(jnp.bfloat16),
        named.astype(jnp.bfloat16),
        preferred_element_type=jnp.float32,
    ).astype(jnp.int32)
    owner = lax.div(slot, held)
    local = slot - owner * held
    hits = owner == lax.broadcasted_iota(jnp.int32, (owners, rows), 0)
    earlier = lax.broadcasted_iota(jnp.int32, (rows, rows), 0) < lax.broadcasted_iota(
        jnp.int32, (rows, rows), 1
    )
    before = jnp.dot(
        hits.astype(jnp.bfloat16), earlier.astype(jnp.bfloat16), preferred_element_type=jnp.float32
    )
    place = jnp.sum(jnp.where(hits, before, 0.0), axis=0, keepdims=True).astype(jnp.int32)
    line = lax.broadcasted_iota(jnp.int32, (owners * slot_count, rows), 0)
    apart = owner ^ lax.axis_index("owner")
    routed = line == apart * slot_count + place
    label = jnp.sum(jnp.where(routed, local.astype(jnp.float32), 0.0), axis=1, keepdims=True)
    return routed, label


def pack_kernel(owners, slot_count, held, slots_hbm, ids_hbm, hidden_hbm, routed_ref, *refs):
    message_refs, (slots_ref, ids_ref, rows_ref, small_sems, sems) = refs[:owners], refs[owners:]
    width = rows_ref.shape[1]
    spans = [(at, min(COLUMNS_STEP, width - at)) for at in range(0, width, COLUMNS_STEP)]
    small = [
        pltpu.make_async_copy(slots_hbm, slots_ref, small_sems.at[0]),
        pltpu.make_async_copy(ids_hbm, ids_ref, small_sems.at[1]),
    ]
    loads = [
        pltpu.make_async_copy(
            hidden_hbm.at[:, pl.ds(at, size)], rows_ref.at[:, pl.ds(at, size)], sems.at[i]
        )
        for i, (at, size) in enumerate(spans)
    ]
    for copy in [*small, *loads]:
        copy.start()
    for copy in small:
        copy.wait()
    routed, label = routing(owners, slot_count, held, slots_ref[...], ids_ref[...])
    routed_ref[...] = jnp.transpose(routed.astype(jnp.float32)).astype(routed_ref.dtype)
    routed = routed.astype(jnp.bfloat16)

    def put(at, lines):
        for i, message_ref in enumerate(message_refs):
            message_ref[:, at : at + lines.shape[1]] = lines[
                i * slot_count : (i + 1) * slot_count
            ].astype(message_ref.dtype)

    put(width, jnp.broadcast_to(label, (label.shape[0], LANES)))
    for load, (at, size) in zip(loads, spans):
        load.wait()
        put(at, jnp.dot(routed, rows_ref[:, at : at + size], preferred_element_type=jnp.float32))


def pack(hidden, adapter_id, adapter_slot, owners, slot_count, held):
    rows, width = hidden.shape
    bins = owners * slot_count
    steps = pl.cdiv(width, COLUMNS_STEP)
    slots = adapter_slot.reshape(1, -1)
    return pl.pallas_call(
        functools.partial(pack_kernel, owners, slot_count, held),
        in_specs=[pl.BlockSpec(memory_space=pl.ANY)] * 3,
        out_specs=[pl.BlockSpec(memory_space=pltpu.VMEM)] * (1 + owners),
        out_shape=[jax.ShapeDtypeStruct((rows, bins), jnp.bfloat16)]
        + [jax.ShapeDtypeStruct((slot_count, width + LANES), hidden.dtype)] * owners,
        scratch_shapes=[
            pltpu.VMEM(slots.shape, jnp.int32),
            pltpu.VMEM((1, rows), jnp.int32),
            pltpu.VMEM((rows, width), hidden.dtype),
            pltpu.SemaphoreType.DMA((2,)),
            pltpu.SemaphoreType.DMA((steps,)),
        ],
        compiler_params=pltpu.CompilerParams(vmem_limit_bytes=56 * 2**20),
        name="pack",
    )(slots, adapter_id.reshape(1, rows), hidden)


def stack(refs, at, size):
    return jnp.concatenate(
        [ref[:, at : at + size].astype(jnp.float32) for ref in refs], axis=0
    ).astype(jnp.bfloat16)


def adapt_kernel(count, *refs):
    arrived_refs, (a_ref, b_ref), change_refs = refs[:count], refs[count : count + 2], refs[-count:]
    width = a_ref.shape[0]
    slot_count = arrived_refs[0].shape[0]
    low = jnp.zeros((count * slot_count, a_ref.shape[1]), jnp.float32)
    for at in range(0, width, ADAPT_STEP):
        low += jnp.dot(
            stack(arrived_refs, at, ADAPT_STEP),
            a_ref[at : at + ADAPT_STEP, :],
            preferred_element_type=jnp.float32,
        )
    label = stack(arrived_refs, width, LANES).astype(jnp.float32)[:, :1].astype(jnp.int32)
    column = lax.broadcasted_iota(jnp.int32, low.shape, 1) // RANK
    low = jnp.where(column == label, low, 0.0).astype(jnp.bfloat16)
    for at in range(0, b_ref.shape[1], OUT_STEP):
        change = SCALE * jnp.dot(low, b_ref[:, at : at + OUT_STEP], preferred_element_type=jnp.float32)
        for i, change_ref in enumerate(change_refs):
            change_ref[:, at : at + OUT_STEP] = change[
                i * slot_count : (i + 1) * slot_count
            ].astype(change_ref.dtype)


def adapt(arrived, a_maps, b_maps, after):
    count = len(arrived)
    change = jax.ShapeDtypeStruct((arrived[0].shape[0], b_maps.shape[1]), jnp.bfloat16)
    return pl.pallas_call(
        functools.partial(adapt_kernel, count),
        in_specs=[pl.BlockSpec(memory_space=pltpu.VMEM)] * (count + 2)
        + [pl.BlockSpec(memory_space=pl.ANY)],
        out_specs=[pl.BlockSpec(memory_space=pltpu.VMEM)] * count,
        out_shape=[change] * count,
        compiler_params=pltpu.CompilerParams(vmem_limit_bytes=GRANT),
        name="adapt",
    )(*arrived, a_maps, b_maps, after)


def tall(rows, group):
    return jnp.concatenate([rows[:, g * HEAD : (g + 1) * HEAD] for g in range(group)], axis=0)


def prep_kernel(group, base_ref, kv_ref, keys_ref, rest_ref):
    step, context = ROWS_STEP, kv_ref.shape[2]
    cells = step * context
    for j in range(PREP_STEPS):
        rows = slice(j * step, (j + 1) * step)
        for k in range(KVH):
            head = slice(k * HEAD, (k + 1) * HEAD)
            keys = kv_ref[rows, 0, :, head].astype(jnp.float32).reshape(cells, HEAD)
            keys_ref[k, :, j * cells : (j + 1) * cells] = jnp.transpose(keys).astype(keys_ref.dtype)
            rest_ref[k, j, :cells] = kv_ref[rows, 1, :, head].reshape(cells, HEAD)
            base = base_ref[:, k * group * HEAD : (k + 1) * group * HEAD].astype(jnp.float32)
            rest_ref[k, j, cells:] = tall(base[rows], group).astype(rest_ref.dtype)


def prep(base_q, kv_cache):
    rows, width = base_q.shape
    context = kv_cache.shape[2]
    group = width // (KVH * HEAD)
    step = ROWS_STEP * PREP_STEPS
    steps = rows // step
    cells = ROWS_STEP * context
    lines = cells + group * ROWS_STEP
    length = max(pl.cdiv(TALL_BYTES, 2 * KVH * lines * HEAD * PREP_STEPS), steps) * PREP_STEPS
    return pl.pallas_call(
        functools.partial(prep_kernel, group),
        grid=(steps,),
        in_specs=[
            pl.BlockSpec((step, width), lambda i: (i, 0)),
            pl.BlockSpec((step, *kv_cache.shape[1:]), lambda i: (i, 0, 0, 0)),
        ],
        out_specs=[
            pl.BlockSpec((KVH, HEAD, PREP_STEPS * cells), lambda i: (0, 0, i)),
            pl.BlockSpec((KVH, PREP_STEPS, lines, HEAD), lambda i: (0, i, 0, 0)),
        ],
        out_shape=[
            jax.ShapeDtypeStruct((KVH, HEAD, rows * context), jnp.bfloat16),
            jax.ShapeDtypeStruct((KVH, length, lines, HEAD), jnp.bfloat16),
        ],
        compiler_params=pltpu.CompilerParams(vmem_limit_bytes=GRANT),
        name="prep",
    )(base_q, kv_cache)


def attend_kernel(group, context, order, *refs):
    returned_refs, refs = refs[: len(order)], refs[len(order) :]
    returned_refs = [returned_refs[order.index(s)] for s in range(len(order))]
    routed_ref, keys_ref, lens_ref, rest_hbm, out_hbm, *scratch = refs
    query_ref, values_ref, bias_ref, scores_ref, expo_ref, out_ref, sems = scratch
    step = ROWS_STEP
    steps, lines, cells = bias_ref.shape
    span = group * HEAD
    factor = LOG2E / jnp.sqrt(jnp.float32(HEAD))
    loads = [
        [
            pltpu.make_async_copy(
                rest_hbm.at[k, pl.ds(0, steps), pl.ds(cells, lines)], query_ref.at[k], sems.at[k, 1]
            ),
            pltpu.make_async_copy(
                rest_hbm.at[k, pl.ds(0, steps), pl.ds(0, cells)], values_ref.at[k], sems.at[k, 2]
            ),
        ]
        for k in range(KVH)
    ]
    stores = [
        pltpu.make_async_copy(
            out_ref.at[:, pl.ds(k * span, span)], out_hbm.at[:, pl.ds(k * span, span)], sems.at[k, 0]
        )
        for k in range(KVH)
    ]
    for load in loads:
        for copy in load:
            copy.start()
    lane = lax.broadcasted_iota(jnp.int32, (lines, cells), 1)
    line = lax.broadcasted_iota(jnp.int32, (lines, cells), 0)
    own = lax.div(lane, context) == lax.rem(line, step)
    position = lax.rem(lane, context)
    ones = jnp.ones((cells, HEAD), expo_ref.dtype)
    for i in range(steps):
        bias_ref[i] = jnp.where(own & (position < lens_ref[i]), 0.0, -jnp.inf)
    for k in range(KVH):
        delta = jnp.dot(
            routed_ref[...],
            stack(returned_refs, k * span, span),
            preferred_element_type=jnp.float32,
        )
        for copy in loads[k]:
            copy.wait()
        for i in range(steps):
            keys = keys_ref[k, :, i * cells : (i + 1) * cells]
            change = tall(delta[i * step : (i + 1) * step], group).astype(jnp.bfloat16)
            scores = jnp.dot(
                jnp.concatenate([query_ref[k, i], change], axis=1),
                jnp.concatenate([keys, keys], axis=0),
                preferred_element_type=jnp.float32,
            )
            scores_ref[k, i] = scores * factor + bias_ref[i]
        for i in range(steps):
            scores = scores_ref[k, i]
            expo = jnp.exp2(scores - jnp.max(scores, axis=1, keepdims=True))
            expo_ref[k, i] = expo.astype(expo_ref.dtype)
        for i in range(steps):
            rows = slice(i * step, (i + 1) * step)
            out = jnp.dot(
                expo_ref[k, i],
                jnp.concatenate([values_ref[k, i], ones], axis=1),
                preferred_element_type=jnp.float32,
            )
            out = out[:, :HEAD] * (1.0 / out[:, HEAD:])
            for g in range(group):
                out_ref[rows, (k * group + g) * HEAD : (k * group + g + 1) * HEAD] = out[
                    g * step : (g + 1) * step
                ].astype(out_ref.dtype)
        stores[k].start()
    for store in stores:
        store.wait()


def attend(routed, returned, order, cache_len, keys, rest, context):
    rows, width = routed.shape[0], returned[0].shape[1]
    group = width // (KVH * HEAD)
    step = ROWS_STEP
    steps = rows // step
    cells = step * context
    lens = jnp.repeat(cache_len, context).reshape(steps, 1, cells)
    return pl.pallas_call(
        functools.partial(attend_kernel, group, context, order),
        in_specs=[pl.BlockSpec(memory_space=pltpu.VMEM)] * (3 + len(order)) + [pl.BlockSpec(memory_space=pl.ANY)],
        out_specs=pl.BlockSpec(memory_space=pl.ANY),
        out_shape=jax.ShapeDtypeStruct((rows, width), jnp.bfloat16),
        scratch_shapes=[
            pltpu.VMEM((KVH, steps, group * step, HEAD), rest.dtype),
            pltpu.VMEM((KVH, steps, cells, HEAD), rest.dtype),
            pltpu.VMEM((steps, group * step, cells), jnp.float32),
            pltpu.VMEM((KVH, steps, group * step, cells), jnp.float32),
            pltpu.VMEM((KVH, steps, group * step, cells), jnp.bfloat16),
            pltpu.VMEM((rows, width), jnp.bfloat16),
            pltpu.SemaphoreType.DMA((KVH, 3)),
        ],
        compiler_params=pltpu.CompilerParams(vmem_limit_bytes=GRANT),
        name="attend",
    )(*returned, routed, keys, lens, rest)


def on_device(hidden, adapter_id, adapter_slot, cache_len, base_q, kv_cache, a_maps, b_maps):
    owners = lax.axis_size("owner")
    rows = hidden.shape[0]
    held = a_maps.shape[1] // RANK
    slot_count = max(2, 2 * ((rows + 2 * owners - 1) // (2 * owners)))
    routed, *messages = pack(hidden, adapter_id, adapter_slot, owners, slot_count, held)
    half = owners // 2
    near = [*range(half // 2, half), *range(1, half // 2)]
    order = [s for pair in zip(range(half, owners), [*near, 0]) for s in pair]

    keys, rest = prep(base_q, kv_cache)
    size = owners // GROUPS
    arrived = exchange(order, owners)(messages[s] for s in order)
    changes = []
    for at in range(0, owners, size):
        changes += adapt(arrived[at : at + size], a_maps, b_maps, rest)
    returned = exchange(order, owners)(changes)
    return attend(routed, returned, order, cache_len, keys, rest, kv_cache.shape[2])


def exchange(order, owners):
    def permutes(messages):
        return [
            lax.ppermute(message, "owner", [(i, i ^ s) for i in range(owners)]) if s else message
            for message, s in zip(messages, order)
        ]

    def whole(messages):
        messages = dict(zip(order, messages))
        place = lax.axis_index("owner") ^ jnp.arange(owners, dtype=jnp.int32)
        blocks = jnp.stack([messages[s] for s in range(owners)])[place]
        blocks = lax.all_to_all(blocks, "owner", split_axis=0, concat_axis=0, tiled=True)[place]
        return [blocks[s] for s in order]

    return permutes if owners <= MOST_PERMUTES else whole


def solution(mesh):
    return jax.shard_map(
        on_device,
        mesh=mesh,
        in_specs=(
            P(("groups", "owner"), None),
            P(("groups", "owner")),
            P("groups"),
            P(("groups", "owner")),
            P(("groups", "owner"), None),
            P(("groups", "owner"), None, None, None),
            P(None, "owner"),
            P("owner", None),
        ),
        out_specs=P(("groups", "owner"), None),
        check_vma=False,
    )
```

```python
import functools

import jax
import jax.numpy as jnp
from jax import lax
from jax.experimental import pallas as pl
from jax.experimental.pallas import tpu as pltpu
from jax.sharding import PartitionSpec as P

HEAD = 128
KVH = 4
RANK = 64
LANES = 128
SCALE = 2.0
ROWS_STEP = 8
PREP_STEPS = 2
GROUPS = 4
HELD = 4
MOST_PERMUTES = 32
COLUMNS_STEP = 1024
ADAPT_STEP = 2048
OUT_STEP = 1024
GRANT = 48 * 2**20
LOG2E = 1.4426950408889634
TALL_BYTES = 17 * 2**20


def routing(owners, slot_count, held, slots, ids):
    rows = ids.shape[1]
    named = lax.broadcasted_iota(jnp.int32, (slots.shape[1], rows), 0) == ids
    slot = jnp.dot(
        slots.astype(jnp.float32).astype(jnp.bfloat16),
        named.astype(jnp.bfloat16),
        preferred_element_type=jnp.float32,
    ).astype(jnp.int32)
    owner = lax.div(slot, held)
    local = slot - owner * held
    hits = owner == lax.broadcasted_iota(jnp.int32, (owners, rows), 0)
    earlier = lax.broadcasted_iota(jnp.int32, (rows, rows), 0) < lax.broadcasted_iota(
        jnp.int32, (rows, rows), 1
    )
    before = jnp.dot(
        hits.astype(jnp.bfloat16), earlier.astype(jnp.bfloat16), preferred_element_type=jnp.float32
    )
    place = jnp.sum(jnp.where(hits, before, 0.0), axis=0, keepdims=True).astype(jnp.int32)
    line = lax.broadcasted_iota(jnp.int32, (owners * slot_count, rows), 0)
    apart = owner ^ lax.axis_index("owner")
    routed = line == apart * slot_count + place
    label = jnp.sum(jnp.where(routed, local.astype(jnp.float32), 0.0), axis=1, keepdims=True)
    return routed, label


def pack_kernel(owners, slot_count, held, slots_hbm, ids_hbm, hidden_hbm, routed_ref, *refs):
    message_refs, (slots_ref, ids_ref, rows_ref, small_sems, sems) = refs[:owners], refs[owners:]
    width = rows_ref.shape[1]
    spans = [(at, min(COLUMNS_STEP, width - at)) for at in range(0, width, COLUMNS_STEP)]
    small = [
        pltpu.make_async_copy(slots_hbm, slots_ref, small_sems.at[0]),
        pltpu.make_async_copy(ids_hbm, ids_ref, small_sems.at[1]),
    ]
    loads = [
        pltpu.make_async_copy(
            hidden_hbm.at[:, pl.ds(at, size)], rows_ref.at[:, pl.ds(at, size)], sems.at[i]
        )
        for i, (at, size) in enumerate(spans)
    ]
    for copy in [*small, *loads]:
        copy.start()
    for copy in small:
        copy.wait()
    routed, label = routing(owners, slot_count, held, slots_ref[...], ids_ref[...])
    routed_ref[...] = jnp.transpose(routed.astype(jnp.float32)).astype(routed_ref.dtype)
    routed = routed.astype(jnp.bfloat16)

    def put(at, lines):
        for i, message_ref in enumerate(message_refs):
            message_ref[:, at : at + lines.shape[1]] = lines[
                i * slot_count : (i + 1) * slot_count
            ].astype(message_ref.dtype)

    put(width, jnp.broadcast_to(label, (label.shape[0], LANES)))
    for load, (at, size) in zip(loads, spans):
        load.wait()
        put(at, jnp.dot(routed, rows_ref[:, at : at + size], preferred_element_type=jnp.float32))


def pack(hidden, adapter_id, adapter_slot, owners, slot_count, held):
    rows, width = hidden.shape
    bins = owners * slot_count
    steps = pl.cdiv(width, COLUMNS_STEP)
    slots = adapter_slot.reshape(1, -1)
    return pl.pallas_call(
        functools.partial(pack_kernel, owners, slot_count, held),
        in_specs=[pl.BlockSpec(memory_space=pl.ANY)] * 3,
        out_specs=[pl.BlockSpec(memory_space=pltpu.VMEM)] * (1 + owners),
        out_shape=[jax.ShapeDtypeStruct((rows, bins), jnp.bfloat16)]
        + [jax.ShapeDtypeStruct((slot_count, width + LANES), hidden.dtype)] * owners,
        scratch_shapes=[
            pltpu.VMEM(slots.shape, jnp.int32),
            pltpu.VMEM((1, rows), jnp.int32),
            pltpu.VMEM((rows, width), hidden.dtype),
            pltpu.SemaphoreType.DMA((2,)),
            pltpu.SemaphoreType.DMA((steps,)),
        ],
        compiler_params=pltpu.CompilerParams(vmem_limit_bytes=56 * 2**20),
        name="pack",
    )(slots, adapter_id.reshape(1, rows), hidden)


def stack(refs, at, size):
    return jnp.concatenate(
        [ref[:, at : at + size].astype(jnp.float32) for ref in refs], axis=0
    ).astype(jnp.bfloat16)


def adapt_kernel(count, *refs):
    arrived_refs, (a_ref, b_ref), change_refs = refs[:count], refs[count : count + 2], refs[-count:]
    width = a_ref.shape[0]
    slot_count = arrived_refs[0].shape[0]
    low = jnp.zeros((count * slot_count, a_ref.shape[1]), jnp.float32)
    for at in range(0, width, ADAPT_STEP):
        low += jnp.dot(
            stack(arrived_refs, at, ADAPT_STEP),
            a_ref[at : at + ADAPT_STEP, :],
            preferred_element_type=jnp.float32,
        )
    label = stack(arrived_refs, width, LANES).astype(jnp.float32)[:, :1].astype(jnp.int32)
    column = lax.broadcasted_iota(jnp.int32, low.shape, 1) // RANK
    low = jnp.where(column == label, low, 0.0).astype(jnp.bfloat16)
    for at in range(0, b_ref.shape[1], OUT_STEP):
        change = SCALE * jnp.dot(low, b_ref[:, at : at + OUT_STEP], preferred_element_type=jnp.float32)
        for i, change_ref in enumerate(change_refs):
            change_ref[:, at : at + OUT_STEP] = change[
                i * slot_count : (i + 1) * slot_count
            ].astype(change_ref.dtype)


def adapt(arrived, a_maps, b_maps):
    count = len(arrived)
    change = jax.ShapeDtypeStruct((arrived[0].shape[0], b_maps.shape[1]), jnp.bfloat16)
    return pl.pallas_call(
        functools.partial(adapt_kernel, count),
        in_specs=[pl.BlockSpec(memory_space=pltpu.VMEM)] * (count + 2),
        out_specs=[pl.BlockSpec(memory_space=pltpu.VMEM)] * count,
        out_shape=[change] * count,
        compiler_params=pltpu.CompilerParams(vmem_limit_bytes=GRANT),
        name="adapt",
    )(*arrived, a_maps, b_maps)


def tall(rows, group):
    return jnp.concatenate([rows[:, g * HEAD : (g + 1) * HEAD] for g in range(group)], axis=0)


def prep_kernel(group, base_ref, kv_ref, given_ref, keys_ref, rest_ref, lens_ref):
    lens_ref[...] = given_ref[...]
    step, context = ROWS_STEP, kv_ref.shape[2]
    cells = step * context
    for j in range(PREP_STEPS):
        rows = slice(j * step, (j + 1) * step)
        for k in range(KVH):
            head = slice(k * HEAD, (k + 1) * HEAD)
            keys = kv_ref[rows, 0, :, head].astype(jnp.float32).reshape(cells, HEAD)
            keys_ref[k, :, j * cells : (j + 1) * cells] = jnp.transpose(keys).astype(keys_ref.dtype)
            rest_ref[k, j, :cells] = kv_ref[rows, 1, :, head].reshape(cells, HEAD)
            base = base_ref[:, k * group * HEAD : (k + 1) * group * HEAD].astype(jnp.float32)
            rest_ref[k, j, cells:] = tall(base[rows], group).astype(rest_ref.dtype)


def prep(base_q, kv_cache, cache_len):
    rows, width = base_q.shape
    context = kv_cache.shape[2]
    group = width // (KVH * HEAD)
    step = ROWS_STEP * PREP_STEPS
    steps = rows // step
    cells = ROWS_STEP * context
    lines = cells + group * ROWS_STEP
    lens = jnp.repeat(cache_len, context).reshape(rows // ROWS_STEP, 1, cells)
    length = max(pl.cdiv(TALL_BYTES, 2 * KVH * lines * HEAD * PREP_STEPS), steps) * PREP_STEPS
    return pl.pallas_call(
        functools.partial(prep_kernel, group),
        grid=(steps,),
        in_specs=[
            pl.BlockSpec((step, width), lambda i: (i, 0)),
            pl.BlockSpec((step, *kv_cache.shape[1:]), lambda i: (i, 0, 0, 0)),
            pl.BlockSpec((PREP_STEPS, 1, cells), lambda i: (i, 0, 0)),
        ],
        out_specs=[
            pl.BlockSpec((KVH, HEAD, PREP_STEPS * cells), lambda i: (0, 0, i)),
            pl.BlockSpec((KVH, PREP_STEPS, lines, HEAD), lambda i: (0, i, 0, 0)),
            pl.BlockSpec((PREP_STEPS, 1, cells), lambda i: (i, 0, 0)),
        ],
        out_shape=[
            jax.ShapeDtypeStruct((KVH, HEAD, rows * context), jnp.bfloat16),
            jax.ShapeDtypeStruct((KVH, length, lines, HEAD), jnp.bfloat16),
            jax.ShapeDtypeStruct(lens.shape, lens.dtype),
        ],
        compiler_params=pltpu.CompilerParams(vmem_limit_bytes=GRANT),
        name="prep",
    )(base_q, kv_cache, lens)


def hold_kernel(*refs):
    del refs


def hold(message, after):
    return pl.pallas_call(
        hold_kernel,
        in_specs=[pl.BlockSpec(memory_space=pl.ANY)] * 2,
        out_specs=pl.BlockSpec(memory_space=pl.ANY),
        out_shape=jax.ShapeDtypeStruct(message.shape, message.dtype),
        input_output_aliases={0: 0},
        compiler_params=pltpu.CompilerParams(vmem_limit_bytes=GRANT),
        name="hold",
    )(message, after)


def attend_kernel(group, context, order, *refs):
    returned_refs, refs = refs[: len(order)], refs[len(order) :]
    returned_refs = [returned_refs[order.index(s)] for s in range(len(order))]
    routed_ref, keys_ref, lens_ref, rest_hbm, out_hbm, *scratch = refs
    query_ref, values_ref, bias_ref, scores_ref, expo_ref, out_ref, sems = scratch
    step = ROWS_STEP
    steps, lines, cells = bias_ref.shape
    span = group * HEAD
    factor = LOG2E / jnp.sqrt(jnp.float32(HEAD))
    loads = [
        [
            pltpu.make_async_copy(
                rest_hbm.at[k, pl.ds(0, steps), pl.ds(cells, lines)], query_ref.at[k], sems.at[k, 1]
            ),
            pltpu.make_async_copy(
                rest_hbm.at[k, pl.ds(0, steps), pl.ds(0, cells)], values_ref.at[k], sems.at[k, 2]
            ),
        ]
        for k in range(KVH)
    ]
    stores = [
        pltpu.make_async_copy(
            out_ref.at[:, pl.ds(k * span, span)], out_hbm.at[:, pl.ds(k * span, span)], sems.at[k, 0]
        )
        for k in range(KVH)
    ]
    for load in loads:
        for copy in load:
            copy.start()
    lane = lax.broadcasted_iota(jnp.int32, (lines, cells), 1)
    line = lax.broadcasted_iota(jnp.int32, (lines, cells), 0)
    own = lax.div(lane, context) == lax.rem(line, step)
    position = lax.rem(lane, context)
    ones = jnp.ones((cells, HEAD), expo_ref.dtype)
    for i in range(steps):
        bias_ref[i] = jnp.where(own & (position < lens_ref[i]), 0.0, -jnp.inf)
    for k in range(KVH):
        delta = jnp.dot(
            routed_ref[...],
            stack(returned_refs, k * span, span),
            preferred_element_type=jnp.float32,
        )
        for copy in loads[k]:
            copy.wait()
        for i in range(steps):
            keys = keys_ref[k, :, i * cells : (i + 1) * cells]
            change = tall(delta[i * step : (i + 1) * step], group).astype(jnp.bfloat16)
            scores = jnp.dot(
                jnp.concatenate([query_ref[k, i], change], axis=1),
                jnp.concatenate([keys, keys], axis=0),
                preferred_element_type=jnp.float32,
            )
            scores_ref[k, i] = scores * factor + bias_ref[i]
        for i in range(steps):
            scores = scores_ref[k, i]
            expo = jnp.exp2(scores - jnp.max(scores, axis=1, keepdims=True))
            expo_ref[k, i] = expo.astype(expo_ref.dtype)
        for i in range(steps):
            rows = slice(i * step, (i + 1) * step)
            out = jnp.dot(
                expo_ref[k, i],
                jnp.concatenate([values_ref[k, i], ones], axis=1),
                preferred_element_type=jnp.float32,
            )
            out = out[:, :HEAD] * (1.0 / out[:, HEAD:])
            for g in range(group):
                out_ref[rows, (k * group + g) * HEAD : (k * group + g + 1) * HEAD] = out[
                    g * step : (g + 1) * step
                ].astype(out_ref.dtype)
        stores[k].start()
    for store in stores:
        store.wait()


def attend(routed, returned, order, keys, rest, lens, context):
    rows, width = routed.shape[0], returned[0].shape[1]
    group = width // (KVH * HEAD)
    step = ROWS_STEP
    steps = rows // step
    cells = step * context
    return pl.pallas_call(
        functools.partial(attend_kernel, group, context, order),
        in_specs=[pl.BlockSpec(memory_space=pltpu.VMEM)] * (3 + len(order)) + [pl.BlockSpec(memory_space=pl.ANY)],
        out_specs=pl.BlockSpec(memory_space=pl.ANY),
        out_shape=jax.ShapeDtypeStruct((rows, width), jnp.bfloat16),
        scratch_shapes=[
            pltpu.VMEM((KVH, steps, group * step, HEAD), rest.dtype),
            pltpu.VMEM((KVH, steps, cells, HEAD), rest.dtype),
            pltpu.VMEM((steps, group * step, cells), jnp.float32),
            pltpu.VMEM((KVH, steps, group * step, cells), jnp.float32),
            pltpu.VMEM((KVH, steps, group * step, cells), jnp.bfloat16),
            pltpu.VMEM((rows, width), jnp.bfloat16),
            pltpu.SemaphoreType.DMA((KVH, 3)),
        ],
        compiler_params=pltpu.CompilerParams(vmem_limit_bytes=GRANT),
        name="attend",
    )(*returned, routed, keys, lens, rest)


def on_device(hidden, adapter_id, adapter_slot, cache_len, base_q, kv_cache, a_maps, b_maps):
    owners = lax.axis_size("owner")
    rows = hidden.shape[0]
    held = a_maps.shape[1] // RANK
    slot_count = max(2, 2 * ((rows + 2 * owners - 1) // (2 * owners)))
    routed, *messages = pack(hidden, adapter_id, adapter_slot, owners, slot_count, held)
    half = owners // 2
    near = [*range(half // 2, half), *range(1, half // 2)]
    order = [s for pair in zip(range(half, owners), [*near, 0]) for s in pair]

    keys, rest, lens = prep(base_q, kv_cache, cache_len)
    messages[order[HELD]] = hold(messages[order[HELD]], rest)
    size = owners // GROUPS
    arrived = exchange(order, owners)(messages[s] for s in order)
    changes = []
    for at in range(0, owners, size):
        changes += adapt(arrived[at : at + size], a_maps, b_maps)
    returned = exchange(order, owners)(changes)
    return attend(routed, returned, order, keys, rest, lens, kv_cache.shape[2])


def exchange(order, owners):
    def permutes(messages):
        return [
            lax.ppermute(message, "owner", [(i, i ^ s) for i in range(owners)]) if s else message
            for message, s in zip(messages, order)
        ]

    def whole(messages):
        messages = dict(zip(order, messages))
        place = lax.axis_index("owner") ^ jnp.arange(owners, dtype=jnp.int32)
        blocks = jnp.stack([messages[s] for s in range(owners)])[place]
        blocks = lax.all_to_all(blocks, "owner", split_axis=0, concat_axis=0, tiled=True)[place]
        return [blocks[s] for s in order]

    return permutes if owners <= MOST_PERMUTES else whole


def solution(mesh):
    return jax.shard_map(
        on_device,
        mesh=mesh,
        in_specs=(
            P(("groups", "owner"), None),
            P(("groups", "owner")),
            P("groups"),
            P(("groups", "owner")),
            P(("groups", "owner"), None),
            P(("groups", "owner"), None, None, None),
            P(None, "owner"),
            P("owner", None),
        ),
        out_specs=P(("groups", "owner"), None),
        check_vma=False,
    )
```

```python
import functools

import jax
import jax.numpy as jnp
from jax import lax
from jax.experimental import pallas as pl
from jax.experimental.pallas import tpu as pltpu
from jax.sharding import PartitionSpec as P

HEAD = 128
KVH = 4
RANK = 64
LANES = 128
SCALE = 2.0
ROWS_STEP = 8
PREP_STEPS = 4
GROUPS = 4
HELD = 13
MOST_PERMUTES = 32
COLUMNS_STEP = 1024
ADAPT_STEP = 2048
OUT_STEP = 1024
GRANT = 48 * 2**20
LOG2E = 1.4426950408889634
TALL_BYTES = 17 * 2**20


def routing(owners, slot_count, held, slots, ids):
    rows = ids.shape[1]
    named = lax.broadcasted_iota(jnp.int32, (slots.shape[1], rows), 0) == ids
    slot = jnp.dot(
        slots.astype(jnp.float32).astype(jnp.bfloat16),
        named.astype(jnp.bfloat16),
        preferred_element_type=jnp.float32,
    ).astype(jnp.int32)
    owner = lax.div(slot, held)
    local = slot - owner * held
    hits = owner == lax.broadcasted_iota(jnp.int32, (owners, rows), 0)
    earlier = lax.broadcasted_iota(jnp.int32, (rows, rows), 0) < lax.broadcasted_iota(
        jnp.int32, (rows, rows), 1
    )
    before = jnp.dot(
        hits.astype(jnp.bfloat16), earlier.astype(jnp.bfloat16), preferred_element_type=jnp.float32
    )
    place = jnp.sum(jnp.where(hits, before, 0.0), axis=0, keepdims=True).astype(jnp.int32)
    line = lax.broadcasted_iota(jnp.int32, (owners * slot_count, rows), 0)
    apart = owner ^ lax.axis_index("owner")
    routed = line == apart * slot_count + place
    label = jnp.sum(jnp.where(routed, local.astype(jnp.float32), 0.0), axis=1, keepdims=True)
    return routed, label


def pack_kernel(owners, slot_count, held, slots_hbm, ids_hbm, hidden_hbm, routed_ref, *refs):
    message_refs, (slots_ref, ids_ref, rows_ref, small_sems, sems) = refs[:owners], refs[owners:]
    width = rows_ref.shape[1]
    spans = [(at, min(COLUMNS_STEP, width - at)) for at in range(0, width, COLUMNS_STEP)]
    small = [
        pltpu.make_async_copy(slots_hbm, slots_ref, small_sems.at[0]),
        pltpu.make_async_copy(ids_hbm, ids_ref, small_sems.at[1]),
    ]
    loads = [
        pltpu.make_async_copy(
            hidden_hbm.at[:, pl.ds(at, size)], rows_ref.at[:, pl.ds(at, size)], sems.at[i]
        )
        for i, (at, size) in enumerate(spans)
    ]
    for copy in [*small, *loads]:
        copy.start()
    for copy in small:
        copy.wait()
    routed, label = routing(owners, slot_count, held, slots_ref[...], ids_ref[...])
    routed_ref[...] = jnp.transpose(routed.astype(jnp.float32)).astype(routed_ref.dtype)
    routed = routed.astype(jnp.bfloat16)

    def put(at, lines):
        for i, message_ref in enumerate(message_refs):
            message_ref[:, at : at + lines.shape[1]] = lines[
                i * slot_count : (i + 1) * slot_count
            ].astype(message_ref.dtype)

    put(width, jnp.broadcast_to(label, (label.shape[0], LANES)))
    for load, (at, size) in zip(loads, spans):
        load.wait()
        put(at, jnp.dot(routed, rows_ref[:, at : at + size], preferred_element_type=jnp.float32))


def pack(hidden, adapter_id, adapter_slot, owners, slot_count, held):
    rows, width = hidden.shape
    bins = owners * slot_count
    steps = pl.cdiv(width, COLUMNS_STEP)
    slots = adapter_slot.reshape(1, -1)
    return pl.pallas_call(
        functools.partial(pack_kernel, owners, slot_count, held),
        in_specs=[pl.BlockSpec(memory_space=pl.ANY)] * 3,
        out_specs=[pl.BlockSpec(memory_space=pltpu.VMEM)] * (1 + owners),
        out_shape=[jax.ShapeDtypeStruct((rows, bins), jnp.bfloat16)]
        + [jax.ShapeDtypeStruct((slot_count, width + LANES), hidden.dtype)] * owners,
        scratch_shapes=[
            pltpu.VMEM(slots.shape, jnp.int32),
            pltpu.VMEM((1, rows), jnp.int32),
            pltpu.VMEM((rows, width), hidden.dtype),
            pltpu.SemaphoreType.DMA((2,)),
            pltpu.SemaphoreType.DMA((steps,)),
        ],
        compiler_params=pltpu.CompilerParams(vmem_limit_bytes=56 * 2**20),
        name="pack",
    )(slots, adapter_id.reshape(1, rows), hidden)


def stack(refs, at, size):
    return jnp.concatenate(
        [ref[:, at : at + size].astype(jnp.float32) for ref in refs], axis=0
    ).astype(jnp.bfloat16)


def adapt_kernel(count, *refs):
    arrived_refs, (a_ref, b_ref), change_refs = refs[:count], refs[count : count + 2], refs[-count:]
    width = a_ref.shape[0]
    slot_count = arrived_refs[0].shape[0]
    low = jnp.zeros((count * slot_count, a_ref.shape[1]), jnp.float32)
    for at in range(0, width, ADAPT_STEP):
        low += jnp.dot(
            stack(arrived_refs, at, ADAPT_STEP),
            a_ref[at : at + ADAPT_STEP, :],
            preferred_element_type=jnp.float32,
        )
    label = stack(arrived_refs, width, LANES).astype(jnp.float32)[:, :1].astype(jnp.int32)
    column = lax.broadcasted_iota(jnp.int32, low.shape, 1) // RANK
    low = jnp.where(column == label, low, 0.0).astype(jnp.bfloat16)
    for at in range(0, b_ref.shape[1], OUT_STEP):
        change = SCALE * jnp.dot(low, b_ref[:, at : at + OUT_STEP], preferred_element_type=jnp.float32)
        for i, change_ref in enumerate(change_refs):
            change_ref[:, at : at + OUT_STEP] = change[
                i * slot_count : (i + 1) * slot_count
            ].astype(change_ref.dtype)


def adapt(arrived, a_maps, b_maps):
    count = len(arrived)
    change = jax.ShapeDtypeStruct((arrived[0].shape[0], b_maps.shape[1]), jnp.bfloat16)
    return pl.pallas_call(
        functools.partial(adapt_kernel, count),
        in_specs=[pl.BlockSpec(memory_space=pltpu.VMEM)] * (count + 2),
        out_specs=[pl.BlockSpec(memory_space=pltpu.VMEM)] * count,
        out_shape=[change] * count,
        compiler_params=pltpu.CompilerParams(vmem_limit_bytes=GRANT),
        name="adapt",
    )(*arrived, a_maps, b_maps)


def tall(rows, group):
    return jnp.concatenate([rows[:, g * HEAD : (g + 1) * HEAD] for g in range(group)], axis=0)


def prep_kernel(group, base_ref, kv_ref, given_ref, keys_ref, rest_ref, lens_ref):
    lens_ref[...] = given_ref[...]
    step, context = ROWS_STEP, kv_ref.shape[2]
    cells = step * context
    for j in range(PREP_STEPS):
        rows = slice(j * step, (j + 1) * step)
        for k in range(KVH):
            head = slice(k * HEAD, (k + 1) * HEAD)
            keys = kv_ref[rows, 0, :, head].astype(jnp.float32).reshape(cells, HEAD)
            keys_ref[k, :, j * cells : (j + 1) * cells] = jnp.transpose(keys).astype(keys_ref.dtype)
            rest_ref[k, j, :cells] = kv_ref[rows, 1, :, head].reshape(cells, HEAD)
            base = base_ref[:, k * group * HEAD : (k + 1) * group * HEAD].astype(jnp.float32)
            rest_ref[k, j, cells:] = tall(base[rows], group).astype(rest_ref.dtype)


def prep(base_q, kv_cache, cache_len):
    rows, width = base_q.shape
    context = kv_cache.shape[2]
    group = width // (KVH * HEAD)
    step = ROWS_STEP * PREP_STEPS
    steps = rows // step
    cells = ROWS_STEP * context
    lines = cells + group * ROWS_STEP
    lens = jnp.repeat(cache_len, context).reshape(rows // ROWS_STEP, 1, cells)
    length = max(pl.cdiv(TALL_BYTES, 2 * KVH * lines * HEAD * PREP_STEPS), steps) * PREP_STEPS
    return pl.pallas_call(
        functools.partial(prep_kernel, group),
        grid=(steps,),
        in_specs=[
            pl.BlockSpec((step, width), lambda i: (i, 0)),
            pl.BlockSpec((step, *kv_cache.shape[1:]), lambda i: (i, 0, 0, 0)),
            pl.BlockSpec((PREP_STEPS, 1, cells), lambda i: (i, 0, 0)),
        ],
        out_specs=[
            pl.BlockSpec((KVH, HEAD, PREP_STEPS * cells), lambda i: (0, 0, i)),
            pl.BlockSpec((KVH, PREP_STEPS, lines, HEAD), lambda i: (0, i, 0, 0)),
            pl.BlockSpec((PREP_STEPS, 1, cells), lambda i: (i, 0, 0)),
        ],
        out_shape=[
            jax.ShapeDtypeStruct((KVH, HEAD, rows * context), jnp.bfloat16),
            jax.ShapeDtypeStruct((KVH, length, lines, HEAD), jnp.bfloat16),
            jax.ShapeDtypeStruct(lens.shape, lens.dtype),
        ],
        compiler_params=pltpu.CompilerParams(vmem_limit_bytes=GRANT),
        name="prep",
    )(base_q, kv_cache, lens)


def hold_kernel(*refs):
    del refs


def hold(message, after):
    return pl.pallas_call(
        hold_kernel,
        in_specs=[pl.BlockSpec(memory_space=pl.ANY)] * 2,
        out_specs=pl.BlockSpec(memory_space=pl.ANY),
        out_shape=jax.ShapeDtypeStruct(message.shape, message.dtype),
        input_output_aliases={0: 0},
        compiler_params=pltpu.CompilerParams(vmem_limit_bytes=GRANT),
        name="hold",
    )(message, after)


def attend_kernel(group, context, order, *refs):
    returned_refs, refs = refs[: len(order)], refs[len(order) :]
    returned_refs = [returned_refs[order.index(s)] for s in range(len(order))]
    routed_ref, keys_ref, lens_ref, rest_hbm, out_hbm, *scratch = refs
    query_ref, values_ref, bias_ref, scores_ref, expo_ref, out_ref, sems = scratch
    step = ROWS_STEP
    steps, lines, cells = bias_ref.shape
    span = group * HEAD
    factor = LOG2E / jnp.sqrt(jnp.float32(HEAD))
    loads = [
        [
            pltpu.make_async_copy(
                rest_hbm.at[k, pl.ds(0, steps), pl.ds(cells, lines)], query_ref.at[k], sems.at[k, 1]
            ),
            pltpu.make_async_copy(
                rest_hbm.at[k, pl.ds(0, steps), pl.ds(0, cells)], values_ref.at[k], sems.at[k, 2]
            ),
        ]
        for k in range(KVH)
    ]
    stores = [
        pltpu.make_async_copy(
            out_ref.at[:, pl.ds(k * span, span)], out_hbm.at[:, pl.ds(k * span, span)], sems.at[k, 0]
        )
        for k in range(KVH)
    ]
    for load in loads:
        for copy in load:
            copy.start()
    lane = lax.broadcasted_iota(jnp.int32, (lines, cells), 1)
    line = lax.broadcasted_iota(jnp.int32, (lines, cells), 0)
    own = lax.div(lane, context) == lax.rem(line, step)
    position = lax.rem(lane, context)
    ones = jnp.ones((cells, HEAD), expo_ref.dtype)
    for i in range(steps):
        bias_ref[i] = jnp.where(own & (position < lens_ref[i]), 0.0, -jnp.inf)
    for k in range(KVH):
        delta = jnp.dot(
            routed_ref[...],
            stack(returned_refs, k * span, span),
            preferred_element_type=jnp.float32,
        )
        for copy in loads[k]:
            copy.wait()
        for i in range(steps):
            keys = keys_ref[k, :, i * cells : (i + 1) * cells]
            change = tall(delta[i * step : (i + 1) * step], group).astype(jnp.bfloat16)
            scores = jnp.dot(
                jnp.concatenate([query_ref[k, i], change], axis=1),
                jnp.concatenate([keys, keys], axis=0),
                preferred_element_type=jnp.float32,
            )
            scores_ref[k, i] = scores * factor + bias_ref[i]
        for i in range(steps):
            scores = scores_ref[k, i]
            expo = jnp.exp2(scores - jnp.max(scores, axis=1, keepdims=True))
            expo_ref[k, i] = expo.astype(expo_ref.dtype)
        for i in range(steps):
            rows = slice(i * step, (i + 1) * step)
            out = jnp.dot(
                expo_ref[k, i],
                jnp.concatenate([values_ref[k, i], ones], axis=1),
                preferred_element_type=jnp.float32,
            )
            out = out[:, :HEAD] * (1.0 / out[:, HEAD:])
            for g in range(group):
                out_ref[rows, (k * group + g) * HEAD : (k * group + g + 1) * HEAD] = out[
                    g * step : (g + 1) * step
                ].astype(out_ref.dtype)
        stores[k].start()
    for store in stores:
        store.wait()


def attend(routed, returned, order, keys, rest, lens, context):
    rows, width = routed.shape[0], returned[0].shape[1]
    group = width // (KVH * HEAD)
    step = ROWS_STEP
    steps = rows // step
    cells = step * context
    return pl.pallas_call(
        functools.partial(attend_kernel, group, context, order),
        in_specs=[pl.BlockSpec(memory_space=pltpu.VMEM)] * (3 + len(order)) + [pl.BlockSpec(memory_space=pl.ANY)],
        out_specs=pl.BlockSpec(memory_space=pl.ANY),
        out_shape=jax.ShapeDtypeStruct((rows, width), jnp.bfloat16),
        scratch_shapes=[
            pltpu.VMEM((KVH, steps, group * step, HEAD), rest.dtype),
            pltpu.VMEM((KVH, steps, cells, HEAD), rest.dtype),
            pltpu.VMEM((steps, group * step, cells), jnp.float32),
            pltpu.VMEM((KVH, steps, group * step, cells), jnp.float32),
            pltpu.VMEM((KVH, steps, group * step, cells), jnp.bfloat16),
            pltpu.VMEM((rows, width), jnp.bfloat16),
            pltpu.SemaphoreType.DMA((KVH, 3)),
        ],
        compiler_params=pltpu.CompilerParams(vmem_limit_bytes=GRANT),
        name="attend",
    )(*returned, routed, keys, lens, rest)


def on_device(hidden, adapter_id, adapter_slot, cache_len, base_q, kv_cache, a_maps, b_maps):
    owners = lax.axis_size("owner")
    rows = hidden.shape[0]
    held = a_maps.shape[1] // RANK
    slot_count = max(2, 2 * ((rows + 2 * owners - 1) // (2 * owners)))
    routed, *messages = pack(hidden, adapter_id, adapter_slot, owners, slot_count, held)
    half = owners // 2
    near = [*range(half // 2, half), *range(1, half // 2)]
    order = [s for pair in zip(range(half, owners), [*near, 0]) for s in pair]

    keys, rest, lens = prep(base_q, kv_cache, cache_len)
    messages[order[HELD]] = hold(messages[order[HELD]], rest)
    size = owners // GROUPS
    arrived = exchange(order, owners)(messages[s] for s in order)
    changes = []
    for at in range(0, owners, size):
        changes += adapt(arrived[at : at + size], a_maps, b_maps)
    returned = exchange(order, owners)(changes)
    return attend(routed, returned, order, keys, rest, lens, kv_cache.shape[2])


def exchange(order, owners):
    def permutes(messages):
        return [
            lax.ppermute(message, "owner", [(i, i ^ s) for i in range(owners)]) if s else message
            for message, s in zip(messages, order)
        ]

    def whole(messages):
        messages = dict(zip(order, messages))
        place = lax.axis_index("owner") ^ jnp.arange(owners, dtype=jnp.int32)
        blocks = jnp.stack([messages[s] for s in range(owners)])[place]
        blocks = lax.all_to_all(blocks, "owner", split_axis=0, concat_axis=0, tiled=True)[place]
        return [blocks[s] for s in order]

    return permutes if owners <= MOST_PERMUTES else whole


def solution(mesh):
    return jax.shard_map(
        on_device,
        mesh=mesh,
        in_specs=(
            P(("groups", "owner"), None),
            P(("groups", "owner")),
            P("groups"),
            P(("groups", "owner")),
            P(("groups", "owner"), None),
            P(("groups", "owner"), None, None, None),
            P(None, "owner"),
            P("owner", None),
        ),
        out_specs=P(("groups", "owner"), None),
        check_vma=False,
    )
```

```python
import functools

import jax
import jax.numpy as jnp
from jax import lax
from jax.experimental import pallas as pl
from jax.experimental.pallas import tpu as pltpu
from jax.sharding import PartitionSpec as P

HEAD = 128
KVH = 4
RANK = 64
LANES = 128
SCALE = 2.0
ROWS_STEP = 8
PREP_STEPS = 4
GROUPS = 4
HELD = 13
FIRST = 4
MOST_PERMUTES = 32
COLUMNS_STEP = 1024
ADAPT_STEP = 2048
OUT_STEP = 1024
GRANT = 48 * 2**20
LOG2E = 1.4426950408889634
TALL_BYTES = 17 * 2**20


def routing(which, owners, slot_count, held, slots, ids):
    rows = ids.shape[1]
    named = lax.broadcasted_iota(jnp.int32, (slots.shape[1], rows), 0) == ids
    slot = jnp.dot(
        slots.astype(jnp.float32).astype(jnp.bfloat16),
        named.astype(jnp.bfloat16),
        preferred_element_type=jnp.float32,
    ).astype(jnp.int32)
    owner = lax.div(slot, held)
    local = slot - owner * held
    hits = owner == lax.broadcasted_iota(jnp.int32, (owners, rows), 0)
    earlier = lax.broadcasted_iota(jnp.int32, (rows, rows), 0) < lax.broadcasted_iota(
        jnp.int32, (rows, rows), 1
    )
    before = jnp.dot(
        hits.astype(jnp.bfloat16), earlier.astype(jnp.bfloat16), preferred_element_type=jnp.float32
    )
    place = jnp.sum(jnp.where(hits, before, 0.0), axis=0, keepdims=True).astype(jnp.int32)
    apart = owner ^ lax.axis_index("owner")
    target = jnp.full_like(apart, -1)
    for j, s in enumerate(which):
        target = jnp.where(apart == s, j * slot_count + place, target)
    routed = target == lax.broadcasted_iota(jnp.int32, (len(which) * slot_count, rows), 0)
    label = jnp.sum(jnp.where(routed, local.astype(jnp.float32), 0.0), axis=1, keepdims=True)
    return routed, label


def pack_kernel(which, owners, slot_count, held, slots_hbm, ids_hbm, hidden_hbm, routed_ref, *refs):
    message_refs, refs = refs[: len(which)], refs[len(which) :]
    slots_ref, ids_ref, rows_ref, small_sems, sems = refs
    width = rows_ref.shape[1]
    spans = [(at, min(COLUMNS_STEP, width - at)) for at in range(0, width, COLUMNS_STEP)]
    small = [
        pltpu.make_async_copy(slots_hbm, slots_ref, small_sems.at[0]),
        pltpu.make_async_copy(ids_hbm, ids_ref, small_sems.at[1]),
    ]
    loads = [
        pltpu.make_async_copy(
            hidden_hbm.at[:, pl.ds(at, size)], rows_ref.at[:, pl.ds(at, size)], sems.at[i]
        )
        for i, (at, size) in enumerate(spans)
    ]
    for copy in [*small, *loads]:
        copy.start()
    for copy in small:
        copy.wait()
    routed, label = routing(which, owners, slot_count, held, slots_ref[...], ids_ref[...])
    routed = routed.astype(jnp.bfloat16)
    routed_ref[...] = routed

    def put(at, lines):
        for i, message_ref in enumerate(message_refs):
            message_ref[:, at : at + lines.shape[1]] = lines[
                i * slot_count : (i + 1) * slot_count
            ].astype(message_ref.dtype)

    put(width, jnp.broadcast_to(label, (label.shape[0], LANES)))
    for load, (at, size) in zip(loads, spans):
        load.wait()
        put(at, jnp.dot(routed, rows_ref[:, at : at + size], preferred_element_type=jnp.float32))


def pack(which, hidden, adapter_id, adapter_slot, owners, slot_count, held):
    rows, width = hidden.shape
    lines = len(which) * slot_count
    steps = pl.cdiv(width, COLUMNS_STEP)
    slots = adapter_slot.reshape(1, -1)
    return pl.pallas_call(
        functools.partial(pack_kernel, which, owners, slot_count, held),
        in_specs=[pl.BlockSpec(memory_space=pl.ANY)] * 3,
        out_specs=[pl.BlockSpec(memory_space=pltpu.VMEM)] * (1 + len(which)),
        out_shape=[jax.ShapeDtypeStruct((lines, rows), jnp.bfloat16)]
        + [jax.ShapeDtypeStruct((slot_count, width + LANES), hidden.dtype)] * len(which),
        scratch_shapes=[
            pltpu.VMEM(slots.shape, jnp.int32),
            pltpu.VMEM((1, rows), jnp.int32),
            pltpu.VMEM((rows, width), hidden.dtype),
            pltpu.SemaphoreType.DMA((2,)),
            pltpu.SemaphoreType.DMA((steps,)),
        ],
        compiler_params=pltpu.CompilerParams(vmem_limit_bytes=56 * 2**20),
        name="pack",
    )(slots, adapter_id.reshape(1, rows), hidden)


def stack(refs, at, size):
    return jnp.concatenate(
        [ref[:, at : at + size].astype(jnp.float32) for ref in refs], axis=0
    ).astype(jnp.bfloat16)


def adapt_kernel(count, *refs):
    arrived_refs, (a_ref, b_ref), change_refs = refs[:count], refs[count : count + 2], refs[-count:]
    width = a_ref.shape[0]
    slot_count = arrived_refs[0].shape[0]
    low = jnp.zeros((count * slot_count, a_ref.shape[1]), jnp.float32)
    for at in range(0, width, ADAPT_STEP):
        low += jnp.dot(
            stack(arrived_refs, at, ADAPT_STEP),
            a_ref[at : at + ADAPT_STEP, :],
            preferred_element_type=jnp.float32,
        )
    label = stack(arrived_refs, width, LANES).astype(jnp.float32)[:, :1].astype(jnp.int32)
    column = lax.broadcasted_iota(jnp.int32, low.shape, 1) // RANK
    low = jnp.where(column == label, low, 0.0).astype(jnp.bfloat16)
    for at in range(0, b_ref.shape[1], OUT_STEP):
        change = SCALE * jnp.dot(low, b_ref[:, at : at + OUT_STEP], preferred_element_type=jnp.float32)
        for i, change_ref in enumerate(change_refs):
            change_ref[:, at : at + OUT_STEP] = change[
                i * slot_count : (i + 1) * slot_count
            ].astype(change_ref.dtype)


def adapt(arrived, a_maps, b_maps):
    count = len(arrived)
    change = jax.ShapeDtypeStruct((arrived[0].shape[0], b_maps.shape[1]), jnp.bfloat16)
    return pl.pallas_call(
        functools.partial(adapt_kernel, count),
        in_specs=[pl.BlockSpec(memory_space=pltpu.VMEM)] * (count + 2),
        out_specs=[pl.BlockSpec(memory_space=pltpu.VMEM)] * count,
        out_shape=[change] * count,
        compiler_params=pltpu.CompilerParams(vmem_limit_bytes=GRANT),
        name="adapt",
    )(*arrived, a_maps, b_maps)


def tall(rows, group):
    return jnp.concatenate([rows[:, g * HEAD : (g + 1) * HEAD] for g in range(group)], axis=0)


def prep_kernel(group, base_ref, kv_ref, given_ref, keys_ref, rest_ref, lens_ref):
    lens_ref[...] = given_ref[...]
    step, context = ROWS_STEP, kv_ref.shape[2]
    cells = step * context
    for j in range(PREP_STEPS):
        rows = slice(j * step, (j + 1) * step)
        for k in range(KVH):
            head = slice(k * HEAD, (k + 1) * HEAD)
            keys = kv_ref[rows, 0, :, head].astype(jnp.float32).reshape(cells, HEAD)
            keys_ref[k, :, j * cells : (j + 1) * cells] = jnp.transpose(keys).astype(keys_ref.dtype)
            rest_ref[k, j, :cells] = kv_ref[rows, 1, :, head].reshape(cells, HEAD)
            base = base_ref[:, k * group * HEAD : (k + 1) * group * HEAD].astype(jnp.float32)
            rest_ref[k, j, cells:] = tall(base[rows], group).astype(rest_ref.dtype)


def prep(base_q, kv_cache, cache_len):
    rows, width = base_q.shape
    context = kv_cache.shape[2]
    group = width // (KVH * HEAD)
    step = ROWS_STEP * PREP_STEPS
    steps = rows // step
    cells = ROWS_STEP * context
    lines = cells + group * ROWS_STEP
    lens = jnp.repeat(cache_len, context).reshape(rows // ROWS_STEP, 1, cells)
    length = max(pl.cdiv(TALL_BYTES, 2 * KVH * lines * HEAD * PREP_STEPS), steps) * PREP_STEPS
    return pl.pallas_call(
        functools.partial(prep_kernel, group),
        grid=(steps,),
        in_specs=[
            pl.BlockSpec((step, width), lambda i: (i, 0)),
            pl.BlockSpec((step, *kv_cache.shape[1:]), lambda i: (i, 0, 0, 0)),
            pl.BlockSpec((PREP_STEPS, 1, cells), lambda i: (i, 0, 0)),
        ],
        out_specs=[
            pl.BlockSpec((KVH, HEAD, PREP_STEPS * cells), lambda i: (0, 0, i)),
            pl.BlockSpec((KVH, PREP_STEPS, lines, HEAD), lambda i: (0, i, 0, 0)),
            pl.BlockSpec((PREP_STEPS, 1, cells), lambda i: (i, 0, 0)),
        ],
        out_shape=[
            jax.ShapeDtypeStruct((KVH, HEAD, rows * context), jnp.bfloat16),
            jax.ShapeDtypeStruct((KVH, length, lines, HEAD), jnp.bfloat16),
            jax.ShapeDtypeStruct(lens.shape, lens.dtype),
        ],
        compiler_params=pltpu.CompilerParams(vmem_limit_bytes=GRANT),
        name="prep",
    )(base_q, kv_cache, lens)


def hold_kernel(*refs):
    del refs


def hold(message, after):
    return pl.pallas_call(
        hold_kernel,
        in_specs=[pl.BlockSpec(memory_space=pl.ANY)] * 2,
        out_specs=pl.BlockSpec(memory_space=pl.ANY),
        out_shape=jax.ShapeDtypeStruct(message.shape, message.dtype),
        input_output_aliases={0: 0},
        compiler_params=pltpu.CompilerParams(vmem_limit_bytes=GRANT),
        name="hold",
    )(message, after)


def attend_kernel(group, context, count, *refs):
    returned_refs, routed_refs, refs = refs[:count], refs[count : count + 2], refs[count + 2 :]
    keys_ref, lens_ref, rest_hbm, out_hbm, *scratch = refs
    query_ref, values_ref, bias_ref, scores_ref, expo_ref, out_ref, sems = scratch
    step = ROWS_STEP
    steps, lines, cells = bias_ref.shape
    span = group * HEAD
    factor = LOG2E / jnp.sqrt(jnp.float32(HEAD))
    loads = [
        [
            pltpu.make_async_copy(
                rest_hbm.at[k, pl.ds(0, steps), pl.ds(cells, lines)], query_ref.at[k], sems.at[k, 1]
            ),
            pltpu.make_async_copy(
                rest_hbm.at[k, pl.ds(0, steps), pl.ds(0, cells)], values_ref.at[k], sems.at[k, 2]
            ),
        ]
        for k in range(KVH)
    ]
    stores = [
        pltpu.make_async_copy(
            out_ref.at[:, pl.ds(k * span, span)], out_hbm.at[:, pl.ds(k * span, span)], sems.at[k, 0]
        )
        for k in range(KVH)
    ]
    for load in loads:
        for copy in load:
            copy.start()
    lane = lax.broadcasted_iota(jnp.int32, (lines, cells), 1)
    line = lax.broadcasted_iota(jnp.int32, (lines, cells), 0)
    own = lax.div(lane, context) == lax.rem(line, step)
    position = lax.rem(lane, context)
    ones = jnp.ones((cells, HEAD), expo_ref.dtype)
    for i in range(steps):
        bias_ref[i] = jnp.where(own & (position < lens_ref[i]), 0.0, -jnp.inf)
    routed = jnp.concatenate([ref[...].astype(jnp.float32) for ref in routed_refs], axis=0)
    routed = jnp.transpose(routed).astype(jnp.bfloat16)
    for k in range(KVH):
        delta = jnp.dot(
            routed,
            stack(returned_refs, k * span, span),
            preferred_element_type=jnp.float32,
        )
        for copy in loads[k]:
            copy.wait()
        for i in range(steps):
            keys = keys_ref[k, :, i * cells : (i + 1) * cells]
            change = tall(delta[i * step : (i + 1) * step], group).astype(jnp.bfloat16)
            scores = jnp.dot(
                jnp.concatenate([query_ref[k, i], change], axis=1),
                jnp.concatenate([keys, keys], axis=0),
                preferred_element_type=jnp.float32,
            )
            scores_ref[k, i] = scores * factor + bias_ref[i]
        for i in range(steps):
            scores = scores_ref[k, i]
            expo = jnp.exp2(scores - jnp.max(scores, axis=1, keepdims=True))
            expo_ref[k, i] = expo.astype(expo_ref.dtype)
        for i in range(steps):
            rows = slice(i * step, (i + 1) * step)
            out = jnp.dot(
                expo_ref[k, i],
                jnp.concatenate([values_ref[k, i], ones], axis=1),
                preferred_element_type=jnp.float32,
            )
            out = out[:, :HEAD] * (1.0 / out[:, HEAD:])
            for g in range(group):
                out_ref[rows, (k * group + g) * HEAD : (k * group + g + 1) * HEAD] = out[
                    g * step : (g + 1) * step
                ].astype(out_ref.dtype)
        stores[k].start()
    for store in stores:
        store.wait()


def attend(routed, returned, keys, rest, lens, context):
    rows, width = routed[0].shape[1], returned[0].shape[1]
    group = width // (KVH * HEAD)
    step = ROWS_STEP
    steps = rows // step
    cells = step * context
    return pl.pallas_call(
        functools.partial(attend_kernel, group, context, len(returned)),
        in_specs=[pl.BlockSpec(memory_space=pltpu.VMEM)] * (4 + len(returned)) + [pl.BlockSpec(memory_space=pl.ANY)],
        out_specs=pl.BlockSpec(memory_space=pl.ANY),
        out_shape=jax.ShapeDtypeStruct((rows, width), jnp.bfloat16),
        scratch_shapes=[
            pltpu.VMEM((KVH, steps, group * step, HEAD), rest.dtype),
            pltpu.VMEM((KVH, steps, cells, HEAD), rest.dtype),
            pltpu.VMEM((steps, group * step, cells), jnp.float32),
            pltpu.VMEM((KVH, steps, group * step, cells), jnp.float32),
            pltpu.VMEM((KVH, steps, group * step, cells), jnp.bfloat16),
            pltpu.VMEM((rows, width), jnp.bfloat16),
            pltpu.SemaphoreType.DMA((KVH, 3)),
        ],
        compiler_params=pltpu.CompilerParams(vmem_limit_bytes=GRANT),
        name="attend",
    )(*returned, *routed, keys, lens, rest)


def on_device(hidden, adapter_id, adapter_slot, cache_len, base_q, kv_cache, a_maps, b_maps):
    owners = lax.axis_size("owner")
    rows = hidden.shape[0]
    held = a_maps.shape[1] // RANK
    slot_count = max(2, 2 * ((rows + 2 * owners - 1) // (2 * owners)))
    half = owners // 2
    near = [*range(half // 2, half), *range(1, half // 2)]
    order = [s for pair in zip(range(half, owners), [*near, 0]) for s in pair]

    routed, messages = [], []
    for which in (order[:FIRST], order[FIRST:]):
        hits, *packed = pack(which, hidden, adapter_id, adapter_slot, owners, slot_count, held)
        routed.append(hits)
        messages += packed
    keys, rest, lens = prep(base_q, kv_cache, cache_len)
    messages[HELD] = hold(messages[HELD], rest)
    size = owners // GROUPS
    arrived = exchange(order, owners)(messages)
    changes = []
    for at in range(0, owners, size):
        changes += adapt(arrived[at : at + size], a_maps, b_maps)
    returned = exchange(order, owners)(changes)
    return attend(routed, returned, keys, rest, lens, kv_cache.shape[2])


def exchange(order, owners):
    def permutes(messages):
        return [
            lax.ppermute(message, "owner", [(i, i ^ s) for i in range(owners)]) if s else message
            for message, s in zip(messages, order)
        ]

    def whole(messages):
        messages = dict(zip(order, messages))
        place = lax.axis_index("owner") ^ jnp.arange(owners, dtype=jnp.int32)
        blocks = jnp.stack([messages[s] for s in range(owners)])[place]
        blocks = lax.all_to_all(blocks, "owner", split_axis=0, concat_axis=0, tiled=True)[place]
        return [blocks[s] for s in order]

    return permutes if owners <= MOST_PERMUTES else whole


def solution(mesh):
    return jax.shard_map(
        on_device,
        mesh=mesh,
        in_specs=(
            P(("groups", "owner"), None),
            P(("groups", "owner")),
            P("groups"),
            P(("groups", "owner")),
            P(("groups", "owner"), None),
            P(("groups", "owner"), None, None, None),
            P(None, "owner"),
            P("owner", None),
        ),
        out_specs=P(("groups", "owner"), None),
        check_vma=False,
    )
```

```python
import functools

import jax
import jax.numpy as jnp
from jax import lax
from jax.experimental import pallas as pl
from jax.experimental.pallas import tpu as pltpu
from jax.sharding import PartitionSpec as P

HEAD = 128
KVH = 4
RANK = 64
LANES = 128
SCALE = 2.0
ROWS_STEP = 8
PREP_STEPS = 4
GROUPS = 4
LEAD = 3
FIRST = 4
MOST_PERMUTES = 32
COLUMNS_STEP = 1024
ADAPT_STEP = 2048
OUT_STEP = 1024
GRANT = 48 * 2**20
LOG2E = 1.4426950408889634
TALL_BYTES = 17 * 2**20


def routing(which, owners, slot_count, held, slots, ids):
    rows = ids.shape[1]
    named = lax.broadcasted_iota(jnp.int32, (slots.shape[1], rows), 0) == ids
    slot = jnp.dot(
        slots.astype(jnp.float32).astype(jnp.bfloat16),
        named.astype(jnp.bfloat16),
        preferred_element_type=jnp.float32,
    ).astype(jnp.int32)
    owner = lax.div(slot, held)
    local = slot - owner * held
    hits = owner == lax.broadcasted_iota(jnp.int32, (owners, rows), 0)
    earlier = lax.broadcasted_iota(jnp.int32, (rows, rows), 0) < lax.broadcasted_iota(
        jnp.int32, (rows, rows), 1
    )
    before = jnp.dot(
        hits.astype(jnp.bfloat16), earlier.astype(jnp.bfloat16), preferred_element_type=jnp.float32
    )
    place = jnp.sum(jnp.where(hits, before, 0.0), axis=0, keepdims=True).astype(jnp.int32)
    apart = owner ^ lax.axis_index("owner")
    target = jnp.full_like(apart, -1)
    for j, s in enumerate(which):
        target = jnp.where(apart == s, j * slot_count + place, target)
    routed = target == lax.broadcasted_iota(jnp.int32, (len(which) * slot_count, rows), 0)
    label = jnp.sum(jnp.where(routed, local.astype(jnp.float32), 0.0), axis=1, keepdims=True)
    return routed, label


def pack_kernel(which, owners, slot_count, held, slots_hbm, ids_hbm, hidden_hbm, routed_ref, *refs):
    message_refs, refs = refs[: len(which)], refs[len(which) :]
    slots_ref, ids_ref, rows_ref, small_sems, sems = refs
    width = rows_ref.shape[1]
    spans = [(at, min(COLUMNS_STEP, width - at)) for at in range(0, width, COLUMNS_STEP)]
    small = [
        pltpu.make_async_copy(slots_hbm, slots_ref, small_sems.at[0]),
        pltpu.make_async_copy(ids_hbm, ids_ref, small_sems.at[1]),
    ]
    loads = [
        pltpu.make_async_copy(
            hidden_hbm.at[:, pl.ds(at, size)], rows_ref.at[:, pl.ds(at, size)], sems.at[i]
        )
        for i, (at, size) in enumerate(spans)
    ]
    for copy in [*small, *loads]:
        copy.start()
    for copy in small:
        copy.wait()
    routed, label = routing(which, owners, slot_count, held, slots_ref[...], ids_ref[...])
    routed = routed.astype(jnp.bfloat16)
    routed_ref[...] = routed

    def put(at, lines):
        for i, message_ref in enumerate(message_refs):
            message_ref[:, at : at + lines.shape[1]] = lines[
                i * slot_count : (i + 1) * slot_count
            ].astype(message_ref.dtype)

    put(width, jnp.broadcast_to(label, (label.shape[0], LANES)))
    for load, (at, size) in zip(loads, spans):
        load.wait()
        put(at, jnp.dot(routed, rows_ref[:, at : at + size], preferred_element_type=jnp.float32))


def pack(which, hidden, adapter_id, adapter_slot, owners, slot_count, held):
    rows, width = hidden.shape
    lines = len(which) * slot_count
    steps = pl.cdiv(width, COLUMNS_STEP)
    slots = adapter_slot.reshape(1, -1)
    return pl.pallas_call(
        functools.partial(pack_kernel, which, owners, slot_count, held),
        in_specs=[pl.BlockSpec(memory_space=pl.ANY)] * 3,
        out_specs=[pl.BlockSpec(memory_space=pltpu.VMEM)] * (1 + len(which)),
        out_shape=[jax.ShapeDtypeStruct((lines, rows), jnp.bfloat16)]
        + [jax.ShapeDtypeStruct((slot_count, width + LANES), hidden.dtype)] * len(which),
        scratch_shapes=[
            pltpu.VMEM(slots.shape, jnp.int32),
            pltpu.VMEM((1, rows), jnp.int32),
            pltpu.VMEM((rows, width), hidden.dtype),
            pltpu.SemaphoreType.DMA((2,)),
            pltpu.SemaphoreType.DMA((steps,)),
        ],
        compiler_params=pltpu.CompilerParams(vmem_limit_bytes=56 * 2**20),
        name="pack",
    )(slots, adapter_id.reshape(1, rows), hidden)


def stack(refs, at, size):
    return jnp.concatenate(
        [ref[:, at : at + size].astype(jnp.float32) for ref in refs], axis=0
    ).astype(jnp.bfloat16)


def adapt_kernel(count, *refs):
    arrived_refs, (a_ref, b_ref), change_refs = refs[:count], refs[count : count + 2], refs[-count:]
    width = a_ref.shape[0]
    slot_count = arrived_refs[0].shape[0]
    low = jnp.zeros((count * slot_count, a_ref.shape[1]), jnp.float32)
    for at in range(0, width, ADAPT_STEP):
        low += jnp.dot(
            stack(arrived_refs, at, ADAPT_STEP),
            a_ref[at : at + ADAPT_STEP, :],
            preferred_element_type=jnp.float32,
        )
    label = stack(arrived_refs, width, LANES).astype(jnp.float32)[:, :1].astype(jnp.int32)
    column = lax.broadcasted_iota(jnp.int32, low.shape, 1) // RANK
    low = jnp.where(column == label, low, 0.0).astype(jnp.bfloat16)
    for at in range(0, b_ref.shape[1], OUT_STEP):
        change = SCALE * jnp.dot(low, b_ref[:, at : at + OUT_STEP], preferred_element_type=jnp.float32)
        for i, change_ref in enumerate(change_refs):
            change_ref[:, at : at + OUT_STEP] = change[
                i * slot_count : (i + 1) * slot_count
            ].astype(change_ref.dtype)


def adapt(arrived, a_maps, b_maps):
    count = len(arrived)
    change = jax.ShapeDtypeStruct((arrived[0].shape[0], b_maps.shape[1]), jnp.bfloat16)
    return pl.pallas_call(
        functools.partial(adapt_kernel, count),
        in_specs=[pl.BlockSpec(memory_space=pltpu.VMEM)] * (count + 2),
        out_specs=[pl.BlockSpec(memory_space=pltpu.VMEM)] * count,
        out_shape=[change] * count,
        compiler_params=pltpu.CompilerParams(vmem_limit_bytes=GRANT),
        name="adapt",
    )(*arrived, a_maps, b_maps)


def tall(rows, group):
    return jnp.concatenate([rows[:, g * HEAD : (g + 1) * HEAD] for g in range(group)], axis=0)


def prep_kernel(group, base_ref, kv_ref, given_ref, keys_ref, rest_ref, lens_ref):
    lens_ref[...] = given_ref[...]
    step, context = ROWS_STEP, kv_ref.shape[2]
    cells = step * context
    for j in range(PREP_STEPS):
        rows = slice(j * step, (j + 1) * step)
        for k in range(KVH):
            head = slice(k * HEAD, (k + 1) * HEAD)
            keys = kv_ref[rows, 0, :, head].astype(jnp.float32).reshape(cells, HEAD)
            keys_ref[k, :, j * cells : (j + 1) * cells] = jnp.transpose(keys).astype(keys_ref.dtype)
            rest_ref[k, j, :cells] = kv_ref[rows, 1, :, head].reshape(cells, HEAD)
            base = base_ref[:, k * group * HEAD : (k + 1) * group * HEAD].astype(jnp.float32)
            rest_ref[k, j, cells:] = tall(base[rows], group).astype(rest_ref.dtype)


def prep(base_q, kv_cache, cache_len):
    rows, width = base_q.shape
    context = kv_cache.shape[2]
    group = width // (KVH * HEAD)
    step = ROWS_STEP * PREP_STEPS
    steps = rows // step
    cells = ROWS_STEP * context
    lines = cells + group * ROWS_STEP
    lens = jnp.repeat(cache_len, context).reshape(rows // ROWS_STEP, 1, cells)
    length = max(pl.cdiv(TALL_BYTES, 2 * KVH * lines * HEAD * PREP_STEPS), steps) * PREP_STEPS
    return pl.pallas_call(
        functools.partial(prep_kernel, group),
        grid=(steps,),
        in_specs=[
            pl.BlockSpec((step, width), lambda i: (i, 0)),
            pl.BlockSpec((step, *kv_cache.shape[1:]), lambda i: (i, 0, 0, 0)),
            pl.BlockSpec((PREP_STEPS, 1, cells), lambda i: (i, 0, 0)),
        ],
        out_specs=[
            pl.BlockSpec((KVH, HEAD, PREP_STEPS * cells), lambda i: (0, 0, i)),
            pl.BlockSpec((KVH, PREP_STEPS, lines, HEAD), lambda i: (0, i, 0, 0)),
            pl.BlockSpec((PREP_STEPS, 1, cells), lambda i: (i, 0, 0)),
        ],
        out_shape=[
            jax.ShapeDtypeStruct((KVH, HEAD, rows * context), jnp.bfloat16),
            jax.ShapeDtypeStruct((KVH, length, lines, HEAD), jnp.bfloat16),
            jax.ShapeDtypeStruct(lens.shape, lens.dtype),
        ],
        compiler_params=pltpu.CompilerParams(vmem_limit_bytes=GRANT),
        name="prep",
    )(base_q, kv_cache, lens)


def hold_kernel(*refs):
    del refs


def hold(message, after):
    return pl.pallas_call(
        hold_kernel,
        in_specs=[pl.BlockSpec(memory_space=pl.ANY)] * 2,
        out_specs=pl.BlockSpec(memory_space=pl.ANY),
        out_shape=jax.ShapeDtypeStruct(message.shape, message.dtype),
        input_output_aliases={0: 0},
        compiler_params=pltpu.CompilerParams(vmem_limit_bytes=GRANT),
        name="hold",
    )(message, after)


def attend_kernel(group, context, count, *refs):
    returned_refs, routed_refs, refs = refs[:count], refs[count : count + 2], refs[count + 2 :]
    keys_ref, lens_ref, rest_hbm, out_hbm, *scratch = refs
    query_ref, values_ref, bias_ref, scores_ref, expo_ref, out_ref, sems = scratch
    step = ROWS_STEP
    steps, lines, cells = bias_ref.shape
    span = group * HEAD
    factor = LOG2E / jnp.sqrt(jnp.float32(HEAD))
    loads = [
        [
            pltpu.make_async_copy(
                rest_hbm.at[k, pl.ds(0, steps), pl.ds(cells, lines)], query_ref.at[k], sems.at[k, 1]
            ),
            pltpu.make_async_copy(
                rest_hbm.at[k, pl.ds(0, steps), pl.ds(0, cells)], values_ref.at[k], sems.at[k, 2]
            ),
        ]
        for k in range(KVH)
    ]
    stores = [
        pltpu.make_async_copy(
            out_ref.at[:, pl.ds(k * span, span)], out_hbm.at[:, pl.ds(k * span, span)], sems.at[k, 0]
        )
        for k in range(KVH)
    ]
    for load in loads:
        for copy in load:
            copy.start()
    lane = lax.broadcasted_iota(jnp.int32, (lines, cells), 1)
    line = lax.broadcasted_iota(jnp.int32, (lines, cells), 0)
    own = lax.div(lane, context) == lax.rem(line, step)
    position = lax.rem(lane, context)
    ones = jnp.ones((cells, HEAD), expo_ref.dtype)
    for i in range(steps):
        bias_ref[i] = jnp.where(own & (position < lens_ref[i]), 0.0, -jnp.inf)
    routed = jnp.concatenate([ref[...].astype(jnp.float32) for ref in routed_refs], axis=0)
    routed = jnp.transpose(routed).astype(jnp.bfloat16)
    for k in range(KVH):
        delta = jnp.dot(
            routed,
            stack(returned_refs, k * span, span),
            preferred_element_type=jnp.float32,
        )
        for copy in loads[k]:
            copy.wait()
        for i in range(steps):
            keys = keys_ref[k, :, i * cells : (i + 1) * cells]
            change = tall(delta[i * step : (i + 1) * step], group).astype(jnp.bfloat16)
            scores = jnp.dot(
                jnp.concatenate([query_ref[k, i], change], axis=1),
                jnp.concatenate([keys, keys], axis=0),
                preferred_element_type=jnp.float32,
            )
            scores_ref[k, i] = scores * factor + bias_ref[i]
        for i in range(steps):
            scores = scores_ref[k, i]
            expo = jnp.exp2(scores - jnp.max(scores, axis=1, keepdims=True))
            expo_ref[k, i] = expo.astype(expo_ref.dtype)
        for i in range(steps):
            rows = slice(i * step, (i + 1) * step)
            out = jnp.dot(
                expo_ref[k, i],
                jnp.concatenate([values_ref[k, i], ones], axis=1),
                preferred_element_type=jnp.float32,
            )
            out = out[:, :HEAD] * (1.0 / out[:, HEAD:])
            for g in range(group):
                out_ref[rows, (k * group + g) * HEAD : (k * group + g + 1) * HEAD] = out[
                    g * step : (g + 1) * step
                ].astype(out_ref.dtype)
        stores[k].start()
    for store in stores:
        store.wait()


def attend(routed, returned, keys, rest, lens, context):
    rows, width = routed[0].shape[1], returned[0].shape[1]
    group = width // (KVH * HEAD)
    step = ROWS_STEP
    steps = rows // step
    cells = step * context
    return pl.pallas_call(
        functools.partial(attend_kernel, group, context, len(returned)),
        in_specs=[pl.BlockSpec(memory_space=pltpu.VMEM)] * (4 + len(returned)) + [pl.BlockSpec(memory_space=pl.ANY)],
        out_specs=pl.BlockSpec(memory_space=pl.ANY),
        out_shape=jax.ShapeDtypeStruct((rows, width), jnp.bfloat16),
        scratch_shapes=[
            pltpu.VMEM((KVH, steps, group * step, HEAD), rest.dtype),
            pltpu.VMEM((KVH, steps, cells, HEAD), rest.dtype),
            pltpu.VMEM((steps, group * step, cells), jnp.float32),
            pltpu.VMEM((KVH, steps, group * step, cells), jnp.float32),
            pltpu.VMEM((KVH, steps, group * step, cells), jnp.bfloat16),
            pltpu.VMEM((rows, width), jnp.bfloat16),
            pltpu.SemaphoreType.DMA((KVH, 3)),
        ],
        compiler_params=pltpu.CompilerParams(vmem_limit_bytes=GRANT),
        name="attend",
    )(*returned, *routed, keys, lens, rest)


def on_device(hidden, adapter_id, adapter_slot, cache_len, base_q, kv_cache, a_maps, b_maps):
    owners = lax.axis_size("owner")
    rows = hidden.shape[0]
    held = a_maps.shape[1] // RANK
    slot_count = max(2, 2 * ((rows + 2 * owners - 1) // (2 * owners)))
    half = owners // 2
    near = [*range(half // 2, half), *range(1, half // 2)]
    far = [*range(half, owners)]
    order = far[:LEAD]
    for i, s in enumerate(near):
        order += [s, *far[LEAD + i : LEAD + i + 1]]
    order.append(0)
    routed, messages = [], []
    for which in (order[:FIRST], order[FIRST:]):
        hits, *packed = pack(which, hidden, adapter_id, adapter_slot, owners, slot_count, held)
        routed.append(hits)
        messages += packed
    keys, rest, lens = prep(base_q, kv_cache, cache_len)
    messages[-2] = hold(messages[-2], rest)
    size = owners // GROUPS
    arrived = exchange(order, owners)(messages)
    changes = []
    for at in range(0, owners, size):
        changes += adapt(arrived[at : at + size], a_maps, b_maps)
    returned = exchange(order, owners)(changes)
    return attend(routed, returned, keys, rest, lens, kv_cache.shape[2])


def exchange(order, owners):
    def permutes(messages):
        return [
            lax.ppermute(message, "owner", [(i, i ^ s) for i in range(owners)]) if s else message
            for message, s in zip(messages, order)
        ]

    def whole(messages):
        messages = dict(zip(order, messages))
        place = lax.axis_index("owner") ^ jnp.arange(owners, dtype=jnp.int32)
        blocks = jnp.stack([messages[s] for s in range(owners)])[place]
        blocks = lax.all_to_all(blocks, "owner", split_axis=0, concat_axis=0, tiled=True)[place]
        return [blocks[s] for s in order]

    return permutes if owners <= MOST_PERMUTES else whole


def solution(mesh):
    return jax.shard_map(
        on_device,
        mesh=mesh,
        in_specs=(
            P(("groups", "owner"), None),
            P(("groups", "owner")),
            P("groups"),
            P(("groups", "owner")),
            P(("groups", "owner"), None),
            P(("groups", "owner"), None, None, None),
            P(None, "owner"),
            P("owner", None),
        ),
        out_specs=P(("groups", "owner"), None),
        check_vma=False,
    )
```

```python
import functools

import jax
import jax.numpy as jnp
from jax import lax
from jax.experimental import pallas as pl
from jax.experimental.pallas import tpu as pltpu
from jax.sharding import PartitionSpec as P

HEAD = 128
KVH = 4
RANK = 64
LANES = 128
SCALE = 2.0
ROWS_STEP = 8
PREP_STEPS = 4
GROUPS = 4
FIRST = 4
MOST_PERMUTES = 32
COLUMNS_STEP = 1024
ADAPT_STEP = 2048
OUT_STEP = 1024
GRANT = 48 * 2**20
LOG2E = 1.4426950408889634
TALL_BYTES = 17 * 2**20


def routing(which, owners, slot_count, held, slots, ids):
    rows = ids.shape[1]
    named = lax.broadcasted_iota(jnp.int32, (slots.shape[1], rows), 0) == ids
    slot = jnp.dot(
        slots.astype(jnp.float32).astype(jnp.bfloat16),
        named.astype(jnp.bfloat16),
        preferred_element_type=jnp.float32,
    ).astype(jnp.int32)
    owner = lax.div(slot, held)
    local = slot - owner * held
    hits = owner == lax.broadcasted_iota(jnp.int32, (owners, rows), 0)
    earlier = lax.broadcasted_iota(jnp.int32, (rows, rows), 0) < lax.broadcasted_iota(
        jnp.int32, (rows, rows), 1
    )
    before = jnp.dot(
        hits.astype(jnp.bfloat16), earlier.astype(jnp.bfloat16), preferred_element_type=jnp.float32
    )
    place = jnp.sum(jnp.where(hits, before, 0.0), axis=0, keepdims=True).astype(jnp.int32)
    apart = owner ^ lax.axis_index("owner")
    target = jnp.full_like(apart, -1)
    for j, s in enumerate(which):
        target = jnp.where(apart == s, j * slot_count + place, target)
    routed = target == lax.broadcasted_iota(jnp.int32, (len(which) * slot_count, rows), 0)
    label = jnp.sum(jnp.where(routed, local.astype(jnp.float32), 0.0), axis=1, keepdims=True)
    return routed, label


def pack_kernel(which, owners, slot_count, held, slots_hbm, ids_hbm, hidden_hbm, routed_ref, *refs):
    message_refs, refs = refs[: len(which)], refs[len(which) :]
    slots_ref, ids_ref, rows_ref, small_sems, sems = refs
    width = rows_ref.shape[1]
    spans = [(at, min(COLUMNS_STEP, width - at)) for at in range(0, width, COLUMNS_STEP)]
    small = [
        pltpu.make_async_copy(slots_hbm, slots_ref, small_sems.at[0]),
        pltpu.make_async_copy(ids_hbm, ids_ref, small_sems.at[1]),
    ]
    loads = [
        pltpu.make_async_copy(
            hidden_hbm.at[:, pl.ds(at, size)], rows_ref.at[:, pl.ds(at, size)], sems.at[i]
        )
        for i, (at, size) in enumerate(spans)
    ]
    for copy in [*small, *loads]:
        copy.start()
    for copy in small:
        copy.wait()
    routed, label = routing(which, owners, slot_count, held, slots_ref[...], ids_ref[...])
    routed = routed.astype(jnp.bfloat16)
    routed_ref[...] = routed

    def put(at, lines):
        for i, message_ref in enumerate(message_refs):
            message_ref[:, at : at + lines.shape[1]] = lines[
                i * slot_count : (i + 1) * slot_count
            ].astype(message_ref.dtype)

    put(width, jnp.broadcast_to(label, (label.shape[0], LANES)))
    for load, (at, size) in zip(loads, spans):
        load.wait()
        put(at, jnp.dot(routed, rows_ref[:, at : at + size], preferred_element_type=jnp.float32))


def pack(which, hidden, adapter_id, adapter_slot, owners, slot_count, held):
    rows, width = hidden.shape
    lines = len(which) * slot_count
    steps = pl.cdiv(width, COLUMNS_STEP)
    slots = adapter_slot.reshape(1, -1)
    return pl.pallas_call(
        functools.partial(pack_kernel, which, owners, slot_count, held),
        in_specs=[pl.BlockSpec(memory_space=pl.ANY)] * 3,
        out_specs=[pl.BlockSpec(memory_space=pltpu.VMEM)] * (1 + len(which)),
        out_shape=[jax.ShapeDtypeStruct((lines, rows), jnp.bfloat16)]
        + [jax.ShapeDtypeStruct((slot_count, width + LANES), hidden.dtype)] * len(which),
        scratch_shapes=[
            pltpu.VMEM(slots.shape, jnp.int32),
            pltpu.VMEM((1, rows), jnp.int32),
            pltpu.VMEM((rows, width), hidden.dtype),
            pltpu.SemaphoreType.DMA((2,)),
            pltpu.SemaphoreType.DMA((steps,)),
        ],
        compiler_params=pltpu.CompilerParams(vmem_limit_bytes=56 * 2**20),
        name="pack",
    )(slots, adapter_id.reshape(1, rows), hidden)


def stack(refs, at, size):
    return jnp.concatenate(
        [ref[:, at : at + size].astype(jnp.float32) for ref in refs], axis=0
    ).astype(jnp.bfloat16)


def adapt_kernel(count, *refs):
    arrived_refs, (a_ref, b_ref), change_refs = refs[:count], refs[count : count + 2], refs[-count:]
    width = a_ref.shape[0]
    slot_count = arrived_refs[0].shape[0]
    low = jnp.zeros((count * slot_count, a_ref.shape[1]), jnp.float32)
    for at in range(0, width, ADAPT_STEP):
        low += jnp.dot(
            stack(arrived_refs, at, ADAPT_STEP),
            a_ref[at : at + ADAPT_STEP, :],
            preferred_element_type=jnp.float32,
        )
    label = stack(arrived_refs, width, LANES).astype(jnp.float32)[:, :1].astype(jnp.int32)
    column = lax.broadcasted_iota(jnp.int32, low.shape, 1) // RANK
    low = jnp.where(column == label, low, 0.0).astype(jnp.bfloat16)
    for at in range(0, b_ref.shape[1], OUT_STEP):
        change = SCALE * jnp.dot(low, b_ref[:, at : at + OUT_STEP], preferred_element_type=jnp.float32)
        for i, change_ref in enumerate(change_refs):
            change_ref[:, at : at + OUT_STEP] = change[
                i * slot_count : (i + 1) * slot_count
            ].astype(change_ref.dtype)


def adapt(arrived, a_maps, b_maps):
    count = len(arrived)
    change = jax.ShapeDtypeStruct((arrived[0].shape[0], b_maps.shape[1]), jnp.bfloat16)
    return pl.pallas_call(
        functools.partial(adapt_kernel, count),
        in_specs=[pl.BlockSpec(memory_space=pltpu.VMEM)] * (count + 2),
        out_specs=[pl.BlockSpec(memory_space=pltpu.VMEM)] * count,
        out_shape=[change] * count,
        compiler_params=pltpu.CompilerParams(vmem_limit_bytes=GRANT),
        name="adapt",
    )(*arrived, a_maps, b_maps)


def tall(rows, group):
    return jnp.concatenate([rows[:, g * HEAD : (g + 1) * HEAD] for g in range(group)], axis=0)


def prep_kernel(group, base_ref, kv_ref, given_ref, keys_ref, rest_ref, lens_ref):
    lens_ref[...] = given_ref[...]
    step, context = ROWS_STEP, kv_ref.shape[2]
    cells = step * context
    for j in range(PREP_STEPS):
        rows = slice(j * step, (j + 1) * step)
        for k in range(KVH):
            head = slice(k * HEAD, (k + 1) * HEAD)
            keys = kv_ref[rows, 0, :, head].astype(jnp.float32).reshape(cells, HEAD)
            keys_ref[k, :, j * cells : (j + 1) * cells] = jnp.transpose(keys).astype(keys_ref.dtype)
            rest_ref[k, j, :cells] = kv_ref[rows, 1, :, head].reshape(cells, HEAD)
            base = base_ref[:, k * group * HEAD : (k + 1) * group * HEAD].astype(jnp.float32)
            rest_ref[k, j, cells:] = tall(base[rows], group).astype(rest_ref.dtype)


def prep(base_q, kv_cache, cache_len):
    rows, width = base_q.shape
    context = kv_cache.shape[2]
    group = width // (KVH * HEAD)
    step = ROWS_STEP * PREP_STEPS
    steps = rows // step
    cells = ROWS_STEP * context
    lines = cells + group * ROWS_STEP
    lens = jnp.repeat(cache_len, context).reshape(rows // ROWS_STEP, 1, cells)
    length = max(pl.cdiv(TALL_BYTES, 2 * KVH * lines * HEAD * PREP_STEPS), steps) * PREP_STEPS
    return pl.pallas_call(
        functools.partial(prep_kernel, group),
        grid=(steps,),
        in_specs=[
            pl.BlockSpec((step, width), lambda i: (i, 0)),
            pl.BlockSpec((step, *kv_cache.shape[1:]), lambda i: (i, 0, 0, 0)),
            pl.BlockSpec((PREP_STEPS, 1, cells), lambda i: (i, 0, 0)),
        ],
        out_specs=[
            pl.BlockSpec((KVH, HEAD, PREP_STEPS * cells), lambda i: (0, 0, i)),
            pl.BlockSpec((KVH, PREP_STEPS, lines, HEAD), lambda i: (0, i, 0, 0)),
            pl.BlockSpec((PREP_STEPS, 1, cells), lambda i: (i, 0, 0)),
        ],
        out_shape=[
            jax.ShapeDtypeStruct((KVH, HEAD, rows * context), jnp.bfloat16),
            jax.ShapeDtypeStruct((KVH, length, lines, HEAD), jnp.bfloat16),
            jax.ShapeDtypeStruct(lens.shape, lens.dtype),
        ],
        compiler_params=pltpu.CompilerParams(vmem_limit_bytes=GRANT),
        name="prep",
    )(base_q, kv_cache, lens)


def hold_kernel(*refs):
    del refs


def hold(message, after):
    return pl.pallas_call(
        hold_kernel,
        in_specs=[pl.BlockSpec(memory_space=pl.ANY)] * 2,
        out_specs=pl.BlockSpec(memory_space=pl.ANY),
        out_shape=jax.ShapeDtypeStruct(message.shape, message.dtype),
        input_output_aliases={0: 0},
        compiler_params=pltpu.CompilerParams(vmem_limit_bytes=GRANT),
        name="hold",
    )(message, after)


def attend_kernel(group, context, count, *refs):
    returned_refs, routed_refs, refs = refs[:count], refs[count : count + 2], refs[count + 2 :]
    keys_ref, lens_ref, rest_hbm, out_hbm, *scratch = refs
    query_ref, values_ref, bias_ref, scores_ref, expo_ref, out_ref, sems = scratch
    step = ROWS_STEP
    steps, lines, cells = bias_ref.shape
    span = group * HEAD
    factor = LOG2E / jnp.sqrt(jnp.float32(HEAD))
    loads = [
        [
            pltpu.make_async_copy(
                rest_hbm.at[k, pl.ds(0, steps), pl.ds(cells, lines)], query_ref.at[k], sems.at[k, 1]
            ),
            pltpu.make_async_copy(
                rest_hbm.at[k, pl.ds(0, steps), pl.ds(0, cells)], values_ref.at[k], sems.at[k, 2]
            ),
        ]
        for k in range(KVH)
    ]
    stores = [
        pltpu.make_async_copy(
            out_ref.at[:, pl.ds(k * span, span)], out_hbm.at[:, pl.ds(k * span, span)], sems.at[k, 0]
        )
        for k in range(KVH)
    ]
    for load in loads:
        for copy in load:
            copy.start()
    lane = lax.broadcasted_iota(jnp.int32, (lines, cells), 1)
    line = lax.broadcasted_iota(jnp.int32, (lines, cells), 0)
    own = lax.div(lane, context) == lax.rem(line, step)
    position = lax.rem(lane, context)
    ones = jnp.ones((cells, HEAD), expo_ref.dtype)
    for i in range(steps):
        bias_ref[i] = jnp.where(own & (position < lens_ref[i]), 0.0, -jnp.inf)
    routed = jnp.concatenate([ref[...].astype(jnp.float32) for ref in routed_refs], axis=0)
    routed = jnp.transpose(routed).astype(jnp.bfloat16)
    for k in range(KVH):
        delta = jnp.dot(
            routed,
            stack(returned_refs, k * span, span),
            preferred_element_type=jnp.float32,
        )
        for copy in loads[k]:
            copy.wait()
        for i in range(steps):
            keys = keys_ref[k, :, i * cells : (i + 1) * cells]
            change = tall(delta[i * step : (i + 1) * step], group).astype(jnp.bfloat16)
            scores = jnp.dot(
                jnp.concatenate([query_ref[k, i], change], axis=1),
                jnp.concatenate([keys, keys], axis=0),
                preferred_element_type=jnp.float32,
            )
            scores_ref[k, i] = scores * factor + bias_ref[i]
        for i in range(steps):
            scores = scores_ref[k, i]
            expo = jnp.exp2(scores - jnp.max(scores, axis=1, keepdims=True))
            expo_ref[k, i] = expo.astype(expo_ref.dtype)
        for i in range(steps):
            rows = slice(i * step, (i + 1) * step)
            out = jnp.dot(
                expo_ref[k, i],
                jnp.concatenate([values_ref[k, i], ones], axis=1),
                preferred_element_type=jnp.float32,
            )
            out = out[:, :HEAD] * (1.0 / out[:, HEAD:])
            for g in range(group):
                out_ref[rows, (k * group + g) * HEAD : (k * group + g + 1) * HEAD] = out[
                    g * step : (g + 1) * step
                ].astype(out_ref.dtype)
        stores[k].start()
    for store in stores:
        store.wait()


def attend(routed, returned, keys, rest, lens, context):
    rows, width = routed[0].shape[1], returned[0].shape[1]
    group = width // (KVH * HEAD)
    step = ROWS_STEP
    steps = rows // step
    cells = step * context
    return pl.pallas_call(
        functools.partial(attend_kernel, group, context, len(returned)),
        in_specs=[pl.BlockSpec(memory_space=pltpu.VMEM)] * (4 + len(returned)) + [pl.BlockSpec(memory_space=pl.ANY)],
        out_specs=pl.BlockSpec(memory_space=pl.ANY),
        out_shape=jax.ShapeDtypeStruct((rows, width), jnp.bfloat16),
        scratch_shapes=[
            pltpu.VMEM((KVH, steps, group * step, HEAD), rest.dtype),
            pltpu.VMEM((KVH, steps, cells, HEAD), rest.dtype),
            pltpu.VMEM((steps, group * step, cells), jnp.float32),
            pltpu.VMEM((KVH, steps, group * step, cells), jnp.float32),
            pltpu.VMEM((KVH, steps, group * step, cells), jnp.bfloat16),
            pltpu.VMEM((rows, width), jnp.bfloat16),
            pltpu.SemaphoreType.DMA((KVH, 3)),
        ],
        compiler_params=pltpu.CompilerParams(vmem_limit_bytes=GRANT),
        name="attend",
    )(*returned, *routed, keys, lens, rest)


def on_device(hidden, adapter_id, adapter_slot, cache_len, base_q, kv_cache, a_maps, b_maps):
    owners = lax.axis_size("owner")
    rows = hidden.shape[0]
    held = a_maps.shape[1] // RANK
    slot_count = max(2, 2 * ((rows + 2 * owners - 1) // (2 * owners)))
    half = owners // 2
    near = [*range(half // 2, half), *range(1, half // 2)]
    far = [*range(half, owners)]
    order = [s for pair in zip(far, near[: half // 2]) for s in pair]
    order += [*far[half // 2 :], *near[half // 2 :], 0]
    routed, messages = [], []
    for which in (order[:FIRST], order[FIRST:]):
        hits, *packed = pack(which, hidden, adapter_id, adapter_slot, owners, slot_count, held)
        routed.append(hits)
        messages += packed
    keys, rest, lens = prep(base_q, kv_cache, cache_len)
    messages[-2] = hold(messages[-2], rest)
    size = owners // GROUPS
    arrived = exchange(order, owners)(messages)
    changes = []
    for at in range(0, owners, size):
        changes += adapt(arrived[at : at + size], a_maps, b_maps)
    returned = exchange(order, owners)(changes)
    return attend(routed, returned, keys, rest, lens, kv_cache.shape[2])


def exchange(order, owners):
    def permutes(messages):
        return [
            lax.ppermute(message, "owner", [(i, i ^ s) for i in range(owners)]) if s else message
            for message, s in zip(messages, order)
        ]

    def whole(messages):
        messages = dict(zip(order, messages))
        place = lax.axis_index("owner") ^ jnp.arange(owners, dtype=jnp.int32)
        blocks = jnp.stack([messages[s] for s in range(owners)])[place]
        blocks = lax.all_to_all(blocks, "owner", split_axis=0, concat_axis=0, tiled=True)[place]
        return [blocks[s] for s in order]

    return permutes if owners <= MOST_PERMUTES else whole


def solution(mesh):
    return jax.shard_map(
        on_device,
        mesh=mesh,
        in_specs=(
            P(("groups", "owner"), None),
            P(("groups", "owner")),
            P("groups"),
            P(("groups", "owner")),
            P(("groups", "owner"), None),
            P(("groups", "owner"), None, None, None),
            P(None, "owner"),
            P("owner", None),
        ),
        out_specs=P(("groups", "owner"), None),
        check_vma=False,
    )
```

```python
import functools

import jax
import jax.numpy as jnp
from jax import lax
from jax.experimental import pallas as pl
from jax.experimental.pallas import tpu as pltpu
from jax.sharding import PartitionSpec as P

HEAD = 128
KVH = 4
RANK = 64
LANES = 128
SCALE = 2.0
ROWS_STEP = 8
PREP_STEPS = 4
GROUPS = 8
HELD = 13
FIRST = 4
MOST_PERMUTES = 32
COLUMNS_STEP = 1024
ADAPT_STEP = 2048
OUT_STEP = 1024
GRANT = 48 * 2**20
LOG2E = 1.4426950408889634
TALL_BYTES = 17 * 2**20


def routing(which, owners, slot_count, held, slots, ids):
    rows = ids.shape[1]
    named = lax.broadcasted_iota(jnp.int32, (slots.shape[1], rows), 0) == ids
    slot = jnp.dot(
        slots.astype(jnp.float32).astype(jnp.bfloat16),
        named.astype(jnp.bfloat16),
        preferred_element_type=jnp.float32,
    ).astype(jnp.int32)
    owner = lax.div(slot, held)
    local = slot - owner * held
    hits = owner == lax.broadcasted_iota(jnp.int32, (owners, rows), 0)
    earlier = lax.broadcasted_iota(jnp.int32, (rows, rows), 0) < lax.broadcasted_iota(
        jnp.int32, (rows, rows), 1
    )
    before = jnp.dot(
        hits.astype(jnp.bfloat16), earlier.astype(jnp.bfloat16), preferred_element_type=jnp.float32
    )
    place = jnp.sum(jnp.where(hits, before, 0.0), axis=0, keepdims=True).astype(jnp.int32)
    apart = owner ^ lax.axis_index("owner")
    target = jnp.full_like(apart, -1)
    for j, s in enumerate(which):
        target = jnp.where(apart == s, j * slot_count + place, target)
    routed = target == lax.broadcasted_iota(jnp.int32, (len(which) * slot_count, rows), 0)
    label = jnp.sum(jnp.where(routed, local.astype(jnp.float32), 0.0), axis=1, keepdims=True)
    return routed, label


def pack_kernel(which, owners, slot_count, held, slots_hbm, ids_hbm, hidden_hbm, routed_ref, *refs):
    message_refs, refs = refs[: len(which)], refs[len(which) :]
    slots_ref, ids_ref, rows_ref, small_sems, sems = refs
    width = rows_ref.shape[1]
    spans = [(at, min(COLUMNS_STEP, width - at)) for at in range(0, width, COLUMNS_STEP)]
    small = [
        pltpu.make_async_copy(slots_hbm, slots_ref, small_sems.at[0]),
        pltpu.make_async_copy(ids_hbm, ids_ref, small_sems.at[1]),
    ]
    loads = [
        pltpu.make_async_copy(
            hidden_hbm.at[:, pl.ds(at, size)], rows_ref.at[:, pl.ds(at, size)], sems.at[i]
        )
        for i, (at, size) in enumerate(spans)
    ]
    for copy in [*small, *loads]:
        copy.start()
    for copy in small:
        copy.wait()
    routed, label = routing(which, owners, slot_count, held, slots_ref[...], ids_ref[...])
    routed = routed.astype(jnp.bfloat16)
    routed_ref[...] = routed

    def put(at, lines):
        for i, message_ref in enumerate(message_refs):
            message_ref[:, at : at + lines.shape[1]] = lines[
                i * slot_count : (i + 1) * slot_count
            ].astype(message_ref.dtype)

    put(width, jnp.broadcast_to(label, (label.shape[0], LANES)))
    for load, (at, size) in zip(loads, spans):
        load.wait()
        put(at, jnp.dot(routed, rows_ref[:, at : at + size], preferred_element_type=jnp.float32))


def pack(which, hidden, adapter_id, adapter_slot, owners, slot_count, held):
    rows, width = hidden.shape
    lines = len(which) * slot_count
    steps = pl.cdiv(width, COLUMNS_STEP)
    slots = adapter_slot.reshape(1, -1)
    return pl.pallas_call(
        functools.partial(pack_kernel, which, owners, slot_count, held),
        in_specs=[pl.BlockSpec(memory_space=pl.ANY)] * 3,
        out_specs=[pl.BlockSpec(memory_space=pltpu.VMEM)] * (1 + len(which)),
        out_shape=[jax.ShapeDtypeStruct((lines, rows), jnp.bfloat16)]
        + [jax.ShapeDtypeStruct((slot_count, width + LANES), hidden.dtype)] * len(which),
        scratch_shapes=[
            pltpu.VMEM(slots.shape, jnp.int32),
            pltpu.VMEM((1, rows), jnp.int32),
            pltpu.VMEM((rows, width), hidden.dtype),
            pltpu.SemaphoreType.DMA((2,)),
            pltpu.SemaphoreType.DMA((steps,)),
        ],
        compiler_params=pltpu.CompilerParams(vmem_limit_bytes=56 * 2**20),
        name="pack",
    )(slots, adapter_id.reshape(1, rows), hidden)


def stack(refs, at, size):
    return jnp.concatenate(
        [ref[:, at : at + size].astype(jnp.float32) for ref in refs], axis=0
    ).astype(jnp.bfloat16)


def adapt_kernel(count, *refs):
    arrived_refs, (a_ref, b_ref), change_refs = refs[:count], refs[count : count + 2], refs[-count:]
    width = a_ref.shape[0]
    slot_count = arrived_refs[0].shape[0]
    low = jnp.zeros((count * slot_count, a_ref.shape[1]), jnp.float32)
    for at in range(0, width, ADAPT_STEP):
        low += jnp.dot(
            stack(arrived_refs, at, ADAPT_STEP),
            a_ref[at : at + ADAPT_STEP, :],
            preferred_element_type=jnp.float32,
        )
    label = stack(arrived_refs, width, LANES).astype(jnp.float32)[:, :1].astype(jnp.int32)
    column = lax.broadcasted_iota(jnp.int32, low.shape, 1) // RANK
    low = jnp.where(column == label, low, 0.0).astype(jnp.bfloat16)
    for at in range(0, b_ref.shape[1], OUT_STEP):
        change = SCALE * jnp.dot(low, b_ref[:, at : at + OUT_STEP], preferred_element_type=jnp.float32)
        for i, change_ref in enumerate(change_refs):
            change_ref[:, at : at + OUT_STEP] = change[
                i * slot_count : (i + 1) * slot_count
            ].astype(change_ref.dtype)


def adapt(arrived, a_maps, b_maps):
    count = len(arrived)
    change = jax.ShapeDtypeStruct((arrived[0].shape[0], b_maps.shape[1]), jnp.bfloat16)
    return pl.pallas_call(
        functools.partial(adapt_kernel, count),
        in_specs=[pl.BlockSpec(memory_space=pltpu.VMEM)] * (count + 2),
        out_specs=[pl.BlockSpec(memory_space=pltpu.VMEM)] * count,
        out_shape=[change] * count,
        compiler_params=pltpu.CompilerParams(vmem_limit_bytes=GRANT),
        name="adapt",
    )(*arrived, a_maps, b_maps)


def tall(rows, group):
    return jnp.concatenate([rows[:, g * HEAD : (g + 1) * HEAD] for g in range(group)], axis=0)


def prep_kernel(group, base_ref, kv_ref, given_ref, keys_ref, rest_ref, lens_ref):
    lens_ref[...] = given_ref[...]
    step, context = ROWS_STEP, kv_ref.shape[2]
    cells = step * context
    for j in range(PREP_STEPS):
        rows = slice(j * step, (j + 1) * step)
        for k in range(KVH):
            head = slice(k * HEAD, (k + 1) * HEAD)
            keys = kv_ref[rows, 0, :, head].astype(jnp.float32).reshape(cells, HEAD)
            keys_ref[k, :, j * cells : (j + 1) * cells] = jnp.transpose(keys).astype(keys_ref.dtype)
            rest_ref[k, j, :cells] = kv_ref[rows, 1, :, head].reshape(cells, HEAD)
            base = base_ref[:, k * group * HEAD : (k + 1) * group * HEAD].astype(jnp.float32)
            rest_ref[k, j, cells:] = tall(base[rows], group).astype(rest_ref.dtype)


def prep(base_q, kv_cache, cache_len):
    rows, width = base_q.shape
    context = kv_cache.shape[2]
    group = width // (KVH * HEAD)
    step = ROWS_STEP * PREP_STEPS
    steps = rows // step
    cells = ROWS_STEP * context
    lines = cells + group * ROWS_STEP
    lens = jnp.repeat(cache_len, context).reshape(rows // ROWS_STEP, 1, cells)
    length = max(pl.cdiv(TALL_BYTES, 2 * KVH * lines * HEAD * PREP_STEPS), steps) * PREP_STEPS
    return pl.pallas_call(
        functools.partial(prep_kernel, group),
        grid=(steps,),
        in_specs=[
            pl.BlockSpec((step, width), lambda i: (i, 0)),
            pl.BlockSpec((step, *kv_cache.shape[1:]), lambda i: (i, 0, 0, 0)),
            pl.BlockSpec((PREP_STEPS, 1, cells), lambda i: (i, 0, 0)),
        ],
        out_specs=[
            pl.BlockSpec((KVH, HEAD, PREP_STEPS * cells), lambda i: (0, 0, i)),
            pl.BlockSpec((KVH, PREP_STEPS, lines, HEAD), lambda i: (0, i, 0, 0)),
            pl.BlockSpec((PREP_STEPS, 1, cells), lambda i: (i, 0, 0)),
        ],
        out_shape=[
            jax.ShapeDtypeStruct((KVH, HEAD, rows * context), jnp.bfloat16),
            jax.ShapeDtypeStruct((KVH, length, lines, HEAD), jnp.bfloat16),
            jax.ShapeDtypeStruct(lens.shape, lens.dtype),
        ],
        compiler_params=pltpu.CompilerParams(vmem_limit_bytes=GRANT),
        name="prep",
    )(base_q, kv_cache, lens)


def hold_kernel(*refs):
    del refs


def hold(message, after):
    return pl.pallas_call(
        hold_kernel,
        in_specs=[pl.BlockSpec(memory_space=pl.ANY)] * 2,
        out_specs=pl.BlockSpec(memory_space=pl.ANY),
        out_shape=jax.ShapeDtypeStruct(message.shape, message.dtype),
        input_output_aliases={0: 0},
        compiler_params=pltpu.CompilerParams(vmem_limit_bytes=GRANT),
        name="hold",
    )(message, after)


def attend_kernel(group, context, count, *refs):
    returned_refs, routed_refs, refs = refs[:count], refs[count : count + 2], refs[count + 2 :]
    keys_ref, lens_ref, rest_hbm, out_hbm, *scratch = refs
    query_ref, values_ref, bias_ref, scores_ref, expo_ref, out_ref, sems = scratch
    step = ROWS_STEP
    steps, lines, cells = bias_ref.shape
    span = group * HEAD
    factor = LOG2E / jnp.sqrt(jnp.float32(HEAD))
    loads = [
        [
            pltpu.make_async_copy(
                rest_hbm.at[k, pl.ds(0, steps), pl.ds(cells, lines)], query_ref.at[k], sems.at[k, 1]
            ),
            pltpu.make_async_copy(
                rest_hbm.at[k, pl.ds(0, steps), pl.ds(0, cells)], values_ref.at[k], sems.at[k, 2]
            ),
        ]
        for k in range(KVH)
    ]
    stores = [
        pltpu.make_async_copy(
            out_ref.at[:, pl.ds(k * span, span)], out_hbm.at[:, pl.ds(k * span, span)], sems.at[k, 0]
        )
        for k in range(KVH)
    ]
    for load in loads:
        for copy in load:
            copy.start()
    lane = lax.broadcasted_iota(jnp.int32, (lines, cells), 1)
    line = lax.broadcasted_iota(jnp.int32, (lines, cells), 0)
    own = lax.div(lane, context) == lax.rem(line, step)
    position = lax.rem(lane, context)
    ones = jnp.ones((cells, HEAD), expo_ref.dtype)
    for i in range(steps):
        bias_ref[i] = jnp.where(own & (position < lens_ref[i]), 0.0, -jnp.inf)
    routed = jnp.concatenate([ref[...].astype(jnp.float32) for ref in routed_refs], axis=0)
    routed = jnp.transpose(routed).astype(jnp.bfloat16)
    for k in range(KVH):
        delta = jnp.dot(
            routed,
            stack(returned_refs, k * span, span),
            preferred_element_type=jnp.float32,
        )
        for copy in loads[k]:
            copy.wait()
        for i in range(steps):
            keys = keys_ref[k, :, i * cells : (i + 1) * cells]
            change = tall(delta[i * step : (i + 1) * step], group).astype(jnp.bfloat16)
            scores = jnp.dot(
                jnp.concatenate([query_ref[k, i], change], axis=1),
                jnp.concatenate([keys, keys], axis=0),
                preferred_element_type=jnp.float32,
            )
            scores_ref[k, i] = scores * factor + bias_ref[i]
        for i in range(steps):
            scores = scores_ref[k, i]
            expo = jnp.exp2(scores - jnp.max(scores, axis=1, keepdims=True))
            expo_ref[k, i] = expo.astype(expo_ref.dtype)
        for i in range(steps):
            rows = slice(i * step, (i + 1) * step)
            out = jnp.dot(
                expo_ref[k, i],
                jnp.concatenate([values_ref[k, i], ones], axis=1),
                preferred_element_type=jnp.float32,
            )
            out = out[:, :HEAD] * (1.0 / out[:, HEAD:])
            for g in range(group):
                out_ref[rows, (k * group + g) * HEAD : (k * group + g + 1) * HEAD] = out[
                    g * step : (g + 1) * step
                ].astype(out_ref.dtype)
        stores[k].start()
    for store in stores:
        store.wait()


def attend(routed, returned, keys, rest, lens, context):
    rows, width = routed[0].shape[1], returned[0].shape[1]
    group = width // (KVH * HEAD)
    step = ROWS_STEP
    steps = rows // step
    cells = step * context
    return pl.pallas_call(
        functools.partial(attend_kernel, group, context, len(returned)),
        in_specs=[pl.BlockSpec(memory_space=pltpu.VMEM)] * (4 + len(returned)) + [pl.BlockSpec(memory_space=pl.ANY)],
        out_specs=pl.BlockSpec(memory_space=pl.ANY),
        out_shape=jax.ShapeDtypeStruct((rows, width), jnp.bfloat16),
        scratch_shapes=[
            pltpu.VMEM((KVH, steps, group * step, HEAD), rest.dtype),
            pltpu.VMEM((KVH, steps, cells, HEAD), rest.dtype),
            pltpu.VMEM((steps, group * step, cells), jnp.float32),
            pltpu.VMEM((KVH, steps, group * step, cells), jnp.float32),
            pltpu.VMEM((KVH, steps, group * step, cells), jnp.bfloat16),
            pltpu.VMEM((rows, width), jnp.bfloat16),
            pltpu.SemaphoreType.DMA((KVH, 3)),
        ],
        compiler_params=pltpu.CompilerParams(vmem_limit_bytes=GRANT),
        name="attend",
    )(*returned, *routed, keys, lens, rest)


def on_device(hidden, adapter_id, adapter_slot, cache_len, base_q, kv_cache, a_maps, b_maps):
    owners = lax.axis_size("owner")
    rows = hidden.shape[0]
    held = a_maps.shape[1] // RANK
    slot_count = max(2, 2 * ((rows + 2 * owners - 1) // (2 * owners)))
    half = owners // 2
    near = [*range(half // 2, half), *range(1, half // 2)]
    order = [s for pair in zip(range(half, owners), [*near, 0]) for s in pair]

    routed, messages = [], []
    for which in (order[:FIRST], order[FIRST:]):
        hits, *packed = pack(which, hidden, adapter_id, adapter_slot, owners, slot_count, held)
        routed.append(hits)
        messages += packed
    keys, rest, lens = prep(base_q, kv_cache, cache_len)
    messages[HELD] = hold(messages[HELD], rest)
    size = owners // GROUPS
    arrived = exchange(order, owners)(messages)
    changes = []
    for at in range(0, owners, size):
        changes += adapt(arrived[at : at + size], a_maps, b_maps)
    returned = exchange(order, owners)(changes)
    return attend(routed, returned, keys, rest, lens, kv_cache.shape[2])


def exchange(order, owners):
    def permutes(messages):
        return [
            lax.ppermute(message, "owner", [(i, i ^ s) for i in range(owners)]) if s else message
            for message, s in zip(messages, order)
        ]

    def whole(messages):
        messages = dict(zip(order, messages))
        place = lax.axis_index("owner") ^ jnp.arange(owners, dtype=jnp.int32)
        blocks = jnp.stack([messages[s] for s in range(owners)])[place]
        blocks = lax.all_to_all(blocks, "owner", split_axis=0, concat_axis=0, tiled=True)[place]
        return [blocks[s] for s in order]

    return permutes if owners <= MOST_PERMUTES else whole


def solution(mesh):
    return jax.shard_map(
        on_device,
        mesh=mesh,
        in_specs=(
            P(("groups", "owner"), None),
            P(("groups", "owner")),
            P("groups"),
            P(("groups", "owner")),
            P(("groups", "owner"), None),
            P(("groups", "owner"), None, None, None),
            P(None, "owner"),
            P("owner", None),
        ),
        out_specs=P(("groups", "owner"), None),
        check_vma=False,
    )
```

```python
import functools

import jax
import jax.numpy as jnp
from jax import lax
from jax.experimental import pallas as pl
from jax.experimental.pallas import tpu as pltpu
from jax.sharding import PartitionSpec as P

HEAD = 128
KVH = 4
RANK = 64
LANES = 128
SCALE = 2.0
ROWS_STEP = 8
PREP_STEPS = 4
GROUPS = 2
HELD = 13
FIRST = 4
MOST_PERMUTES = 32
COLUMNS_STEP = 1024
ADAPT_STEP = 2048
OUT_STEP = 1024
GRANT = 48 * 2**20
LOG2E = 1.4426950408889634
TALL_BYTES = 17 * 2**20


def routing(which, owners, slot_count, held, slots, ids):
    rows = ids.shape[1]
    named = lax.broadcasted_iota(jnp.int32, (slots.shape[1], rows), 0) == ids
    slot = jnp.dot(
        slots.astype(jnp.float32).astype(jnp.bfloat16),
        named.astype(jnp.bfloat16),
        preferred_element_type=jnp.float32,
    ).astype(jnp.int32)
    owner = lax.div(slot, held)
    local = slot - owner * held
    hits = owner == lax.broadcasted_iota(jnp.int32, (owners, rows), 0)
    earlier = lax.broadcasted_iota(jnp.int32, (rows, rows), 0) < lax.broadcasted_iota(
        jnp.int32, (rows, rows), 1
    )
    before = jnp.dot(
        hits.astype(jnp.bfloat16), earlier.astype(jnp.bfloat16), preferred_element_type=jnp.float32
    )
    place = jnp.sum(jnp.where(hits, before, 0.0), axis=0, keepdims=True).astype(jnp.int32)
    apart = owner ^ lax.axis_index("owner")
    target = jnp.full_like(apart, -1)
    for j, s in enumerate(which):
        target = jnp.where(apart == s, j * slot_count + place, target)
    routed = target == lax.broadcasted_iota(jnp.int32, (len(which) * slot_count, rows), 0)
    label = jnp.sum(jnp.where(routed, local.astype(jnp.float32), 0.0), axis=1, keepdims=True)
    return routed, label


def pack_kernel(which, owners, slot_count, held, slots_hbm, ids_hbm, hidden_hbm, routed_ref, *refs):
    message_refs, refs = refs[: len(which)], refs[len(which) :]
    slots_ref, ids_ref, rows_ref, small_sems, sems = refs
    width = rows_ref.shape[1]
    spans = [(at, min(COLUMNS_STEP, width - at)) for at in range(0, width, COLUMNS_STEP)]
    small = [
        pltpu.make_async_copy(slots_hbm, slots_ref, small_sems.at[0]),
        pltpu.make_async_copy(ids_hbm, ids_ref, small_sems.at[1]),
    ]
    loads = [
        pltpu.make_async_copy(
            hidden_hbm.at[:, pl.ds(at, size)], rows_ref.at[:, pl.ds(at, size)], sems.at[i]
        )
        for i, (at, size) in enumerate(spans)
    ]
    for copy in [*small, *loads]:
        copy.start()
    for copy in small:
        copy.wait()
    routed, label = routing(which, owners, slot_count, held, slots_ref[...], ids_ref[...])
    routed = routed.astype(jnp.bfloat16)
    routed_ref[...] = routed

    def put(at, lines):
        for i, message_ref in enumerate(message_refs):
            message_ref[:, at : at + lines.shape[1]] = lines[
                i * slot_count : (i + 1) * slot_count
            ].astype(message_ref.dtype)

    put(width, jnp.broadcast_to(label, (label.shape[0], LANES)))
    for load, (at, size) in zip(loads, spans):
        load.wait()
        put(at, jnp.dot(routed, rows_ref[:, at : at + size], preferred_element_type=jnp.float32))


def pack(which, hidden, adapter_id, adapter_slot, owners, slot_count, held):
    rows, width = hidden.shape
    lines = len(which) * slot_count
    steps = pl.cdiv(width, COLUMNS_STEP)
    slots = adapter_slot.reshape(1, -1)
    return pl.pallas_call(
        functools.partial(pack_kernel, which, owners, slot_count, held),
        in_specs=[pl.BlockSpec(memory_space=pl.ANY)] * 3,
        out_specs=[pl.BlockSpec(memory_space=pltpu.VMEM)] * (1 + len(which)),
        out_shape=[jax.ShapeDtypeStruct((lines, rows), jnp.bfloat16)]
        + [jax.ShapeDtypeStruct((slot_count, width + LANES), hidden.dtype)] * len(which),
        scratch_shapes=[
            pltpu.VMEM(slots.shape, jnp.int32),
            pltpu.VMEM((1, rows), jnp.int32),
            pltpu.VMEM((rows, width), hidden.dtype),
            pltpu.SemaphoreType.DMA((2,)),
            pltpu.SemaphoreType.DMA((steps,)),
        ],
        compiler_params=pltpu.CompilerParams(vmem_limit_bytes=56 * 2**20),
        name="pack",
    )(slots, adapter_id.reshape(1, rows), hidden)


def stack(refs, at, size):
    return jnp.concatenate(
        [ref[:, at : at + size].astype(jnp.float32) for ref in refs], axis=0
    ).astype(jnp.bfloat16)


def adapt_kernel(count, *refs):
    arrived_refs, (a_ref, b_ref), change_refs = refs[:count], refs[count : count + 2], refs[-count:]
    width = a_ref.shape[0]
    slot_count = arrived_refs[0].shape[0]
    low = jnp.zeros((count * slot_count, a_ref.shape[1]), jnp.float32)
    for at in range(0, width, ADAPT_STEP):
        low += jnp.dot(
            stack(arrived_refs, at, ADAPT_STEP),
            a_ref[at : at + ADAPT_STEP, :],
            preferred_element_type=jnp.float32,
        )
    label = stack(arrived_refs, width, LANES).astype(jnp.float32)[:, :1].astype(jnp.int32)
    column = lax.broadcasted_iota(jnp.int32, low.shape, 1) // RANK
    low = jnp.where(column == label, low, 0.0).astype(jnp.bfloat16)
    for at in range(0, b_ref.shape[1], OUT_STEP):
        change = SCALE * jnp.dot(low, b_ref[:, at : at + OUT_STEP], preferred_element_type=jnp.float32)
        for i, change_ref in enumerate(change_refs):
            change_ref[:, at : at + OUT_STEP] = change[
                i * slot_count : (i + 1) * slot_count
            ].astype(change_ref.dtype)


def adapt(arrived, a_maps, b_maps):
    count = len(arrived)
    change = jax.ShapeDtypeStruct((arrived[0].shape[0], b_maps.shape[1]), jnp.bfloat16)
    return pl.pallas_call(
        functools.partial(adapt_kernel, count),
        in_specs=[pl.BlockSpec(memory_space=pltpu.VMEM)] * (count + 2),
        out_specs=[pl.BlockSpec(memory_space=pltpu.VMEM)] * count,
        out_shape=[change] * count,
        compiler_params=pltpu.CompilerParams(vmem_limit_bytes=GRANT),
        name="adapt",
    )(*arrived, a_maps, b_maps)


def tall(rows, group):
    return jnp.concatenate([rows[:, g * HEAD : (g + 1) * HEAD] for g in range(group)], axis=0)


def prep_kernel(group, base_ref, kv_ref, given_ref, keys_ref, rest_ref, lens_ref):
    lens_ref[...] = given_ref[...]
    step, context = ROWS_STEP, kv_ref.shape[2]
    cells = step * context
    for j in range(PREP_STEPS):
        rows = slice(j * step, (j + 1) * step)
        for k in range(KVH):
            head = slice(k * HEAD, (k + 1) * HEAD)
            keys = kv_ref[rows, 0, :, head].astype(jnp.float32).reshape(cells, HEAD)
            keys_ref[k, :, j * cells : (j + 1) * cells] = jnp.transpose(keys).astype(keys_ref.dtype)
            rest_ref[k, j, :cells] = kv_ref[rows, 1, :, head].reshape(cells, HEAD)
            base = base_ref[:, k * group * HEAD : (k + 1) * group * HEAD].astype(jnp.float32)
            rest_ref[k, j, cells:] = tall(base[rows], group).astype(rest_ref.dtype)


def prep(base_q, kv_cache, cache_len):
    rows, width = base_q.shape
    context = kv_cache.shape[2]
    group = width // (KVH * HEAD)
    step = ROWS_STEP * PREP_STEPS
    steps = rows // step
    cells = ROWS_STEP * context
    lines = cells + group * ROWS_STEP
    lens = jnp.repeat(cache_len, context).reshape(rows // ROWS_STEP, 1, cells)
    length = max(pl.cdiv(TALL_BYTES, 2 * KVH * lines * HEAD * PREP_STEPS), steps) * PREP_STEPS
    return pl.pallas_call(
        functools.partial(prep_kernel, group),
        grid=(steps,),
        in_specs=[
            pl.BlockSpec((step, width), lambda i: (i, 0)),
            pl.BlockSpec((step, *kv_cache.shape[1:]), lambda i: (i, 0, 0, 0)),
            pl.BlockSpec((PREP_STEPS, 1, cells), lambda i: (i, 0, 0)),
        ],
        out_specs=[
            pl.BlockSpec((KVH, HEAD, PREP_STEPS * cells), lambda i: (0, 0, i)),
            pl.BlockSpec((KVH, PREP_STEPS, lines, HEAD), lambda i: (0, i, 0, 0)),
            pl.BlockSpec((PREP_STEPS, 1, cells), lambda i: (i, 0, 0)),
        ],
        out_shape=[
            jax.ShapeDtypeStruct((KVH, HEAD, rows * context), jnp.bfloat16),
            jax.ShapeDtypeStruct((KVH, length, lines, HEAD), jnp.bfloat16),
            jax.ShapeDtypeStruct(lens.shape, lens.dtype),
        ],
        compiler_params=pltpu.CompilerParams(vmem_limit_bytes=GRANT),
        name="prep",
    )(base_q, kv_cache, lens)


def hold_kernel(*refs):
    del refs


def hold(message, after):
    return pl.pallas_call(
        hold_kernel,
        in_specs=[pl.BlockSpec(memory_space=pl.ANY)] * 2,
        out_specs=pl.BlockSpec(memory_space=pl.ANY),
        out_shape=jax.ShapeDtypeStruct(message.shape, message.dtype),
        input_output_aliases={0: 0},
        compiler_params=pltpu.CompilerParams(vmem_limit_bytes=GRANT),
        name="hold",
    )(message, after)


def attend_kernel(group, context, count, *refs):
    returned_refs, routed_refs, refs = refs[:count], refs[count : count + 2], refs[count + 2 :]
    keys_ref, lens_ref, rest_hbm, out_hbm, *scratch = refs
    query_ref, values_ref, bias_ref, scores_ref, expo_ref, out_ref, sems = scratch
    step = ROWS_STEP
    steps, lines, cells = bias_ref.shape
    span = group * HEAD
    factor = LOG2E / jnp.sqrt(jnp.float32(HEAD))
    loads = [
        [
            pltpu.make_async_copy(
                rest_hbm.at[k, pl.ds(0, steps), pl.ds(cells, lines)], query_ref.at[k], sems.at[k, 1]
            ),
            pltpu.make_async_copy(
                rest_hbm.at[k, pl.ds(0, steps), pl.ds(0, cells)], values_ref.at[k], sems.at[k, 2]
            ),
        ]
        for k in range(KVH)
    ]
    stores = [
        pltpu.make_async_copy(
            out_ref.at[:, pl.ds(k * span, span)], out_hbm.at[:, pl.ds(k * span, span)], sems.at[k, 0]
        )
        for k in range(KVH)
    ]
    for load in loads:
        for copy in load:
            copy.start()
    lane = lax.broadcasted_iota(jnp.int32, (lines, cells), 1)
    line = lax.broadcasted_iota(jnp.int32, (lines, cells), 0)
    own = lax.div(lane, context) == lax.rem(line, step)
    position = lax.rem(lane, context)
    ones = jnp.ones((cells, HEAD), expo_ref.dtype)
    for i in range(steps):
        bias_ref[i] = jnp.where(own & (position < lens_ref[i]), 0.0, -jnp.inf)
    routed = jnp.concatenate([ref[...].astype(jnp.float32) for ref in routed_refs], axis=0)
    routed = jnp.transpose(routed).astype(jnp.bfloat16)
    for k in range(KVH):
        delta = jnp.dot(
            routed,
            stack(returned_refs, k * span, span),
            preferred_element_type=jnp.float32,
        )
        for copy in loads[k]:
            copy.wait()
        for i in range(steps):
            keys = keys_ref[k, :, i * cells : (i + 1) * cells]
            change = tall(delta[i * step : (i + 1) * step], group).astype(jnp.bfloat16)
            scores = jnp.dot(
                jnp.concatenate([query_ref[k, i], change], axis=1),
                jnp.concatenate([keys, keys], axis=0),
                preferred_element_type=jnp.float32,
            )
            scores_ref[k, i] = scores * factor + bias_ref[i]
        for i in range(steps):
            scores = scores_ref[k, i]
            expo = jnp.exp2(scores - jnp.max(scores, axis=1, keepdims=True))
            expo_ref[k, i] = expo.astype(expo_ref.dtype)
        for i in range(steps):
            rows = slice(i * step, (i + 1) * step)
            out = jnp.dot(
                expo_ref[k, i],
                jnp.concatenate([values_ref[k, i], ones], axis=1),
                preferred_element_type=jnp.float32,
            )
            out = out[:, :HEAD] * (1.0 / out[:, HEAD:])
            for g in range(group):
                out_ref[rows, (k * group + g) * HEAD : (k * group + g + 1) * HEAD] = out[
                    g * step : (g + 1) * step
                ].astype(out_ref.dtype)
        stores[k].start()
    for store in stores:
        store.wait()


def attend(routed, returned, keys, rest, lens, context):
    rows, width = routed[0].shape[1], returned[0].shape[1]
    group = width // (KVH * HEAD)
    step = ROWS_STEP
    steps = rows // step
    cells = step * context
    return pl.pallas_call(
        functools.partial(attend_kernel, group, context, len(returned)),
        in_specs=[pl.BlockSpec(memory_space=pltpu.VMEM)] * (4 + len(returned)) + [pl.BlockSpec(memory_space=pl.ANY)],
        out_specs=pl.BlockSpec(memory_space=pl.ANY),
        out_shape=jax.ShapeDtypeStruct((rows, width), jnp.bfloat16),
        scratch_shapes=[
            pltpu.VMEM((KVH, steps, group * step, HEAD), rest.dtype),
            pltpu.VMEM((KVH, steps, cells, HEAD), rest.dtype),
            pltpu.VMEM((steps, group * step, cells), jnp.float32),
            pltpu.VMEM((KVH, steps, group * step, cells), jnp.float32),
            pltpu.VMEM((KVH, steps, group * step, cells), jnp.bfloat16),
            pltpu.VMEM((rows, width), jnp.bfloat16),
            pltpu.SemaphoreType.DMA((KVH, 3)),
        ],
        compiler_params=pltpu.CompilerParams(vmem_limit_bytes=GRANT),
        name="attend",
    )(*returned, *routed, keys, lens, rest)


def on_device(hidden, adapter_id, adapter_slot, cache_len, base_q, kv_cache, a_maps, b_maps):
    owners = lax.axis_size("owner")
    rows = hidden.shape[0]
    held = a_maps.shape[1] // RANK
    slot_count = max(2, 2 * ((rows + 2 * owners - 1) // (2 * owners)))
    half = owners // 2
    near = [*range(half // 2, half), *range(1, half // 2)]
    order = [s for pair in zip(range(half, owners), [*near, 0]) for s in pair]

    routed, messages = [], []
    for which in (order[:FIRST], order[FIRST:]):
        hits, *packed = pack(which, hidden, adapter_id, adapter_slot, owners, slot_count, held)
        routed.append(hits)
        messages += packed
    keys, rest, lens = prep(base_q, kv_cache, cache_len)
    messages[HELD] = hold(messages[HELD], rest)
    size = owners // GROUPS
    arrived = exchange(order, owners)(messages)
    changes = []
    for at in range(0, owners, size):
        changes += adapt(arrived[at : at + size], a_maps, b_maps)
    returned = exchange(order, owners)(changes)
    return attend(routed, returned, keys, rest, lens, kv_cache.shape[2])


def exchange(order, owners):
    def permutes(messages):
        return [
            lax.ppermute(message, "owner", [(i, i ^ s) for i in range(owners)]) if s else message
            for message, s in zip(messages, order)
        ]

    def whole(messages):
        messages = dict(zip(order, messages))
        place = lax.axis_index("owner") ^ jnp.arange(owners, dtype=jnp.int32)
        blocks = jnp.stack([messages[s] for s in range(owners)])[place]
        blocks = lax.all_to_all(blocks, "owner", split_axis=0, concat_axis=0, tiled=True)[place]
        return [blocks[s] for s in order]

    return permutes if owners <= MOST_PERMUTES else whole


def solution(mesh):
    return jax.shard_map(
        on_device,
        mesh=mesh,
        in_specs=(
            P(("groups", "owner"), None),
            P(("groups", "owner")),
            P("groups"),
            P(("groups", "owner")),
            P(("groups", "owner"), None),
            P(("groups", "owner"), None, None, None),
            P(None, "owner"),
            P("owner", None),
        ),
        out_specs=P(("groups", "owner"), None),
        check_vma=False,
    )
```
